32 devices in a mesh: dp: 16 (over z, x, core), tensor: 2 (over y).
Axes of the slice: x: 2, y: 2, z: 4, core: 2. Of those that a mesh axis runs over, the one named last changes fastest.
Arguments:
- frames: bfloat16 [128, 16, 1024], P('dp'), may hold values from -6 to 6
- cotangent: bfloat16 [128, 16, 1024], P('dp'), may hold values from -8 to 8
- dialogue: int32 [128], P('dp'), may hold values from 0 to 15, never falling along the last dimension, each value on 1 to 32 neighbouring positions
- padding: int32 [128], P('dp'), may hold values 0 or 1
- position_set: int32 [16], replicated, may hold values from 0 to 1, as said below
- query_weight: bfloat16 [2, 1024, 1024], P(None, 'dp', 'tensor'), may hold values from -0.1875 to 0.1875
- key_weight: bfloat16 [2, 1024, 1024], P(None, 'dp', 'tensor'), may hold values from -0.1875 to 0.1875
- value_weight: bfloat16 [2, 1024, 1024], P(None, 'dp', 'tensor'), may hold values from -0.1875 to 0.1875
- output_weight: bfloat16 [2, 1024, 1024], P(None, 'tensor', 'dp'), may hold values from -0.375 to 0.375
- gate_weight: bfloat16 [2, 1024, 2816], P(None, 'dp', 'tensor'), may hold values from -0.1875 to 0.1875
- up_weight: bfloat16 [2, 1024, 2816], P(None, 'dp', 'tensor'), may hold values from -0.1875 to 0.1875
- down_weight: bfloat16 [2, 2816, 1024], P(None, 'tensor', 'dp'), may hold values from -0.109375 to 0.109375
- attention_gain: float32 [2, 1024], replicated, may hold values from 0.25 to 1.75
- feedforward_gain: float32 [2, 1024], replicated, may hold values from 0.25 to 1.75
Outputs:
- mixed: bfloat16 [128, 16, 1024], P('dp')
- frames_grad: bfloat16 [128, 16, 1024], P('dp')
- query_grad: float32 [2, 1024, 1024], P(None, 'dp', 'tensor')
- key_grad: float32 [2, 1024, 1024], P(None, 'dp', 'tensor')
- value_grad: float32 [2, 1024, 1024], P(None, 'dp', 'tensor')
- output_grad: float32 [2, 1024, 1024], P(None, 'tensor', 'dp')
- gate_grad: float32 [2, 1024, 2816], P(None, 'dp', 'tensor')
- up_grad: float32 [2, 1024, 2816], P(None, 'dp', 'tensor')
- down_grad: float32 [2, 2816, 1024], P(None, 'tensor', 'dp')
- attention_gain_grad: float32 [2, 1024], P(None, 'dp')
- feedforward_gain_grad: float32 [2, 1024], P(None, 'dp')
The draws below stay inside these ranges and needn't reach their ends.
Inputs may be any that keep to these rules, and one draw needn't show every extreme that they name: `position_set`: never falls along the positions; each of the 2 sets holds some position. `dialogue`: never falls along the frames; each dialogue holds 1 to 32 frames, and at least one dialogue holds exactly 32.
All inputs are finite; a program needn't handle non-finite values. No bound on the sum of `padding` on one device may be relied on, other than what follows from the above.
Results may differ from the reference program's by a relative error of at most 0.013.
Values may be sent and summed in bfloat16 or wider, within the bound.
A program may use at most 192 MiB of HBM per device.

```python
import math
import jax
import jax.numpy as jnp
import numpy as np
from jax import lax

D = 1024
HEADS = 16
HDIM = 64
FF = 2816
POS = 16
WSETS = 2
FR_DEV = 8
FRAMES = 128
NDIAL = 16


def draw_position_set(key, part):
    key = jax.random.fold_in(key, 5)
    shuffled = jax.random.permutation(key, POS - 1) + 1
    boundaries = shuffled[:WSETS - 1]
    positions = jnp.arange(POS, dtype=jnp.int32)
    return jnp.sum((positions[:, None] >= boundaries[None, :]).astype(jnp.int32), axis=1)


def plant(result, rng, low, high):
    extent = result.shape
    index_at = [jax.random.randint(jax.random.fold_in(rng, axis), (), 0, extent[axis]) for axis in range(len(extent))]
    result = result.at[tuple(index_at)].set(low)
    longest = extent.index(max(extent))
    index_at[longest] = (index_at[longest] + 1) % extent[longest]
    return result.at[tuple(index_at)].set(high)


def with_spikes(result, key, source, target, shards_of, factor):
    owner, partner = [(jnp.arange(result.shape[dim]) // (result.shape[dim] // shards_of)).reshape([-1 if axis == dim else 1 for axis in range(result.ndim)]) for dim in (source, target)]
    chosen = jax.random.permutation(key, shards_of)[partner]
    strong = (owner == chosen) | (owner == (partner + shards_of // 2) % shards_of)
    return jnp.where(strong, factor * result, result)


def level_of(own_key, extent, split, smallest, high):
    def one(dim, shards_of):
        heights = jax.random.uniform(jax.random.fold_in(jax.random.fold_in(own_key, 6), dim), (shards_of,), jnp.float32, smallest / len(split), high / len(split))
        return jnp.repeat(jnp.exp(heights), extent[dim] // shards_of).reshape((-1,) + (1,) * (len(extent) - dim - 1))

    factor_of = one(*split[0])
    for cut in split[1:]:
        factor_of = factor_of * one(*cut)
    return factor_of


def split_up(number_of, total, reach, lean):
    portions = [(1 << 20) // math.isqrt(grade ** lean) + 1 for grade in range(2, number_of + 1)]
    surplus, given = total - reach - (number_of - 1), [1] * (number_of - 1)
    while surplus > 0:
        free = [i for i in range(number_of - 1) if given[i] < reach]
        whole, budget = sum([portions[i] for i in free]), surplus
        for i in free:
            extra = min(reach - given[i], max(1, budget * portions[i] // whole), surplus)
            given[i] = given[i] + extra
            surplus = surplus - extra
    return np.array([reach] + given)


def ragged(stream_key, amount, total, bound, slope):
    if amount == 2:
        one = jax.random.randint(stream_key, (), max(1, total - bound), min(bound, total - 1) + 1)
        return jnp.stack([one, total - one])
    sizes = jnp.asarray(split_up(amount, total, bound, slope), jnp.int32)
    twos = (amount - 1) // 2
    source_of, receiver = sizes[1:1 + 2 * twos:2], sizes[2:2 + 2 * twos:2]
    room = jnp.minimum(source_of - 1, bound - receiver)
    moved = jax.random.randint(jax.random.fold_in(stream_key, 1), (twos,), 0, 1 << 20) % (room + 1)
    sizes = sizes.at[1:1 + 2 * twos:2].set(source_of - moved).at[2:2 + 2 * twos:2].set(receiver + moved)
    return sizes[jax.random.permutation(jax.random.fold_in(stream_key, 2), amount)]


def scatter_about(key, extent, width, bound, split=(), kind=jnp.bfloat16):
    factor_of = level_of(key, extent, split, -0.22, 0.18) if split else 1.0
    result = jax.random.normal(key, extent, jnp.float32) * width * factor_of
    return jnp.minimum(jnp.maximum(result, -bound), bound).astype(kind)


def bell_draw_with(key, extent, scale, reach, cuts, heavy, kind=jnp.bfloat16):
    array = scale * jax.random.normal(key, extent, jnp.float32)
    if cuts:
        array = array * level_of(key, extent, cuts, -0.22, 0.18)
    return jnp.clip(with_spikes(array, jax.random.fold_in(key, 3), *heavy), -reach, reach).astype(kind)


def setup_inputs(seed: int = 0) -> dict:
    key_of = jax.random.split(jax.random.key(seed), 15)
    frames = scatter_about(key_of[0], (FRAMES, POS, D), 1.0, 6.0, ((0, 16),))
    cotangent = bell_draw_with(key_of[1], (FRAMES, POS, D), 1.0, 8.0, ((0, 16),), (0, 2, 16, 2.0))
    dialogue = jnp.searchsorted(jnp.cumsum(ragged(key_of[2], NDIAL, FRAMES, 4 * FR_DEV, 0)), jnp.arange(FRAMES), side="right").astype(jnp.int32)
    padding = plant((jax.random.randint(key_of[3], (FRAMES,), 0, 4) < 3).astype(jnp.int32), jax.random.fold_in(key_of[3], 1), 0, 1)
    position_set = draw_position_set(jax.random.fold_in(key_of[14], 71), 0)
    query_weight = scatter_about(key_of[5], (WSETS, D, HEADS * HDIM), D ** -0.5, 0.1875, ((1, 16), (2, 2)))
    key_weight = scatter_about(key_of[6], (WSETS, D, HEADS * HDIM), D ** -0.5, 0.1875, ((1, 16), (2, 2)))
    value_weight = scatter_about(key_of[7], (WSETS, D, HEADS * HDIM), D ** -0.5, 0.1875, ((1, 16), (2, 2)))
    output_weight = scatter_about(key_of[8], (WSETS, HEADS * HDIM, D), (HEADS * HDIM // 4) ** -0.5, 0.375, ((1, 2), (2, 16)))
    gate_weight = scatter_about(key_of[9], (WSETS, D, FF), D ** -0.5, 0.1875, ((1, 16), (2, 2)))
    up_weight = scatter_about(key_of[10], (WSETS, D, FF), D ** -0.5, 0.1875, ((1, 16), (2, 2)))
    down_weight = scatter_about(key_of[11], (WSETS, FF, D), FF ** -0.5, 0.109375, ((1, 2), (2, 16)))
    attention_gain = jnp.clip(1.0 + 0.15 * jax.random.normal(key_of[12], (WSETS, D), jnp.float32), 0.25, 1.75)
    feedforward_gain = jnp.clip(1.0 + 0.15 * jax.random.normal(key_of[13], (WSETS, D), jnp.float32), 0.25, 1.75)
    return dict(frames=frames, cotangent=cotangent, dialogue=dialogue, padding=padding, position_set=position_set, query_weight=query_weight, key_weight=key_weight, value_weight=value_weight, output_weight=output_weight, gate_weight=gate_weight, up_weight=up_weight, down_weight=down_weight, attention_gain=attention_gain, feedforward_gain=feedforward_gain)


epsilon = 1e-05
highest = lax.Precision.HIGHEST

@jax.custom_vjp
def low(v):
    return lax.optimization_barrier(v.astype(jnp.bfloat16)).astype(jnp.float32)

@jax.custom_vjp
def low_back(v):
    return v

def low_keep(v):
    return (low(v), None)

def low_pass(kept, grad):
    return (grad,)

def back_keep(v):
    return (v, None)

def back_low(kept, grad):
    return (low(grad),)
low.defvjp(low_keep, low_pass)
low_back.defvjp(back_keep, back_low)

def normalize(values, gain):
    return values * lax.rsqrt(lax.optimization_barrier(jnp.mean(values * values, axis=-1, keepdims=True)) + epsilon) * gain

def layer(block_rows, query_w, key_w, value_w, output_w, gate_w, up_w, down_w, first_gain, second_gain, position_set):

    def project(values, weight):
        return jnp.einsum('fpk,pke->fpe', values, weight[position_set], precision=highest)
    frame_count = block_rows.shape[0]
    head_shape = (frame_count, POS, HEADS, HDIM)
    normed = low(normalize(block_rows, first_gain[position_set][None]))
    queries = low(low_back(project(normed, query_w))).reshape(head_shape)
    key_rows = low(low_back(project(normed, key_w))).reshape(head_shape)
    value_rows = low(low_back(project(normed, value_w))).reshape(head_shape)
    scores = low_back(jnp.einsum('fphd,fqhd->fhpq', queries, key_rows, precision=highest) * HDIM ** (-0.5))
    causal = jnp.arange(POS)[:, None] >= jnp.arange(POS)[None, :]
    masked = jnp.where(causal, scores, -1e+30)
    attention_probs = low(jax.nn.softmax(masked, axis=-1))
    attended = jnp.einsum('fhpq,fqhd->fphd', attention_probs, value_rows, precision=highest)
    attended = low(low_back(attended.reshape(frame_count, POS, HEADS * HDIM)))
    hidden = block_rows + low_back(project(attended, output_w))
    normed_two = low(normalize(hidden, second_gain[position_set][None]))
    gated = low_back(project(normed_two, gate_w))
    upward = low_back(project(normed_two, up_w))
    active = low(jax.nn.silu(gated) * upward)
    return hidden + low_back(project(active, down_w))

def reference(frames, cotangent, dialogue, padding, position_set, query_weight, key_weight, value_weight, output_weight, gate_weight, up_weight, down_weight, attention_gain, feedforward_gain):
    unpadded = padding.astype(jnp.float32)
    dialogue_table = (dialogue[:, None] == jnp.arange(NDIAL, dtype=jnp.int32)[None, :]).astype(jnp.float32)
    counts = lax.optimization_barrier(jnp.sum(dialogue_table * unpadded[:, None], axis=0))
    per_frame = lax.optimization_barrier(jnp.sum(dialogue_table * counts[None, :], axis=1))
    loss_weight = unpadded * (FR_DEV * 1.0) / (per_frame + 1.0)
    params = tuple((argument.astype(jnp.float32) for argument in (query_weight, key_weight, value_weight, output_weight, gate_weight, up_weight, down_weight, attention_gain, feedforward_gain)))
    block_frames = math.gcd(FRAMES, 256)
    step_count = FRAMES // block_frames
    rows_all = frames.astype(jnp.float32).reshape(step_count, block_frames, POS, D)
    seeds = (cotangent.astype(jnp.float32) * loss_weight[:, None, None]).reshape(step_count, block_frames, POS, D)

    def forward(rows_in, *weights):
        return layer(rows_in, *weights, position_set)

    def visit_block(running, pieces):
        block_rows, seed_rows = pieces
        output, pullback = jax.vjp(forward, block_rows, *params)
        gradients = pullback(seed_rows)
        running = tuple((prior + added for prior, added in zip(running, gradients[1:])))
        return (running, (output.astype(jnp.bfloat16), gradients[0].astype(jnp.bfloat16)))
    initial = tuple((jnp.zeros(argument.shape, jnp.float32) for argument in params))
    totals, (outputs, input_grads) = lax.scan(visit_block, initial, (rows_all, seeds))
    return (outputs.reshape(FRAMES, POS, D), input_grads.reshape(FRAMES, POS, D), totals[0], totals[1], totals[2], totals[3], totals[4], totals[5], totals[6], totals[7], totals[8])
```

```python
import jax
import jax.numpy as jnp
from jax import lax
from jax.experimental import pallas as pl
from jax.experimental.pallas import tpu as pltpu
from jax.sharding import PartitionSpec as P

HDIM = 64
EPSILON = 1e-05
INNER = 16
ZN = 4
LANES = 128
MESH = pl.DeviceIdType.MESH
BF = jnp.bfloat16
F32 = jnp.float32
NN = (((1,), (0,)), ((), ()))
NT = (((1,), (1,)), ((), ()))
TN = (((0,), (0,)), ((), ()))


def dot(a, b, dims=NN):
    return lax.dot_general(a, b, dims, preferred_element_type=F32)


def layer_kernel(
    frames, cot, dialogue, padding, table, set_mask, gain_one, gain_two,
    wq, wk, wv, wo, wg, wu, wd,
    mixed, frames_grad, dq, dk, dv, do, dg, du, dd, gains_grad,
    st1, st2, ga1, ga2, w1, w2,
    n1, sd, n2, hl, pf,
    sb, sr, so, ru, rd,
    qs, ks, vs, att, probs, act, gg, ug, gt, up,
    dw1, dw2, re1, re2, fi1, fi2,
    cnt, gain_col, gain_face, halves,
    u_one, u_two, hid, hgrad, small,
    z1_s, z1_r, z2_s, z2_r, m1_s, m1_r, m2_s, m2_r,
    ag_s, ag_r, rs_sib_s, rs_sib_r, rs_s, rs_ru, rs_rd,
    gr_s, gr_r, gf_s, gf_r, c_s, c_r, y_s, y_r, gcs, gcr, gfs, gfr,
):
    idx = lax.axis_index("dp")
    y = lax.axis_index("tensor")
    inner = lax.rem(idx, INNER)
    base = idx - inner
    z = lax.div(inner, 4)
    x = lax.rem(lax.div(inner, 2), 2)
    c = lax.rem(inner, 2)

    def dev(zz, xx, cc, yy):
        return (base + zz * 4 + xx * 2 + cc, yy)

    def flip(v, bit):
        return 1 - v if bit else v

    def remote(src, dst, ssem, rsem, device):
        return pltpu.make_async_remote_copy(
            src_ref=src, dst_ref=dst, send_sem=ssem, recv_sem=rsem,
            device_id=device, device_id_type=MESH,
        )

    me = dev(z, x, c, y)
    sibling = dev(z, x, 1 - c, y)
    above = dev(lax.rem(z + 1, ZN), x, c, y)
    below = dev(lax.rem(z + ZN - 1, ZN), x, c, y)
    column = [dev(lax.rem(z + k, ZN), x, c, y) for k in (1, 2, 3)]
    face = [
        (flip(x, a), flip(c, b), flip(y, d))
        for a in (0, 1) for b in (0, 1) for d in (0, 1) if a or b or d
    ]
    rows = n1.shape[1]
    group = 8 * rows
    width = n1.shape[2]
    half = rows // 16
    qb = w1.shape[2] // 4
    fb = w2.shape[2] // 3
    hidden_units = wg.shape[2]
    d_rows = wq.shape[1]
    own_slot = 2 * z + c
    mine = pl.ds(half * y, half)
    slice_mine = 2 * x + c
    pending = []

    def send(cond, src, dst, ssem, rsem, device):
        def go():
            remote(src, dst, ssem, rsem, device).start()

        def done():
            remote(src, dst, ssem, rsem, device).wait_send()

        if cond is None:
            go()
        else:
            pl.when(cond)(go)
        pending.append((cond, done))

    def arrived(dst, rsem):
        remote(dst, dst, rsem, rsem, sibling).wait_recv()

    barrier = pltpu.get_barrier_semaphore()
    for d in column:
        pl.semaphore_signal(barrier, inc=1, device_id=d, device_id_type=MESH)
    for xx, cc, yy in face:
        pl.semaphore_signal(barrier, inc=1, device_id=dev(z, xx, cc, yy), device_id_type=MESH)

    eye = (
        lax.broadcasted_iota(jnp.int32, (d_rows, d_rows), 0)
        == lax.broadcasted_iota(jnp.int32, (d_rows, d_rows), 1)
    ).astype(BF)
    for s in range(2):
        wot = dot(eye, wo[s], NT).astype(BF)
        for b in range(ZN):
            part = slice(b * qb, (b + 1) * qb)
            st1[b, s, :, 0:qb] = wq[s, :, part]
            st1[b, s, :, qb:2 * qb] = wk[s, :, part]
            st1[b, s, :, 2 * qb:3 * qb] = wv[s, :, part]
            st1[b, s, :, 3 * qb:4 * qb] = wot[:, part]

    def zero(ref):
        ref[...] = jnp.zeros_like(ref)

    pl.when(z == 0)(lambda: zero(ru))
    pl.when(z == ZN - 1)(lambda: zero(rd))

    pl.semaphore_wait(barrier, len(column) + len(face))

    def spread(st, ga, ssem, rsem):
        for k in (1, 2, 3):
            zz = lax.rem(z + k, ZN)
            send(None, st.at[zz], ga.at[z], ssem.at[k], rsem.at[z], dev(zz, x, c, y))

    def multicast(src, zz, w, ssem, rsem):
        piece = zz * 4 + slice_mine
        dst = w.at[:, pl.ds(pl.multiple_of(piece * d_rows, d_rows), d_rows), :]
        for a in (0, 1):
            for b in (0, 1):
                target = dev(z, flip(x, a), y, flip(y, b))
                sem = ssem.at[zz, 2 * a + b]
                if a or b:
                    send(None, src, dst, sem, rsem.at[piece], target)
                else:
                    send(c != y, src, dst, sem, rsem.at[piece], sibling)
                    local = pltpu.make_async_copy(src, dst, rsem.at[piece])
                    pl.when(c == y)(local.start)

    def weights_here(w, rsem):
        for piece in range(INNER):
            arrived(w.at[:, pl.ds(piece * d_rows, d_rows), :], rsem.at[piece])

    spread(st1, ga1, z1_s, z1_r)
    multicast(st1.at[z], z, w1, m1_s, m1_r)

    def gain_full(gain):
        m1 = set_mask[1].astype(F32)[:, 0:1]
        g0 = gain[0:1, :]
        g1 = gain[1:2, :]
        return jnp.where(m1 > 0.5, g1, g0)

    def tile_rows(v):
        return jnp.broadcast_to(v[None], (half, 16, v.shape[1])).reshape(rows, v.shape[1])

    def normalize(values, gain):
        inverse = lax.rsqrt(jnp.sum(values * values, axis=-1, keepdims=True) / width + EPSILON)
        unit = values * inverse
        return unit, inverse, (unit * tile_rows(gain_full(gain))).astype(BF)

    block = frames[mine].reshape(rows, width).astype(F32)
    unit, inverse, normed = normalize(block, gain_one)
    u_one[...] = unit
    small[0] = jnp.broadcast_to(inverse, (rows, LANES))
    n1[own_slot] = normed

    def gather_start(which, buf):
        s, r = ag_s.at[which], ag_r.at[which]
        src = buf.at[own_slot]
        send(z < ZN - 1, src, src, s.at[own_slot, 1], r.at[own_slot], above)
        send(z > 0, src, src, s.at[own_slot, 2], r.at[own_slot], below)
        send(None, src, src, s.at[own_slot, 0], r.at[own_slot], sibling)

    def gather_step(which, buf, k):
        s, r = ag_s.at[which], ag_r.at[which]

        def from_below():
            slot = 2 * (z - k) + c
            arrived(buf.at[slot], r.at[slot])

        def from_above():
            slot = 2 * (z + k) + c
            arrived(buf.at[slot], r.at[slot])

        pl.when(z >= k)(from_below)
        lo = 2 * jnp.maximum(z - k, 0) + c
        send((z >= k) & (z < ZN - 1), buf.at[lo], buf.at[lo], s.at[lo, 1], r.at[lo], above)
        send(z >= k, buf.at[lo], buf.at[lo], s.at[lo, 0], r.at[lo], sibling)
        pl.when(z + k <= ZN - 1)(from_above)
        hi = 2 * jnp.minimum(z + k, ZN - 1) + c
        send((z + k <= ZN - 1) & (z > 0), buf.at[hi], buf.at[hi], s.at[hi, 2], r.at[hi], below)
        send(z + k <= ZN - 1, buf.at[hi], buf.at[hi], s.at[hi, 0], r.at[hi], sibling)

    def gather_end(which, buf):
        for zz in range(ZN):
            slot = 2 * zz + (1 - c)
            arrived(buf.at[slot], ag_r.at[which, slot])

    gather_start(0, n1)

    cnt[0, z] = table[...]
    for k in (1, 2, 3):
        send(None, table, cnt.at[0, z], c_s.at[0, k], c_r.at[0, z], dev(lax.rem(z + k, ZN), x, c, y))

    for k in (1, 2, 3):
        zz = lax.rem(z + k, ZN)
        arrived(ga1.at[zz], z1_r.at[zz])
        multicast(ga1.at[zz], zz, w1, m1_s, m1_r)
        gather_step(0, n1, k)

    for k in (1, 2, 3):
        zz = lax.rem(z + k, ZN)
        arrived(cnt.at[0, zz], c_r.at[0, zz])
    cnt[1, slice_mine] = cnt[0, 0] + cnt[0, 1] + cnt[0, 2] + cnt[0, 3]
    for a, b in ((0, 1), (1, 0), (1, 1)):
        send(None, cnt.at[1, slice_mine], cnt.at[1, slice_mine], c_s.at[1, 2 * a + b], c_r.at[1, slice_mine],
             dev(z, flip(x, a), flip(c, b), y))

    for s in range(2):
        wdt = dot(eye, wd[s], NT).astype(BF)
        for b in range(ZN):
            n = min(fb, hidden_units - b * fb)
            part = slice(b * fb, b * fb + n)
            for j, v in enumerate((wg[s, :, part], wu[s, :, part], wdt[:, part])):
                st2[b, s, :, j * fb:j * fb + n] = v
                if n < fb:
                    st2[b, s, :, j * fb + n:(j + 1) * fb] = jnp.zeros((d_rows, fb - n), BF)
    spread(st2, ga2, z2_s, z2_r)
    multicast(st2.at[z], z, w2, m2_s, m2_r)

    for a, b in ((0, 1), (1, 0), (1, 1)):
        j = 2 * flip(x, a) + flip(c, b)
        arrived(cnt.at[1, j], c_r.at[1, j])
    counts = cnt[1, 0] + cnt[1, 1] + cnt[1, 2] + cnt[1, 3]
    lane = lax.broadcasted_iota(jnp.int32, (8, LANES), 1)
    unpadded = padding[...].astype(F32)
    per_frame = jnp.sum(jnp.where(dialogue[...] == lane, counts, 0.0), axis=1, keepdims=True)
    loss = unpadded * (frames.shape[0] * 1.0) / (per_frame + 1.0)
    small[1, 0:8, :] = loss
    loss_mine = small[1, mine, :]
    weight_rows = jnp.broadcast_to(loss_mine[:, None, 0:1], (half, 16, width)).reshape(rows, width)
    seed = cot[mine].reshape(rows, width).astype(F32) * weight_rows
    sd[own_slot] = seed.astype(BF)
    gather_start(1, sd)
    gather_end(0, n1)

    def masked(v, s):
        n = v.shape[1]
        m = set_mask[s]
        m = m if n == width else m[:, 0:n]
        return (v.reshape(group // 16, 16, n) * m[None]).reshape(group, n)

    def flat(buf):
        return buf[...].reshape(group, width)

    weights_here(w1, m1_r)
    qkv = dot(masked(flat(n1), 0), w1[0, :, 0:3 * qb]) + dot(masked(flat(n1), 1), w1[1, :, 0:3 * qb])
    qkv = qkv.astype(BF)
    qs[...] = qkv[:, 0:qb]
    ks[...] = qkv[:, qb:2 * qb]
    vs[...] = qkv[:, 2 * qb:3 * qb]

    bl = LANES
    r_at = lax.broadcasted_iota(jnp.int32, (bl, bl), 0)
    c_at = lax.broadcasted_iota(jnp.int32, (bl, bl), 1)
    seen = (c_at <= r_at) & (lax.div(r_at, 16) == lax.div(c_at, 16))
    heads = qb // HDIM
    head_of = lax.div(lax.broadcasted_iota(jnp.int32, (bl, qb), 1), HDIM)
    scale = HDIM ** (-0.5)

    def only(v, h):
        return jnp.where(head_of == h, v, jnp.zeros_like(v))

    for t in range(group // bl):
        rs_ = pl.ds(t * bl, bl)
        q, kk, v = qs[rs_, :], ks[rs_, :], vs[rs_, :]
        out = jnp.zeros((bl, qb), F32)
        for h in range(heads):
            scores = dot(only(q, h), kk, NT) * scale
            scores = jnp.where(seen, scores, -1e30)
            e = jnp.exp(scores - jnp.max(scores, axis=-1, keepdims=True))
            e = jnp.where(seen, e, 0.0)
            p = e / jnp.sum(e, axis=-1, keepdims=True)
            probs[t, h] = p
            out = jnp.where(head_of == h, dot(p.astype(BF), v), out)
        att[rs_, :] = out.astype(BF)

    def scatter_start(n):
        for b in (3, 0, 2, 1):
            sb[n, b] = pf[2 * b + 1 - c].astype(BF)
            send(None, sb.at[n, b], sr.at[n, b], rs_sib_s.at[n, b], rs_sib_r.at[n, b], sibling)

    def chip_sum(n, b):
        arrived(sr.at[n, b], rs_sib_r.at[n, b])
        return pf[2 * b + c] + sr[n, b].astype(F32)

    def scatter_chain(n):
        for rising, b in ((True, 3), (False, 0), (True, 2), (False, 1), (True, 1), (False, 2)):
            if rising:
                cond, inflow, buf, r, target = b > z, z > 0, ru, rs_ru, above
            else:
                cond, inflow, buf, r, target = b < z, z < ZN - 1, rd, rs_rd, below

            def step(b=b, inflow=inflow, buf=buf, r=r):
                total = chip_sum(n, b)
                pl.when(inflow)(lambda: arrived(buf.at[n, b], r.at[n, b]))
                so[n, b] = (total + buf[n, b].astype(F32)).astype(BF)

            pl.when(cond)(step)
            send(cond, so.at[n, b], buf.at[n, b], rs_s.at[n, b], r.at[n, b], target)

    def scatter_end(n):
        total = chip_sum(n, z)
        pl.when(z > 0)(lambda: arrived(ru.at[n, z], rs_ru.at[n, z]))
        pl.when(z < ZN - 1)(lambda: arrived(rd.at[n, z], rs_rd.at[n, z]))
        return total + ru[n, z].astype(F32) + rd[n, z].astype(F32)

    def put_partial(v):
        pf[...] = v.reshape(8, rows, width)

    put_partial(
        dot(masked(att[...], 0), w1[0, :, 3 * qb:4 * qb], NT)
        + dot(masked(att[...], 1), w1[1, :, 3 * qb:4 * qb], NT)
    )
    scatter_start(0)
    gather_step(1, sd, 1)
    scatter_chain(0)
    attention = scatter_end(0)

    hidden = block + attention
    hid[...] = hidden
    unit, inverse, normed = normalize(hidden, gain_two)
    u_two[...] = unit
    small[2] = jnp.broadcast_to(inverse, (rows, LANES))
    n2[own_slot] = normed
    gather_start(2, n2)
    for k in (1, 2, 3):
        gather_step(2, n2, k)

    for k in (2, 3):
        gather_step(1, sd, k)
    for k in (1, 2, 3):
        zz = lax.rem(z + k, ZN)
        arrived(ga2.at[zz], z2_r.at[zz])
        multicast(ga2.at[zz], zz, w2, m2_s, m2_r)
    gather_end(1, sd)
    weights_here(w2, m2_r)
    gather_end(2, n2)

    g0, u0, d0 = slice(0, fb), slice(fb, 2 * fb), slice(2 * fb, 3 * fb)
    gu = dot(masked(flat(n2), 0), w2[0, :, 0:2 * fb]) + dot(masked(flat(n2), 1), w2[1, :, 0:2 * fb])
    gt[...] = gu[:, 0:fb]
    up[...] = gu[:, fb:2 * fb]
    active_grad = dot(masked(flat(sd), 0), w2[0, :, d0]) + dot(masked(flat(sd), 1), w2[1, :, d0])
    gate = gt[...]
    sig = jax.nn.sigmoid(gate)
    silu = gate * sig
    act[...] = (silu * up[...]).astype(BF)
    gg[...] = (active_grad * up[...] * sig * (1.0 + gate * (1.0 - sig))).astype(BF)
    ug[...] = (active_grad * silu).astype(BF)

    put_partial(
        dot(masked(gg[...], 0), w2[0, :, g0], NT)
        + dot(masked(gg[...], 1), w2[1, :, g0], NT)
        + dot(masked(ug[...], 0), w2[0, :, u0], NT)
        + dot(masked(ug[...], 1), w2[1, :, u0], NT)
    )
    scatter_start(1)

    def reduce_send(n, dw, re, lo, cols):
        for a in (0, 1):
            for b in (0, 1):
                xx, cc = flip(x, a), flip(c, b)
                src = dw.at[:, :, 2 * xx + cc, :, pl.ds(lo, cols)]
                dst = re.at[2 * x + y, :, :, :, pl.ds(lo, cols)]
                rsem = gr_r.at[n, 2 * x + y]
                if a or b:
                    send(None, src, dst, gr_s.at[n, 2 * a + b], rsem, dev(z, xx, cc, c))
                else:
                    send(c != y, src, dst, gr_s.at[n, 0], rsem, dev(z, x, c, c))
                    local = pltpu.make_async_copy(src, dst, rsem)
                    pl.when(c == y)(local.start)

    def reduce_sum(n, re, fi, lo, cols):
        cs = pl.ds(lo, cols)
        for j in range(4):
            arrived(re.at[j, :, :, :, cs], gr_r.at[n, j])
        for k in (1, 2, 3, 0):
            zz = lax.rem(z + k, ZN)
            for s in range(2):
                total = re[0, s, zz, :, cs].astype(F32)
                for j in (1, 2, 3):
                    total = total + re[j, s, zz, :, cs].astype(F32)
                if k:
                    re[0, s, zz, :, cs] = total.astype(BF)
                else:
                    fi[z, s, :, cs] = total.astype(BF)
            if k:
                send(None, re.at[0, :, zz, :, cs], fi.at[z, :, :, cs], gf_s.at[n, k], gf_r.at[n, z],
                     dev(zz, x, c, y))

    def reduce_end(n, fi, lo, cols):
        for k in (1, 2, 3):
            zz = lax.rem(z + k, ZN)
            arrived(fi.at[zz, :, :, pl.ds(lo, cols)], gf_r.at[n, zz])

    def weight_grad(dw, lo, cols, values, grads):
        for s in range(2):
            product = dot(masked(values, s), grads, TN).astype(BF)
            dw[s, :, :, :, pl.ds(lo, cols)] = product.reshape(ZN, 4, d_rows, cols)

    scatter_chain(1)
    normed_two_grad = scatter_end(1)

    def set_sums(v, at):
        three = v.reshape(half, 16, width)
        for s in range(2):
            m = set_mask[s].astype(F32)
            gain_col[z, at + s:at + s + 1, :] = jnp.sum(
                (three * m[None]).reshape(rows, width), axis=0, keepdims=True
            )

    def norm_back(gradient, gain, unit, inverse):
        scaled = gradient * tile_rows(gain_full(gain))
        return inverse * (scaled - unit * (jnp.sum(scaled * unit, axis=-1, keepdims=True) / width))

    gain_col[z] = jnp.zeros((8, width), F32)
    unit = u_two[...]
    set_sums(normed_two_grad * unit, 2)
    seed = cot[mine].reshape(rows, width).astype(F32) * weight_rows
    hidden_grad = seed + norm_back(normed_two_grad, gain_two, unit, small[2][:, 0:1])
    hgrad[...] = hidden_grad
    hl[own_slot] = hidden_grad.astype(BF)
    gather_start(3, hl)

    put_partial(
        dot(masked(act[...], 0), w2[0, :, d0], NT)
        + dot(masked(act[...], 1), w2[1, :, d0], NT)
    )
    scatter_start(2)
    gather_step(3, hl, 1)
    weight_grad(dw2, 2 * fb, fb, flat(sd), act[...])
    reduce_send(0, dw2, re2, 2 * fb, fb)
    gather_step(3, hl, 2)
    weight_grad(dw2, 0, fb, flat(n2), gg[...])
    gather_step(3, hl, 3)
    weight_grad(dw2, fb, fb, flat(n2), ug[...])
    reduce_send(1, dw2, re2, 0, 2 * fb)
    gather_end(3, hl)

    attended_grad = dot(masked(flat(hl), 0), w1[0, :, 3 * qb:4 * qb]) + dot(
        masked(flat(hl), 1), w1[1, :, 3 * qb:4 * qb]
    )
    datt = attended_grad.astype(BF)
    gq, gk, gv = [], [], []
    for t in range(group // bl):
        rs_ = pl.ds(t * bl, bl)
        q, kk, v = qs[rs_, :], ks[rs_, :], vs[rs_, :]
        da = datt[t * bl:(t + 1) * bl, :]
        tq = jnp.zeros((bl, qb), F32)
        tk, tv = tq, tq
        for h in range(heads):
            p = probs[t, h]
            dp_ = dot(only(da, h), v, NT)
            tv = jnp.where(head_of == h, dot(p.astype(BF), da, TN), tv)
            ds_ = (p * (dp_ - jnp.sum(dp_ * p, axis=-1, keepdims=True))).astype(BF)
            tq = jnp.where(head_of == h, dot(ds_, kk) * scale, tq)
            tk = jnp.where(head_of == h, dot(ds_, q, TN) * scale, tk)
        gq.append(tq.astype(BF))
        gk.append(tk.astype(BF))
        gv.append(tv.astype(BF))
    for t in range(group // bl):
        rs_ = pl.ds(t * bl, bl)
        qs[rs_, :] = gq[t]
        ks[rs_, :] = gk[t]
        vs[rs_, :] = gv[t]
    total = None
    for s in range(2):
        for j, ref in enumerate((qs, ks, vs)):
            term = dot(masked(ref[...], s), w1[s, :, j * qb:(j + 1) * qb], NT)
            total = term if total is None else total + term
    scatter_chain(2)
    branch = scatter_end(2)
    put_partial(total)
    scatter_start(3)
    weight_grad(dw1, 3 * qb, qb, flat(hl), att[...])
    for j, ref in enumerate((qs, ks, vs)):
        weight_grad(dw1, j * qb, qb, flat(n1), ref[...])
    reduce_send(2, dw1, re1, 0, 4 * qb)

    halves[0, mine] = (hid[...] + branch).astype(BF).reshape(half, 16, width)
    other = dev(z, x, c, 1 - y)
    send(None, halves.at[0, mine], halves.at[0, mine], y_s.at[0], y_r.at[0], other)

    scatter_chain(3)
    normed_one_grad = scatter_end(3)
    unit = u_one[...]
    set_sums(normed_one_grad * unit, 0)
    for k in (1, 2, 3):
        send(None, gain_col.at[z], gain_col.at[z], gcs.at[k], gcr.at[z], dev(lax.rem(z + k, ZN), x, c, y))
    result = hgrad[...] + norm_back(normed_one_grad, gain_one, unit, small[0][:, 0:1])
    halves[1, mine] = result.astype(BF).reshape(half, 16, width)
    send(None, halves.at[1, mine], halves.at[1, mine], y_s.at[1], y_r.at[1], other)

    reduce_sum(0, re2, fi2, 2 * fb, fb)
    reduce_sum(1, re2, fi2, 0, 2 * fb)
    reduce_sum(2, re1, fi1, 0, 4 * qb)

    for k in (1, 2, 3):
        zz = lax.rem(z + k, ZN)
        arrived(gain_col.at[zz], gcr.at[zz])
    place = 4 * x + 2 * c + y
    gain_face[place] = gain_col[0] + gain_col[1] + gain_col[2] + gain_col[3]
    for k, (xx, cc, yy) in enumerate(face):
        send(None, gain_face.at[place], gain_face.at[place], gfs.at[k], gfr.at[place], dev(z, xx, cc, yy))

    reduce_end(0, fi2, 2 * fb, fb)
    for b in range(ZN):
        n = min(fb, hidden_units - b * fb)
        both = fi2[b, :, :, d0].reshape(2 * d_rows, fb).astype(F32).T
        for s in range(2):
            dd[s, b * fb:b * fb + n, :] = both[0:n, s * d_rows:(s + 1) * d_rows]
    reduce_end(1, fi2, 0, 2 * fb)
    for b in range(ZN):
        n = min(fb, hidden_units - b * fb)
        dg[:, :, b * fb:b * fb + n] = fi2[b, :, :, 0:n].astype(F32)
        du[:, :, b * fb:b * fb + n] = fi2[b, :, :, fb:fb + n].astype(F32)
    reduce_end(2, fi1, 0, 4 * qb)
    for b in range(ZN):
        part = slice(b * qb, (b + 1) * qb)
        dq[:, :, part] = fi1[b, :, :, 0:qb].astype(F32)
        dk[:, :, part] = fi1[b, :, :, qb:2 * qb].astype(F32)
        dv[:, :, part] = fi1[b, :, :, 2 * qb:3 * qb].astype(F32)
        both = fi1[b, :, :, 3 * qb:4 * qb].reshape(2 * d_rows, qb).astype(F32).T
        for s in range(2):
            do[s, part, :] = both[:, s * d_rows:(s + 1) * d_rows]

    for j, out in ((0, mixed), (1, frames_grad)):
        theirs = pl.ds(half * (1 - y), half)
        arrived(halves.at[j, theirs], y_r.at[j])
        out[...] = halves[j]
    for xx, cc, yy in face:
        j = 4 * xx + 2 * cc + yy
        arrived(gain_face.at[j], gfr.at[j])
    total = gain_face[0]
    for j in range(1, 8):
        total = total + gain_face[j]
    gains_grad[...] = total

    for cond, done in pending:
        if cond is None:
            done()
        else:
            pl.when(cond)(done)


def run_layer(frames, cot, dialogue, padding, table, set_mask, gain_one, gain_two, weights):
    wq, wk, wv, wo, wg, wu, wd = weights
    width = frames.shape[2]
    rows = frames.shape[0] * frames.shape[1] // 2
    d_rows = wq.shape[1]
    qb = wq.shape[2] // ZN
    units = wg.shape[2]
    fb = -(-units // (ZN * LANES)) * LANES
    group = 8 * rows
    dma = pltpu.SemaphoreType.DMA
    vm = pltpu.VMEM
    out_shape = [
        jax.ShapeDtypeStruct(frames.shape, BF),
        jax.ShapeDtypeStruct(frames.shape, BF),
        jax.ShapeDtypeStruct(wq.shape, F32),
        jax.ShapeDtypeStruct(wk.shape, F32),
        jax.ShapeDtypeStruct(wv.shape, F32),
        jax.ShapeDtypeStruct(wo.shape, F32),
        jax.ShapeDtypeStruct(wg.shape, F32),
        jax.ShapeDtypeStruct(wu.shape, F32),
        jax.ShapeDtypeStruct(wd.shape, F32),
        jax.ShapeDtypeStruct((8, width), F32),
    ]
    scratch = [
        vm((ZN, 2, d_rows, 4 * qb), BF), vm((ZN, 2, d_rows, 3 * fb), BF),
        vm((ZN, 2, d_rows, 4 * qb), BF), vm((ZN, 2, d_rows, 3 * fb), BF),
        vm((2, width, 4 * qb), BF), vm((2, width, 3 * fb), BF),
        vm((8, rows, width), BF), vm((8, rows, width), BF), vm((8, rows, width), BF), vm((8, rows, width), BF),
        vm((8, rows, width), F32),
        vm((4, 4, rows, width), BF), vm((4, 4, rows, width), BF), vm((4, 4, rows, width), BF),
        vm((4, 4, rows, width), BF), vm((4, 4, rows, width), BF),
        vm((group, qb), BF), vm((group, qb), BF), vm((group, qb), BF), vm((group, qb), BF),
        vm((group // LANES, qb // HDIM, LANES, LANES), F32),
        vm((group, fb), BF), vm((group, fb), BF), vm((group, fb), BF), vm((group, fb), F32), vm((group, fb), F32),
        vm((2, ZN, 4, d_rows, 4 * qb), BF), vm((2, ZN, 4, d_rows, 3 * fb), BF),
        vm((4, 2, ZN, d_rows, 4 * qb), BF), vm((4, 2, ZN, d_rows, 3 * fb), BF),
        vm((ZN, 2, d_rows, 4 * qb), BF), vm((ZN, 2, d_rows, 3 * fb), BF),
        vm((2, 4, 8, LANES), F32), vm((ZN, 8, width), F32), vm((8, 8, width), F32),
        vm((2,) + frames.shape, BF),
        vm((rows, width), F32), vm((rows, width), F32), vm((rows, width), F32), vm((rows, width), F32),
        vm((3, rows, LANES), F32),
        dma((4,)), dma((4,)), dma((4,)), dma((4,)),
        dma((4, 4)), dma((INNER,)), dma((4, 4)), dma((INNER,)),
        dma((4, 8, 3)), dma((4, 8)),
        dma((4, 4)), dma((4, 4)), dma((4, 4)), dma((4, 4)), dma((4, 4)),
        dma((3, 4)), dma((3, 4)), dma((3, 4)), dma((3, 4)),
        dma((2, 4)), dma((2, 4)), dma((2,)), dma((2,)),
        dma((4,)), dma((4,)), dma((8,)), dma((8,)),
    ]
    spec = pl.BlockSpec(memory_space=pltpu.VMEM)
    return pl.pallas_call(
        layer_kernel,
        out_shape=out_shape,
        in_specs=[spec] * 15,
        out_specs=[spec] * 10,
        scratch_shapes=scratch,
        compiler_params=pltpu.CompilerParams(
            collective_id=0, has_side_effects=True, vmem_limit_bytes=63 * 2**20
        ),
        cost_estimate=pl.CostEstimate(flops=10**10, bytes_accessed=10**7, transcendentals=0),
        name="layer",
    )(frames, cot, dialogue, padding, table, set_mask, gain_one, gain_two, wq, wk, wv, wo, wg, wu, wd)


def per_device(
    frames, cotangent, dialogue, padding, position_set,
    query_weight, key_weight, value_weight, output_weight, gate_weight, up_weight, down_weight,
    attention_gain, feedforward_gain,
):
    dp = lax.axis_size("dp")
    outer = dp // INNER
    groups = [[o * INNER + i for o in range(outer)] for i in range(INNER)]
    weights = [query_weight, key_weight, value_weight, output_weight, gate_weight, up_weight, down_weight]
    axes = [1, 1, 1, 2, 1, 1, 2]
    width = frames.shape[-1]

    def to_kernel(v):
        if outer == 1:
            return v
        cut = v.reshape(v.shape[:-1] + (outer, INNER, width // dp))
        return jnp.swapaxes(cut, -3, -2).reshape(v.shape)

    def from_kernel(v):
        if outer == 1:
            return v
        cut = v.reshape(v.shape[:-1] + (INNER, outer, width // dp))
        return jnp.swapaxes(cut, -3, -2).reshape(v.shape)

    if outer > 1:
        weights = [
            lax.all_gather(w, "dp", axis=a, tiled=True, axis_index_groups=groups) for w, a in zip(weights, axes)
        ]
    unpadded = padding.astype(F32)
    hit = dialogue[:, None] == jnp.arange(LANES, dtype=jnp.int32)[None, :]
    table = jnp.sum(jnp.where(hit, unpadded[:, None], 0.0), axis=0, keepdims=True)
    if outer > 1:
        table = lax.psum(table, "dp", axis_index_groups=groups)
    table = jnp.broadcast_to(table, (8, LANES))
    set_mask = jnp.stack([position_set == s for s in range(2)]).astype(BF)
    set_mask = jnp.broadcast_to(set_mask[:, :, None], set_mask.shape + (width,))
    (mixed, frames_grad, *grads, gains) = run_layer(
        to_kernel(frames), to_kernel(cotangent),
        jnp.broadcast_to(dialogue[:, None], (dialogue.shape[0], LANES)),
        jnp.broadcast_to(padding[:, None], (padding.shape[0], LANES)),
        table, set_mask, to_kernel(attention_gain), to_kernel(feedforward_gain), weights,
    )
    index = lax.axis_index("dp")
    gains = gains[0:4]
    if outer > 1:
        grads = [
            lax.psum_scatter(g, "dp", scatter_dimension=a, tiled=True, axis_index_groups=groups)
            for g, a in zip(grads, axes)
        ]
        gains = from_kernel(lax.psum(gains, "dp", axis_index_groups=groups))
    gains = lax.dynamic_slice_in_dim(gains, index * (width // dp), width // dp, axis=1)
    return (from_kernel(mixed), from_kernel(frames_grad), *grads, gains[0:2], gains[2:4])


def solution(mesh):
    column = P(None, "dp", "tensor")
    row = P(None, "tensor", "dp")
    rows = P("dp", None, None)
    in_specs = (
        rows, rows, P("dp"), P("dp"), P(),
        column, column, column, row, column, column, row, P(), P(),
    )
    out_specs = (
        rows, rows, column, column, column, row, column, column, row, P(None, "dp"), P(None, "dp"),
    )
    return jax.shard_map(per_device, mesh=mesh, in_specs=in_specs, out_specs=out_specs, check_vma=False)
```

```python
import jax
import jax.numpy as jnp
from jax import lax
from jax.experimental import pallas as pl
from jax.experimental.pallas import tpu as pltpu
from jax.sharding import PartitionSpec as P

HDIM = 64
EPSILON = 1e-05
INNER = 16
ZN = 4
LANES = 128
CUTS = 2
MESH = pl.DeviceIdType.MESH
BF = jnp.bfloat16
F32 = jnp.float32
NN = (((1,), (0,)), ((), ()))
NT = (((1,), (1,)), ((), ()))
TN = (((0,), (0,)), ((), ()))
QKV, OUT, UPS, DOWN = range(4)


def dot(a, b, dims=NN):
    return lax.dot_general(a, b, dims, preferred_element_type=F32)


def layer_kernel(
    frames, cot, dialogue, padding, position_set, gain_one, gain_two,
    wq, wk, wv, wo, wg, wu, wd,
    fi0, fi1, fi2, fi3, halves, gains_out,
    st0, st1, st2, st3, ga0, ga1, ga2, ga3, w0, w1, w2, w3,
    dw0, dw1, dw2, dw3, rc0, rc1, rc2, rc3, sx0, sx1, sx2, sx3, rx0, rx1, rx2, rx3,
    set_mask, n1, sd, n2, hl, pf,
    sb, sr, so, ru, rd,
    qs, ks, vs, att2, probs, act2, gu2, gt, up,
    cnt, gain_col, gain_face,
    u_one, u_two, hid, hgrad, small,
    sp_s, sp_r, mc_s, mc_r, fw_s, ag_s, ag_r, rs_sib_s, rs_sib_r, rs_s, rs_ru, rs_rd,
    gc_s, gc_r, gx_s, gx_r, gf_s, gf_r, c_s, c_r, y_s, y_r, gcs, gcr, gfs, gfr,
):
    st, ga, w = (st0, st1, st2, st3), (ga0, ga1, ga2, ga3), (w0, w1, w2, w3)
    dw, fi = (dw0, dw1, dw2, dw3), (fi0, fi1, fi2, fi3)
    rc, sx, rx = (rc0, rc1, rc2, rc3), (sx0, sx1, sx2, sx3), (rx0, rx1, rx2, rx3)
    idx = lax.axis_index("dp")
    y = lax.axis_index("tensor")
    inner = lax.rem(idx, INNER)
    base = idx - inner
    z = lax.div(inner, 4)
    x = lax.rem(lax.div(inner, 2), 2)
    c = lax.rem(inner, 2)

    def dev(zz, xx, cc, yy):
        return (base + zz * 4 + xx * 2 + cc, yy)

    def flip(v, bit):
        return 1 - v if bit else v

    def hop(k):
        return lax.rem(z + k, ZN)

    def remote(src, dst, ssem, rsem, device):
        return pltpu.make_async_remote_copy(
            src_ref=src, dst_ref=dst, send_sem=ssem, recv_sem=rsem,
            device_id=device, device_id_type=MESH,
        )

    partner = dev(z, x, c, 1 - y)
    sibling = dev(z, x, 1 - c, y)
    across = dev(z, 1 - x, c, y)
    above = dev(hop(1), x, c, y)
    below = dev(hop(ZN - 1), x, c, y)
    column = [dev(hop(k), x, c, y) for k in (1, 2, 3)]
    face = [
        (flip(x, a), flip(c, b), flip(y, d))
        for a in (0, 1) for b in (0, 1) for d in (0, 1) if a or b or d
    ]
    rows, width = n1.shape[1:]
    group = 8 * rows
    half = rows // 16
    qb = w0.shape[1] // 6
    fb = w3.shape[1] // 2
    units = wg.shape[2]
    d_rows = wq.shape[1]
    own_slot = 2 * z + y
    mine = pl.ds(half * y, half)
    slice_mine = 2 * x + c
    pending = []

    def send(cond, src, dst, ssem, rsem, device):
        def go():
            remote(src, dst, ssem, rsem, device).start()

        def done():
            remote(src, dst, ssem, rsem, device).wait_send()

        if cond is None:
            go()
        else:
            pl.when(cond)(go)
        pending.append((cond, done))

    def keep(src, dst, rsem):
        pltpu.make_async_copy(src, dst, rsem).start()

    def arrived(dst, rsem, cond=None):
        def wait():
            remote(dst, dst, rsem, rsem, sibling).wait_recv()

        if cond is None:
            wait()
        else:
            pl.when(cond)(wait)

    barrier = pltpu.get_barrier_semaphore()
    for d in column:
        pl.semaphore_signal(barrier, inc=1, device_id=d, device_id_type=MESH)
    for xx, cc, yy in face:
        pl.semaphore_signal(barrier, inc=1, device_id=dev(z, xx, cc, yy), device_id_type=MESH)

    def stage(g, parts, cols, total):
        for b in range(ZN):
            n = min(cols, total - b * cols)
            for s in range(2):
                for j, ref in enumerate(parts):
                    at = (s * len(parts) + j) * cols
                    st[g][b, :, at:at + n] = ref[s, :, b * cols:b * cols + n]
                    if n < cols:
                        st[g][b, :, at + n:at + cols] = jnp.zeros((d_rows, cols - n), BF)

    stage(QKV, (wq, wk, wv), qb, wq.shape[2])

    row_at = lax.broadcasted_iota(jnp.int32, (16, width), 0)
    row_set = jnp.zeros((16, width), jnp.int32)
    for p in range(16):
        row_set = jnp.where(row_at == p, position_set[p], row_set)
    for s in range(2):
        set_mask[s] = jnp.where(row_set == s, 1.0, 0.0).astype(BF)

    def gain_full(gain):
        m1 = set_mask[1].astype(F32)
        return jnp.where(m1 > 0.5, gain[1:2, :], gain[0:1, :])

    def tile_rows(v):
        return jnp.broadcast_to(v[None], (half, 16, v.shape[1])).reshape(rows, v.shape[1])

    def normalize(values, gain):
        inverse = lax.rsqrt(jnp.sum(values * values, axis=-1, keepdims=True) / width + EPSILON)
        unit = values * inverse
        return unit, inverse, (unit * tile_rows(gain_full(gain))).astype(BF)

    def own_rows(ref):
        return ref[mine].reshape(rows, width).astype(F32)

    def zero(ref):
        ref[...] = jnp.zeros_like(ref)

    unit, inverse, normed = normalize(own_rows(frames), gain_one)
    u_one[...] = unit
    small[0] = jnp.broadcast_to(inverse, (rows, LANES))
    n1[own_slot] = normed
    pl.when(z == 0)(lambda: zero(ru))
    pl.when(z == ZN - 1)(lambda: zero(rd))

    lane = lax.broadcasted_iota(jnp.int32, (8, LANES), 1)
    table = jnp.zeros((8, LANES), F32)
    for f in range(frames.shape[0]):
        table = table + jnp.where(lane == dialogue[f], padding[f].astype(F32), 0.0)
    cnt[0, z] = table
    pl.semaphore_wait(barrier, len(column) + len(face))

    def spread(g, k):
        send(None, st[g].at[hop(k)], ga[g].at[z], sp_s.at[g, k], sp_r.at[g, z], dev(hop(k), x, c, y))

    def piece_of(g, k, xx, cc):
        piece = hop(k) * 4 + 2 * xx + cc
        return w[g].at[pl.ds(pl.multiple_of(piece * d_rows, d_rows), d_rows), :], mc_r.at[g, piece]

    def multicast(g, k):
        if k:
            arrived(ga[g].at[hop(k)], sp_r.at[g, hop(k)])
        src = ga[g].at[hop(k)] if k else st[g].at[z]
        dst, rsem = piece_of(g, k, x, c)
        send(None, src, dst, mc_s.at[g, k, 0], rsem, across)
        send(None, src, dst, mc_s.at[g, k, 1], rsem, sibling)
        keep(src, dst, rsem)

    def forward(g, k):
        dst, rsem = piece_of(g, k, 1 - x, c)
        arrived(dst, rsem)
        send(None, dst, dst, fw_s.at[g, k], rsem, sibling)

    def weights_here(g):
        for k in range(ZN):
            for cc in (c, 1 - c):
                dst, rsem = piece_of(g, k, x, cc)
                arrived(dst, rsem)
            dst, rsem = piece_of(g, k, 1 - x, 1 - c)
            arrived(dst, rsem)

    cut_rows = rows // CUTS

    def cut(q):
        return pl.ds(q * cut_rows, cut_rows)

    def gather_send(which, buf, slot, q, cond, way, device):
        src = buf.at[slot, cut(q)]
        send(cond, src, src, ag_s.at[which, 3 * slot + way, q], ag_r.at[which, slot, q], device)

    def gather_start(which, buf):
        for q in range(CUTS):
            gather_send(which, buf, own_slot, q, z < ZN - 1, 1, above)
            gather_send(which, buf, own_slot, q, z > 0, 2, below)
            gather_send(which, buf, own_slot, q, None, 0, partner)

    def gather_step(which, buf, k):
        lo = 2 * jnp.maximum(z - k, 0) + y
        hi = 2 * jnp.minimum(z + k, ZN - 1) + y
        up, down = z >= k, z + k <= ZN - 1
        for q in range(CUTS):
            arrived(buf.at[lo, cut(q)], ag_r.at[which, lo, q], cond=up)
            gather_send(which, buf, lo, q, up & (z < ZN - 1), 1, above)
            gather_send(which, buf, lo, q, up, 0, partner)
            arrived(buf.at[hi, cut(q)], ag_r.at[which, hi, q], cond=down)
            gather_send(which, buf, hi, q, down & (z > 0), 2, below)
            gather_send(which, buf, hi, q, down, 0, partner)

    def gather_end(which, buf):
        slot = 2 * z + 1 - y
        for q in range(CUTS):
            arrived(buf.at[slot, cut(q)], ag_r.at[which, slot, q])
        for k in (1, 2, 3):
            lo = 2 * jnp.maximum(z - k, 0) + 1 - y
            hi = 2 * jnp.minimum(z + k, ZN - 1) + 1 - y
            for q in range(CUTS):
                arrived(buf.at[lo, cut(q)], ag_r.at[which, lo, q], cond=z >= k)
                arrived(buf.at[hi, cut(q)], ag_r.at[which, hi, q], cond=z + k <= ZN - 1)

    def far_first(i):
        orders = ((3, 2, 1, 0), (3, 0, 2, 1), (0, 3, 1, 2), (0, 1, 2, 3))
        b = jnp.int32(0)
        for zz, order in enumerate(orders):
            b = b + jnp.where(z == zz, order[i], 0)
        return b

    def scatter_put(n, partial):
        pf[n % 2] = partial.reshape(8, rows, width)

    def scatter_send(n, i):
        b = far_first(i)
        for q in range(CUTS):
            sb[n, b, cut(q), :] = pf[n % 2, 2 * b + 1 - y, cut(q), :].astype(BF)
            send(None, sb.at[n, b, cut(q)], sr.at[n, b, cut(q)], rs_sib_s.at[n, b, q], rs_sib_r.at[n, b, q], partner)

    def scatter_start(n, partial):
        scatter_put(n, partial)
        for i in range(4):
            scatter_send(n, i)

    def chip_sum(n, b, q):
        arrived(sr.at[n, b, cut(q)], rs_sib_r.at[n, b, q])
        return pf[n % 2, 2 * b + y, cut(q), :] + sr[n, b, cut(q), :].astype(F32)

    def scatter_chain(n, between=None):
        plan = (
            (True, 3, z <= 1), (False, 0, z >= 2), (True, 3, z == 2), (False, 0, z == 1),
            (True, 2, z <= 1), (False, 1, z >= 2), (True, 1, z == 0), (False, 2, z == 3),
        )
        for at, (rising, b, cond) in enumerate(plan):
            if rising:
                inflow, buf, r, target = z > 0, ru, rs_ru, above
            else:
                inflow, buf, r, target = z < ZN - 1, rd, rs_rd, below
            for q in range(CUTS):

                def step(b=b, q=q, inflow=inflow, buf=buf, r=r):
                    total = chip_sum(n, b, q)
                    arrived(buf.at[n, b, cut(q)], r.at[n, b, q], cond=inflow)
                    so[n, b, cut(q), :] = (total + buf[n, b, cut(q), :].astype(F32)).astype(BF)

                pl.when(cond)(step)
                send(cond, so.at[n, b, cut(q)], buf.at[n, b, cut(q)], rs_s.at[n, b, q], r.at[n, b, q], target)
            for action in (between or {}).get(at, ()):
                action()

    def scatter_end(n):
        totals = []
        for q in range(CUTS):
            total = chip_sum(n, z, q)
            arrived(ru.at[n, z, cut(q)], rs_ru.at[n, z, q], cond=z > 0)
            arrived(rd.at[n, z, cut(q)], rs_rd.at[n, z, q], cond=z < ZN - 1)
            totals.append(total + ru[n, z, cut(q), :].astype(F32) + rd[n, z, cut(q), :].astype(F32))
        return jnp.concatenate(totals, axis=0)

    def both_sets(v):
        n = v.shape[1]
        three = v.reshape(group // 16, 16, n)
        return jnp.concatenate([(three * set_mask[s, :, 0:n][None]).reshape(group, n) for s in range(2)], axis=1)

    def choose(v):
        n = v.shape[1] // 2
        m = jnp.broadcast_to(set_mask[1, :, 0:n].astype(F32)[None], (group // 16, 16, n)).reshape(group, n)
        return jnp.where(m > 0.5, v[:, n:], v[:, 0:n])

    def flat(buf):
        return buf[...].reshape(group, width)

    for k in (1, 2, 3):
        send(None, cnt.at[0, z], cnt.at[0, z], c_s.at[0, k], c_r.at[0, z], dev(hop(k), x, c, y))
    gather_start(0, n1)
    spread(QKV, 1)
    multicast(QKV, 0)
    stage(OUT, (wo,), qb, wo.shape[2])
    stage(UPS, (wg, wu), fb, units)
    stage(DOWN, (wd,), fb, units)
    for k in (1, 2, 3):
        arrived(cnt.at[0, hop(k)], c_r.at[0, hop(k)])
    cnt[1, slice_mine] = cnt[0, 0] + cnt[0, 1] + cnt[0, 2] + cnt[0, 3]
    for a, b in ((0, 1), (1, 0), (1, 1)):
        send(None, cnt.at[1, slice_mine], cnt.at[1, slice_mine], c_s.at[1, 2 * a + b], c_r.at[1, slice_mine],
             dev(z, flip(x, a), flip(c, b), y))
    gather_step(0, n1, 1)
    spread(QKV, 2)
    forward(QKV, 0)
    gather_step(0, n1, 2)
    spread(QKV, 3)
    for k in (2, 1, 3):
        spread(OUT, k)
    multicast(QKV, 3)
    gather_step(0, n1, 3)
    spread(UPS, 2)
    spread(UPS, 1)
    multicast(QKV, 2)
    forward(QKV, 3)
    multicast(QKV, 1)
    forward(QKV, 2)
    for a, b in ((0, 1), (1, 0), (1, 1)):
        j = 2 * flip(x, a) + flip(c, b)
        arrived(cnt.at[1, j], c_r.at[1, j])
    counts = cnt[1, 0] + cnt[1, 1] + cnt[1, 2] + cnt[1, 3]
    for f in range(frames.shape[0]):
        found = jnp.sum(jnp.where(lane == dialogue[f], counts, 0.0), axis=1, keepdims=True)
        loss = padding[f].astype(F32) * (frames.shape[0] * 1.0) / (found + 1.0)
        small[1, f:f + 1, :] = jnp.broadcast_to(loss[0:1, :], (1, LANES))
    frame_weight = small[1, mine, :]
    weight_rows = jnp.broadcast_to(frame_weight[:, None, 0:1], (half, 16, width)).reshape(rows, width)
    sd[own_slot] = (own_rows(cot) * weight_rows).astype(BF)
    forward(QKV, 1)
    multicast(OUT, 0)
    multicast(UPS, 0)
    gather_end(0, n1)
    weights_here(QKV)
    qkv = choose(dot(flat(n1), w[QKV][...])).astype(BF)
    qs[...] = qkv[:, 0:qb]
    ks[...] = qkv[:, qb:2 * qb]
    vs[...] = qkv[:, 2 * qb:3 * qb]
    for k in (2, 1, 3):
        multicast(OUT, k)
    forward(OUT, 0)

    bl = LANES
    r_at = lax.broadcasted_iota(jnp.int32, (bl, bl), 0)
    c_at = lax.broadcasted_iota(jnp.int32, (bl, bl), 1)
    seen = (c_at <= r_at) & (lax.div(r_at, 16) == lax.div(c_at, 16))
    heads = qb // HDIM
    head_of = lax.div(lax.broadcasted_iota(jnp.int32, (bl, qb), 1), HDIM)
    scale = HDIM ** (-0.5)

    def only(v, h):
        return jnp.where(head_of == h, v, jnp.zeros_like(v))

    attended = []
    for t in range(group // bl):
        at = pl.ds(t * bl, bl)
        q, kk, v = qs[at, :], ks[at, :], vs[at, :]
        out = jnp.zeros((bl, qb), F32)
        for h in range(heads):
            scores = dot(only(q, h), kk, NT) * scale
            scores = jnp.where(seen, scores, -1e30)
            e = jnp.exp(scores - jnp.max(scores, axis=-1, keepdims=True))
            e = jnp.where(seen, e, 0.0)
            p = e / jnp.sum(e, axis=-1, keepdims=True)
            probs[t, h] = p
            out = jnp.where(head_of == h, dot(p.astype(BF), v), out)
        attended.append(out.astype(BF))
    att2[...] = both_sets(jnp.concatenate(attended, axis=0))
    for k in (2, 1, 3):
        forward(OUT, k)
    weights_here(OUT)
    scatter_start(0, dot(att2[...], w[OUT][...], NT))
    multicast(UPS, 2)
    forward(UPS, 0)
    scatter_chain(0, {
        1: (lambda: gather_start(1, sd),),
        5: (lambda: multicast(UPS, 3), lambda: forward(UPS, 2)),
    })
    spread(UPS, 3)
    gather_step(1, sd, 1)
    attention = scatter_end(0)

    hidden = own_rows(frames) + attention
    hid[...] = hidden
    unit, inverse, normed = normalize(hidden, gain_two)
    u_two[...] = unit
    small[2] = jnp.broadcast_to(inverse, (rows, LANES))
    n2[own_slot] = normed
    gather_start(2, n2)
    spread(DOWN, 2)
    multicast(DOWN, 0)
    forward(UPS, 3)
    gather_step(2, n2, 1)
    gather_step(1, sd, 2)
    spread(DOWN, 1)
    multicast(UPS, 1)
    forward(DOWN, 0)
    gather_step(2, n2, 2)
    spread(DOWN, 3)
    forward(UPS, 1)
    gather_step(2, n2, 3)
    gather_step(1, sd, 3)
    for k in (2, 3, 1):
        multicast(DOWN, k)
    gather_end(1, sd)
    gather_end(2, n2)
    weights_here(UPS)

    gu = choose(dot(flat(n2), w[UPS][...]))
    gt[...] = gu[:, 0:fb]
    up[...] = gu[:, fb:2 * fb]
    for k in (2, 3, 1):
        forward(DOWN, k)
    weights_here(DOWN)
    active_grad = choose(dot(flat(sd), w[DOWN][...]))
    gate = gt[...]
    sig = jax.nn.sigmoid(gate)
    silu = gate * sig
    act2[...] = both_sets((silu * up[...]).astype(BF))
    gate_grad = (active_grad * up[...] * sig * (1.0 + gate * (1.0 - sig))).astype(BF)
    up_grad = (active_grad * silu).astype(BF)
    gu2[...] = both_sets(jnp.concatenate([gate_grad, up_grad], axis=1))
    scatter_start(1, dot(gu2[...], w[UPS][...], NT))

    def weight_grad(g, values, grads):
        dw[g][...] = dot(values, grads, TN).astype(BF).reshape(dw[g].shape)
        for xx in (1 - x, x):
            send(None, dw[g].at[:, 2 * xx + 1 - c], rc[g].at[xx], gc_s.at[g, xx], gc_r.at[g, xx], sibling)

    def reduce_across(g):
        arrived(rc[g].at[1 - x], gc_r.at[g, 1 - x])
        for k in (2, 1, 3, 0):
            zz = hop(k)
            sx[g][zz] = (dw[g][zz, 2 * (1 - x) + c].astype(F32) + rc[g][1 - x, zz].astype(F32)).astype(BF)
            send(None, sx[g].at[zz], rx[g].at[zz], gx_s.at[g, zz], gx_r.at[g, zz], across)

    def reduce_column(g, ks):
        for k in ks:
            zz = hop(k)
            if k == 2:
                arrived(rc[g].at[x], gc_r.at[g, x])
            arrived(rx[g].at[zz], gx_r.at[g, zz])
            total = dw[g][zz, 2 * x + c].astype(F32) + rc[g][x, zz].astype(F32) + rx[g][zz].astype(F32)
            if k:
                rx[g][zz] = total.astype(BF)
                send(None, rx[g].at[zz], fi[g].at[z], gf_s.at[g, k], gf_r.at[g, z], dev(zz, x, c, y))
            else:
                fi[g][z] = total.astype(BF)

    def reduce_end(g):
        for k in (1, 2, 3):
            arrived(fi[g].at[hop(k)], gf_r.at[g, hop(k)])

    weight_grad(DOWN, flat(sd), act2[...])
    weight_grad(UPS, flat(n2), gu2[...])
    scatter_chain(1, {1: (lambda: reduce_across(DOWN),), 3: (lambda: reduce_across(UPS),)})
    scatter_put(2, dot(act2[...], w[DOWN][...], NT))
    scatter_send(2, 0)
    scatter_send(2, 1)
    normed_two_grad = scatter_end(1)

    def set_sums(v, at):
        three = v.reshape(half, 16, width)
        for s in range(2):
            part = (three * set_mask[s].astype(F32)[None]).reshape(rows, width)
            gain_col[z, at + s:at + s + 1, :] = jnp.sum(part, axis=0, keepdims=True)

    def norm_back(gradient, gain, unit, inverse):
        scaled = gradient * tile_rows(gain_full(gain))
        return inverse * (scaled - unit * (jnp.sum(scaled * unit, axis=-1, keepdims=True) / width))

    unit = u_two[...]
    seed = own_rows(cot) * weight_rows
    hidden_grad = seed + norm_back(normed_two_grad, gain_two, unit, small[2][:, 0:1])
    hgrad[...] = hidden_grad
    hl[own_slot] = hidden_grad.astype(BF)
    gather_start(3, hl)
    gain_col[z] = jnp.zeros((8, width), F32)
    set_sums(normed_two_grad * unit, 2)
    gather_step(3, hl, 1)
    reduce_column(DOWN, (2,))
    gather_step(3, hl, 2)
    reduce_column(DOWN, (1,))
    gather_step(3, hl, 3)
    reduce_column(DOWN, (3, 0))
    reduce_column(UPS, (2,))
    scatter_send(2, 2)
    scatter_send(2, 3)
    gather_end(3, hl)

    datt = choose(dot(flat(hl), w[OUT][...])).astype(BF)
    gq, gk, gv = [], [], []
    for t in range(group // bl):
        at = pl.ds(t * bl, bl)
        q, kk, v = qs[at, :], ks[at, :], vs[at, :]
        da = datt[t * bl:(t + 1) * bl, :]
        tq = jnp.zeros((bl, qb), F32)
        tk, tv = tq, tq
        for h in range(heads):
            p = probs[t, h]
            dp = dot(only(da, h), v, NT)
            tv = jnp.where(head_of == h, dot(p.astype(BF), da, TN), tv)
            ds = (p * (dp - jnp.sum(dp * p, axis=-1, keepdims=True))).astype(BF)
            tq = jnp.where(head_of == h, dot(ds, kk) * scale, tq)
            tk = jnp.where(head_of == h, dot(ds, q, TN) * scale, tk)
        gq.append(tq.astype(BF))
        gk.append(tk.astype(BF))
        gv.append(tv.astype(BF))
    low_grads = jnp.concatenate([jnp.concatenate(v, axis=0) for v in (gq, gk, gv)], axis=1)
    gqkv2 = both_sets(low_grads)
    scatter_start(3, dot(gqkv2, w[QKV][...], NT))
    weight_grad(QKV, flat(n1), gqkv2)
    weight_grad(OUT, flat(hl), att2[...])
    scatter_chain(3, {1: (lambda: reduce_across(QKV), lambda: reduce_across(OUT))})
    reduce_column(UPS, (1, 3, 0))
    scatter_chain(2)
    normed_one_grad = scatter_end(3)
    unit = u_one[...]
    set_sums(normed_one_grad * unit, 0)
    for k in (1, 2, 3):
        send(None, gain_col.at[z], gain_col.at[z], gcs.at[k], gcr.at[z], dev(hop(k), x, c, y))
    result = hgrad[...] + norm_back(normed_one_grad, gain_one, unit, small[0][:, 0:1])
    halves[1, mine] = result.astype(BF).reshape(half, 16, width)
    send(None, halves.at[1, mine], halves.at[1, mine], y_s.at[1], y_r.at[1], partner)
    reduce_column(QKV, (2, 1, 3, 0))
    reduce_column(OUT, (2, 1, 3, 0))
    branch = scatter_end(2)
    halves[0, mine] = (hid[...] + branch).astype(BF).reshape(half, 16, width)
    send(None, halves.at[0, mine], halves.at[0, mine], y_s.at[0], y_r.at[0], partner)

    for k in (1, 2, 3):
        arrived(gain_col.at[hop(k)], gcr.at[hop(k)])
    place = 4 * x + 2 * c + y
    gain_face[place] = gain_col[0] + gain_col[1] + gain_col[2] + gain_col[3]
    for k, (xx, cc, yy) in enumerate(face):
        send(None, gain_face.at[place], gain_face.at[place], gfs.at[k], gfr.at[place], dev(z, xx, cc, yy))
    for g in (DOWN, UPS, QKV, OUT):
        reduce_end(g)
    for j in (0, 1):
        theirs = pl.ds(half * (1 - y), half)
        arrived(halves.at[j, theirs], y_r.at[j])
    total = gain_face[place]
    for xx, cc, yy in face:
        j = 4 * xx + 2 * cc + yy
        arrived(gain_face.at[j], gfr.at[j])
    total = gain_face[0]
    for j in range(1, 8):
        total = total + gain_face[j]
    gains_out[...] = total

    for cond, done in pending:
        if cond is None:
            done()
        else:
            pl.when(cond)(done)


def output_kernel(
    fi0, fi1, fi2, fi3, halves, gains,
    mixed, frames_grad, dq, dk, dv, do, dg, du, dd, first_gain, second_gain,
):
    inner = lax.rem(lax.axis_index("dp"), INNER)
    mixed[...] = halves[0]
    frames_grad[...] = halves[1]
    for fi, outs in ((fi0, (dq, dk, dv)), (fi1, (do,)), (fi2, (dg, du)), (fi3, (dd,))):
        cols = fi.shape[2] // (2 * len(outs))
        for b in range(ZN):
            n = min(cols, outs[0].shape[2] - b * cols)
            for s in range(2):
                for j, out in enumerate(outs):
                    at = (s * len(outs) + j) * cols
                    out[s, :, b * cols:b * cols + n] = fi[b, :, at:at + n].astype(F32)
    width = gains.shape[1]
    share = first_gain.shape[1]
    turned = pltpu.roll(gains[...], lax.rem(width - inner * share, width), 1)
    first_gain[...] = turned[0:2, 0:share]
    second_gain[...] = turned[2:4, 0:share]


def run_layer(frames, cot, dialogue, padding, position_set, gain_one, gain_two, weights):
    wq, wk, wv, wo, wg, wu, wd = weights
    width = frames.shape[2]
    rows = frames.shape[0] * frames.shape[1] // 2
    d_rows = wq.shape[1]
    qb = wq.shape[2] // ZN
    units = wg.shape[2]
    fb = -(-units // (ZN * LANES)) * LANES
    group = 8 * rows
    dma = pltpu.SemaphoreType.DMA
    vm = pltpu.VMEM
    shape = jax.ShapeDtypeStruct
    cols = (6 * qb, 2 * qb, 4 * fb, 2 * fb)
    blocks = [(ZN, d_rows, n) for n in cols]
    block_rows = (8, rows, width)
    four = (4, 4, rows, width)
    scratch = (
        [vm(b, BF) for b in blocks] * 2
        + [vm((width, n), BF) for n in cols]
        + [vm((ZN, 4, d_rows, n), BF) for n in cols]
        + [vm((2, ZN, d_rows, n), BF) for n in cols]
        + [vm((ZN, d_rows, n), BF) for n in cols] * 2
        + [vm((2, 16, width), BF)]
        + [vm(block_rows, BF)] * 4 + [vm((2,) + block_rows, F32)]
        + [vm(four, BF)] * 5
        + [vm((group, qb), BF)] * 3
        + [vm((group, 2 * qb), BF), vm((group // LANES, qb // HDIM, LANES, LANES), F32)]
        + [vm((group, 2 * fb), BF), vm((group, 4 * fb), BF), vm((group, fb), F32), vm((group, fb), F32)]
        + [vm((2, 4, 8, LANES), F32), vm((ZN, 8, width), F32), vm((8, 8, width), F32)]
        + [vm((rows, width), F32)] * 4 + [vm((3, rows, LANES), F32)]
        + [dma((4, 4)), dma((4, 4)), dma((4, 4, 2)), dma((4, INNER)), dma((4, 4)), dma((4, 24, CUTS)), dma((4, 8, CUTS))]
        + [dma((4, 4, CUTS))] * 5
        + [dma((4, 2)), dma((4, 2)), dma((4, 4)), dma((4, 4)), dma((4, 4)), dma((4, 4))]
        + [dma((2, 4)), dma((2, 4)), dma((2,)), dma((2,)), dma((4,)), dma((4,)), dma((8,)), dma((8,))]
    )
    spec = pl.BlockSpec(memory_space=pltpu.VMEM)
    scalars = pl.BlockSpec(memory_space=pltpu.SMEM)
    packed = pl.pallas_call(
        layer_kernel,
        out_shape=[shape(b, BF) for b in blocks] + [shape((2,) + frames.shape, BF), shape((8, width), F32)],
        in_specs=[spec] * 2 + [scalars] * 3 + [spec] * 9,
        out_specs=[spec] * 6,
        scratch_shapes=scratch,
        compiler_params=pltpu.CompilerParams(
            collective_id=0, has_side_effects=True, vmem_limit_bytes=63 * 2**20
        ),
        cost_estimate=pl.CostEstimate(flops=10**10, bytes_accessed=10**7, transcendentals=0),
        name="layer",
    )(frames, cot, dialogue, padding, position_set, gain_one, gain_two, *weights)
    grads = [shape(v.shape, F32) for v in weights]
    return pl.pallas_call(
        output_kernel,
        out_shape=[shape(frames.shape, BF)] * 2 + grads + [shape((2, d_rows), F32)] * 2,
        in_specs=[spec] * 6,
        out_specs=[spec] * 11,
        compiler_params=pltpu.CompilerParams(vmem_limit_bytes=63 * 2**20),
        cost_estimate=pl.CostEstimate(flops=10**6, bytes_accessed=10**7, transcendentals=0),
        name="outputs",
    )(*packed)


def per_device(
    frames, cotangent, dialogue, padding, position_set,
    query_weight, key_weight, value_weight, output_weight, gate_weight, up_weight, down_weight,
    attention_gain, feedforward_gain,
):
    dp = lax.axis_size("dp")
    outer = dp // INNER
    groups = [[o * INNER + i for o in range(outer)] for i in range(INNER)]
    width = frames.shape[-1]
    turn = (False, False, False, True, False, False, True)
    weights = [query_weight, key_weight, value_weight, output_weight, gate_weight, up_weight, down_weight]
    weights = [jnp.swapaxes(v, 1, 2) if t else v for v, t in zip(weights, turn)]

    def to_kernel(v):
        if outer == 1:
            return v
        cut = v.reshape(v.shape[:-1] + (outer, INNER, width // dp))
        return jnp.swapaxes(cut, -3, -2).reshape(v.shape)

    def from_kernel(v):
        if outer == 1:
            return v
        cut = v.reshape(v.shape[:-1] + (INNER, outer, width // dp))
        return jnp.swapaxes(cut, -3, -2).reshape(v.shape)

    if outer > 1:
        weights = [lax.all_gather(v, "dp", axis=1, tiled=True, axis_index_groups=groups) for v in weights]
    mixed, frames_grad, *rest = run_layer(
        to_kernel(frames), to_kernel(cotangent), dialogue, padding, position_set,
        to_kernel(attention_gain), to_kernel(feedforward_gain), weights,
    )
    grads, gains = rest[:7], rest[7:]
    if outer > 1:
        grads = [
            lax.psum_scatter(v, "dp", scatter_dimension=1, tiled=True, axis_index_groups=groups) for v in grads
        ]
        gains = [
            lax.psum_scatter(v, "dp", scatter_dimension=1, tiled=True, axis_index_groups=groups) for v in gains
        ]
    grads = [jnp.swapaxes(v, 1, 2) if t else v for v, t in zip(grads, turn)]
    return (from_kernel(mixed), from_kernel(frames_grad), *grads, *gains)


def solution(mesh):
    column = P(None, "dp", "tensor")
    row = P(None, "tensor", "dp")
    rows = P("dp", None, None)
    in_specs = (
        rows, rows, P("dp"), P("dp"), P(),
        column, column, column, row, column, column, row, P(), P(),
    )
    out_specs = (
        rows, rows, column, column, column, row, column, column, row, P(None, "dp"), P(None, "dp"),
    )
    return jax.shard_map(per_device, mesh=mesh, in_specs=in_specs, out_specs=out_specs, check_vma=False)
```

```python
import jax
import jax.numpy as jnp
from jax import lax
from jax.experimental import pallas as pl
from jax.experimental.pallas import tpu as pltpu
from jax.sharding import PartitionSpec as P

HDIM = 64
EPSILON = 1e-05
INNER = 16
ZN = 4
LANES = 128
CUTS = 2
MESH = pl.DeviceIdType.MESH
BF = jnp.bfloat16
F32 = jnp.float32
NN = (((1,), (0,)), ((), ()))
NT = (((1,), (1,)), ((), ()))
TN = (((0,), (0,)), ((), ()))
QKV, OUT, UPS, DOWN = range(4)
BLOCKS = (2, 2, 4, 4)


def dot(a, b, dims=NN):
    return lax.dot_general(a, b, dims, preferred_element_type=F32)


def layer_kernel(
    frames, cot, dialogue, padding, position_set, gain_one, gain_two,
    wq, wk, wv, wo, wg, wu, wd,
    fi0, fi1, fi2, fi3, halves, gains_out,
    st0, st1, st2, st3, ga0, ga1, ga2, ga3, w0, w1, w2, w3,
    dw0, dw1, dw2, dw3, rc0, rc1, rc2, rc3, sx0, sx1, sx2, sx3, rx0, rx1, rx2, rx3,
    set_mask, n1, sd, n2, hl, pf,
    sb, sr, so, ru, rd,
    qs, ks, vs, att2, probs, gqkv2, act2, gu2, gt, up,
    cnt, gain_col, gain_face,
    u_one, u_two, hid, hgrad, small,
    sp_s, sp_r, mc_s, mc_r, fw_s, ag_s, ag_r, rs_sib_s, rs_sib_r, rs_s, rs_ru, rs_rd,
    gc_s, gc_r, gx_s, gx_r, gf_s, gf_r, c_s, c_r, y_s, y_r, gcs, gcr, gfs, gfr,
):
    st, ga, w = (st0, st1, st2, st3), (ga0, ga1, ga2, ga3), (w0, w1, w2, w3)
    dw, fi = (dw0, dw1, dw2, dw3), (fi0, fi1, fi2, fi3)
    rc, sx, rx = (rc0, rc1, rc2, rc3), (sx0, sx1, sx2, sx3), (rx0, rx1, rx2, rx3)
    idx = lax.axis_index("dp")
    y = lax.axis_index("tensor")
    inner = lax.rem(idx, INNER)
    base = idx - inner
    z = lax.div(inner, 4)
    x = lax.rem(lax.div(inner, 2), 2)
    c = lax.rem(inner, 2)

    def dev(zz, xx, cc, yy):
        return (base + zz * 4 + xx * 2 + cc, yy)

    def flip(v, bit):
        return 1 - v if bit else v

    def hop(k):
        return lax.rem(z + k, ZN)

    def remote(src, dst, ssem, rsem, device):
        return pltpu.make_async_remote_copy(
            src_ref=src, dst_ref=dst, send_sem=ssem, recv_sem=rsem,
            device_id=device, device_id_type=MESH,
        )

    low = lax.rem(z, 2)
    partner = dev(z, x, c, 1 - y)
    beside = dev(z + 1 - 2 * low, x, c, y)
    sibling = dev(z, x, 1 - c, y)
    across = dev(z, 1 - x, c, y)
    above = dev(hop(1), x, c, y)
    below = dev(hop(ZN - 1), x, c, y)
    column = [dev(hop(k), x, c, y) for k in (1, 2, 3)]
    face = [
        (flip(x, a), flip(c, b), flip(y, d))
        for a in (0, 1) for b in (0, 1) for d in (0, 1) if a or b or d
    ]
    rows, width = n1.shape[1:]
    half = rows // 16
    qb = w0.shape[1] // 6
    fb = w3.shape[1] // 2
    units = wg.shape[2]
    d_rows = wq.shape[1]
    own_slot = 2 * z + y
    pair_slot = 2 * low + y
    mine = pl.ds(half * y, half)
    slice_mine = 2 * x + c
    pending = []

    def send(cond, src, dst, ssem, rsem, device):
        def go():
            remote(src, dst, ssem, rsem, device).start()

        def done():
            remote(src, dst, ssem, rsem, device).wait_send()

        if cond is None:
            go()
        else:
            pl.when(cond)(go)
        pending.append((cond, done))

    def arrived(dst, rsem, cond=None):
        def wait():
            remote(dst, dst, rsem, rsem, sibling).wait_recv()

        if cond is None:
            wait()
        else:
            pl.when(cond)(wait)

    barrier = pltpu.get_barrier_semaphore()
    for d in column:
        pl.semaphore_signal(barrier, inc=1, device_id=d, device_id_type=MESH)
    for xx, cc, yy in face:
        pl.semaphore_signal(barrier, inc=1, device_id=dev(z, xx, cc, yy), device_id_type=MESH)

    def stage(g, parts, cols, total):
        for b in range(BLOCKS[g]):
            n = min(cols, total - b * cols)
            for s in range(2):
                for j, ref in enumerate(parts):
                    at = (s * len(parts) + j) * cols
                    st[g][b, :, at:at + n] = ref[s, :, b * cols:b * cols + n]
                    if n < cols:
                        st[g][b, :, at + n:at + cols] = jnp.zeros((d_rows, cols - n), BF)

    stage(QKV, (wq, wk, wv), qb, wq.shape[2])

    row_at = lax.broadcasted_iota(jnp.int32, (16, width), 0)
    row_set = jnp.zeros((16, width), jnp.int32)
    for p in range(16):
        row_set = jnp.where(row_at == p, position_set[p], row_set)
    for s in range(2):
        set_mask[s] = jnp.where(row_set == s, 1.0, 0.0).astype(BF)

    def gain_full(gain):
        m1 = set_mask[1].astype(F32)
        return jnp.where(m1 > 0.5, gain[1:2, :], gain[0:1, :])

    def tile_rows(v):
        return jnp.broadcast_to(v[None], (half, 16, v.shape[1])).reshape(rows, v.shape[1])

    def normalize(values, gain):
        inverse = lax.rsqrt(jnp.sum(values * values, axis=-1, keepdims=True) / width + EPSILON)
        unit = values * inverse
        return unit, inverse, (unit * tile_rows(gain_full(gain))).astype(BF)

    def own_rows(ref):
        return ref[mine].reshape(rows, width).astype(F32)

    def zero(ref):
        for n in (1, 2):
            ref[n] = jnp.zeros(ref.shape[1:], ref.dtype)

    unit, inverse, normed = normalize(own_rows(frames), gain_one)
    u_one[...] = unit
    small[0] = jnp.broadcast_to(inverse, (rows, LANES))
    n1[pair_slot] = normed
    pl.when(z == 0)(lambda: zero(ru))
    pl.when(z == ZN - 1)(lambda: zero(rd))

    lane = lax.broadcasted_iota(jnp.int32, (8, LANES), 1)
    table = jnp.zeros((8, LANES), F32)
    for f in range(frames.shape[0]):
        table = table + jnp.where(lane == dialogue[f], padding[f].astype(F32), 0.0)
    cnt[0, z] = table
    pl.semaphore_wait(barrier, len(column) + len(face))

    def spread(g, k):
        send(None, st[g].at[lax.rem(hop(k), BLOCKS[g])], ga[g].at[z], sp_s.at[g, k], sp_r.at[g, z], dev(hop(k), x, c, y))

    def piece_of(g, k, xx, cc):
        piece = hop(k) * 4 + 2 * xx + cc
        return w[g].at[pl.ds(pl.multiple_of(piece * d_rows, d_rows), d_rows), :], mc_r.at[g, piece]

    def multicast(g, k):
        if k:
            arrived(ga[g].at[hop(k)], sp_r.at[g, hop(k)])
        src = ga[g].at[hop(k)] if k else st[g].at[lax.rem(z, BLOCKS[g])]
        dst, rsem = piece_of(g, k, x, c)
        send(None, src, dst, mc_s.at[g, k, 0], rsem, across)
        send(None, src, dst, mc_s.at[g, k, 1], rsem, sibling)
        dst[...] = src[...]

    def forward(g, k):
        dst, rsem = piece_of(g, k, 1 - x, c)
        arrived(dst, rsem)
        send(None, dst, dst, fw_s.at[g, k], rsem, sibling)

    def weights_here(g):
        for k in range(ZN):
            dst, rsem = piece_of(g, k, x, 1 - c)
            arrived(dst, rsem)
            dst, rsem = piece_of(g, k, 1 - x, 1 - c)
            arrived(dst, rsem)

    cut_rows = rows // CUTS

    def cut(q):
        return pl.ds(q * cut_rows, cut_rows)

    def gather_send(which, buf, slot, q, cond, way, device):
        src = buf.at[slot, cut(q)]
        send(cond, src, src, ag_s.at[which, 3 * slot + way, q], ag_r.at[which, slot, q], device)

    def gather_start(which, buf):
        for q in range(CUTS):
            gather_send(which, buf, own_slot, q, z < ZN - 1, 1, above)
            gather_send(which, buf, own_slot, q, z > 0, 2, below)
            gather_send(which, buf, own_slot, q, None, 0, partner)

    def gather_step(which, buf, k):
        lo = 2 * jnp.maximum(z - k, 0) + y
        hi = 2 * jnp.minimum(z + k, ZN - 1) + y
        up, down = z >= k, z + k <= ZN - 1
        for q in range(CUTS):
            arrived(buf.at[lo, cut(q)], ag_r.at[which, lo, q], cond=up)
            gather_send(which, buf, lo, q, up & (z < ZN - 1), 1, above)
            gather_send(which, buf, lo, q, up, 0, partner)
            arrived(buf.at[hi, cut(q)], ag_r.at[which, hi, q], cond=down)
            gather_send(which, buf, hi, q, down & (z > 0), 2, below)
            gather_send(which, buf, hi, q, down, 0, partner)

    def gather_end(which, buf):
        slot = 2 * z + 1 - y
        for q in range(CUTS):
            arrived(buf.at[slot, cut(q)], ag_r.at[which, slot, q])
        for k in (1, 2, 3):
            lo = 2 * jnp.maximum(z - k, 0) + 1 - y
            hi = 2 * jnp.minimum(z + k, ZN - 1) + 1 - y
            for q in range(CUTS):
                arrived(buf.at[lo, cut(q)], ag_r.at[which, lo, q], cond=z >= k)
                arrived(buf.at[hi, cut(q)], ag_r.at[which, hi, q], cond=z + k <= ZN - 1)

    def pair_start(which, buf):
        for q in range(CUTS):
            gather_send(which, buf, pair_slot, q, None, 1, beside)
            gather_send(which, buf, pair_slot, q, None, 0, partner)

    def pair_step(which, buf):
        slot = 2 * (1 - low) + y
        for q in range(CUTS):
            arrived(buf.at[slot, cut(q)], ag_r.at[which, slot, q])
            gather_send(which, buf, slot, q, None, 0, partner)

    def pair_end(which, buf):
        slot, far = 2 * low + 1 - y, 2 * (1 - low) + 1 - y
        for q in range(CUTS):
            arrived(buf.at[slot, cut(q)], ag_r.at[which, slot, q])
            arrived(buf.at[far, cut(q)], ag_r.at[which, far, q])

    def far_first(i):
        orders = ((3, 2, 1, 0), (3, 0, 2, 1), (0, 3, 1, 2), (0, 1, 2, 3))
        b = jnp.int32(0)
        for zz, order in enumerate(orders):
            b = b + jnp.where(z == zz, order[i], 0)
        return b

    def scatter_put(n, partial):
        blocks = partial.shape[0] // rows
        pf[n % 2, 0:blocks] = partial.reshape(blocks, rows, width)

    def scatter_send(n, i, b=None):
        b = far_first(i) if b is None else b
        for q in range(CUTS):
            sb[n, b, cut(q), :] = pf[n % 2, 2 * b + 1 - y, cut(q), :].astype(BF)
            send(None, sb.at[n, b, cut(q)], sr.at[n, b, cut(q)], rs_sib_s.at[n, b, q], rs_sib_r.at[n, b, q], partner)

    def chip_sum(n, b, q):
        arrived(sr.at[n, b, cut(q)], rs_sib_r.at[n, b, q])
        return pf[n % 2, 2 * b + y, cut(q), :] + sr[n, b, cut(q), :].astype(F32)

    plan = (
        (True, 3, z <= 1), (False, 0, z >= 2), (True, 3, z == 2), (False, 0, z == 1),
        (True, 2, z <= 1), (False, 1, z >= 2), (True, 1, z == 0), (False, 2, z == 3),
    )

    def scatter_step(n, at):
        rising, b, cond = plan[at]
        if rising:
            inflow, buf, r, target = z > 0, ru, rs_ru, above
        else:
            inflow, buf, r, target = z < ZN - 1, rd, rs_rd, below
        for q in range(CUTS):

            def step(q=q):
                total = chip_sum(n, b, q)
                arrived(buf.at[n, b, cut(q)], r.at[n, b, q], cond=inflow)
                so[n, b, cut(q), :] = (total + buf[n, b, cut(q), :].astype(F32)).astype(BF)

            pl.when(cond)(step)
            send(cond, so.at[n, b, cut(q)], buf.at[n, b, cut(q)], rs_s.at[n, b, q], r.at[n, b, q], target)

    def scatter_end(n):
        totals = []
        for q in range(CUTS):
            total = chip_sum(n, z, q)
            arrived(ru.at[n, z, cut(q)], rs_ru.at[n, z, q], cond=z > 0)
            arrived(rd.at[n, z, cut(q)], rs_rd.at[n, z, q], cond=z < ZN - 1)
            totals.append(total + ru[n, z, cut(q), :].astype(F32) + rd[n, z, cut(q), :].astype(F32))
        return jnp.concatenate(totals, axis=0)

    def pair_scatter_send(n):
        scatter_send(n, 2, 1 - low)
        scatter_send(n, 3, low)

    def pair_scatter_step(n):
        b = 1 - low
        for q in range(CUTS):
            so[n, b, cut(q), :] = chip_sum(n, b, q).astype(BF)
            send(None, so.at[n, b, cut(q)], ru.at[n, b, cut(q)], rs_s.at[n, b, q], rs_ru.at[n, b, q], beside)

    def pair_scatter_end(n):
        totals = []
        for q in range(CUTS):
            total = chip_sum(n, low, q)
            arrived(ru.at[n, low, cut(q)], rs_ru.at[n, low, q])
            totals.append(total + ru[n, low, cut(q), :].astype(F32))
        return jnp.concatenate(totals, axis=0)

    def both_sets(v):
        count, n = v.shape
        three = v.reshape(count // 16, 16, n)
        return jnp.concatenate([(three * set_mask[s, :, 0:n][None]).reshape(count, n) for s in range(2)], axis=1)

    def choose(v):
        count, n = v.shape[0], v.shape[1] // 2
        m = jnp.broadcast_to(set_mask[1, :, 0:n].astype(F32)[None], (count // 16, 16, n)).reshape(count, n)
        return jnp.where(m > 0.5, v[:, n:], v[:, 0:n])

    def flat(buf):
        return buf[...].reshape(buf.shape[0] * rows, width)

    def weight_grad(g, values, grads):
        dw[g][...] = dot(values, grads, TN).astype(BF).reshape(dw[g].shape)
        for xx in (1 - x, x):
            send(None, dw[g].at[:, 2 * xx + 1 - c], rc[g].at[xx], gc_s.at[g, xx], gc_r.at[g, xx], sibling)

    def reduce_across(g):
        arrived(rc[g].at[1 - x], gc_r.at[g, 1 - x])
        for k in (2, 1, 3, 0):
            zz = hop(k)
            sx[g][zz] = (dw[g][zz, 2 * (1 - x) + c].astype(F32) + rc[g][1 - x, zz].astype(F32)).astype(BF)
            send(None, sx[g].at[zz], rx[g].at[zz], gx_s.at[g, zz], gx_r.at[g, zz], across)

    def reduce_column(g, k):
        zz = hop(k)
        if k == 2:
            arrived(rc[g].at[x], gc_r.at[g, x])
        arrived(rx[g].at[zz], gx_r.at[g, zz])
        total = dw[g][zz, 2 * x + c].astype(F32) + rc[g][x, zz].astype(F32) + rx[g][zz].astype(F32)
        if k:
            rx[g][zz] = total.astype(BF)
            send(None, rx[g].at[zz], fi[g].at[z], gf_s.at[g, k], gf_r.at[g, z], dev(zz, x, c, y))
        else:
            fi[g][z] = total.astype(BF)

    def reduce_end(g):
        for k in (1, 2, 3):
            arrived(fi[g].at[hop(k)], gf_r.at[g, hop(k)])

    def counts_start():
        for k in (1, 2, 3):
            send(None, cnt.at[0, z], cnt.at[0, z], c_s.at[0, k], c_r.at[0, z], dev(hop(k), x, c, y))

    def counts_step():
        for k in (1, 2, 3):
            arrived(cnt.at[0, hop(k)], c_r.at[0, hop(k)])
        cnt[1, slice_mine] = cnt[0, 0] + cnt[0, 1] + cnt[0, 2] + cnt[0, 3]
        for a, b in ((0, 1), (1, 0), (1, 1)):
            send(None, cnt.at[1, slice_mine], cnt.at[1, slice_mine], c_s.at[1, 2 * a + b], c_r.at[1, slice_mine],
                 dev(z, flip(x, a), flip(c, b), y))

    def seed_rows():
        frame_weight = small[1, mine, :]
        weight_rows = jnp.broadcast_to(frame_weight[:, None, 0:1], (half, 16, width)).reshape(rows, width)
        return own_rows(cot) * weight_rows

    def seed_here():
        for a, b in ((0, 1), (1, 0), (1, 1)):
            j = 2 * flip(x, a) + flip(c, b)
            arrived(cnt.at[1, j], c_r.at[1, j])
        counts = cnt[1, 0] + cnt[1, 1] + cnt[1, 2] + cnt[1, 3]
        for f in range(frames.shape[0]):
            found = jnp.sum(jnp.where(lane == dialogue[f], counts, 0.0), axis=1, keepdims=True)
            loss = padding[f].astype(F32) * (frames.shape[0] * 1.0) / (found + 1.0)
            small[1, f:f + 1, :] = jnp.broadcast_to(loss[0:1, :], (1, LANES))
        sd[own_slot] = seed_rows().astype(BF)

    def stage_rest():
        stage(OUT, (wo,), qb, wo.shape[2])
        stage(UPS, (wg, wu), fb, units)
        stage(DOWN, (wd,), fb, units)

    bl = LANES
    r_at = lax.broadcasted_iota(jnp.int32, (bl, bl), 0)
    c_at = lax.broadcasted_iota(jnp.int32, (bl, bl), 1)
    seen = (c_at <= r_at) & (lax.div(r_at, 16) == lax.div(c_at, 16))
    heads = qb // HDIM
    head_of = lax.div(lax.broadcasted_iota(jnp.int32, (bl, qb), 1), HDIM)
    scale = HDIM ** (-0.5)

    def only(v, h):
        return jnp.where(head_of == h, v, jnp.zeros_like(v))

    def project_heads():
        qkv = choose(dot(flat(n1), w[QKV][...])).astype(BF)
        qs[...] = qkv[:, 0:qb]
        ks[...] = qkv[:, qb:2 * qb]
        vs[...] = qkv[:, 2 * qb:3 * qb]

    def attend():
        attended = []
        for t in range(qs.shape[0] // bl):
            at = pl.ds(t * bl, bl)
            q, kk, v = qs[at, :], ks[at, :], vs[at, :]
            out = jnp.zeros((bl, qb), F32)
            for h in range(heads):
                scores = dot(only(q, h), kk, NT) * scale
                scores = jnp.where(seen, scores, -1e30)
                e = jnp.exp(scores - jnp.max(scores, axis=-1, keepdims=True))
                e = jnp.where(seen, e, 0.0)
                p = e / jnp.sum(e, axis=-1, keepdims=True)
                probs[t, h] = p
                out = jnp.where(head_of == h, dot(p.astype(BF), v), out)
            attended.append(out.astype(BF))
        att2[...] = both_sets(jnp.concatenate(attended, axis=0))

    def attend_back():
        datt = choose(dot(flat(hl), w[OUT][...])).astype(BF)
        gq, gk, gv = [], [], []
        for t in range(qs.shape[0] // bl):
            at = pl.ds(t * bl, bl)
            q, kk, v = qs[at, :], ks[at, :], vs[at, :]
            da = datt[t * bl:(t + 1) * bl, :]
            tq = jnp.zeros((bl, qb), F32)
            tk, tv = tq, tq
            for h in range(heads):
                p = probs[t, h]
                dp = dot(only(da, h), v, NT)
                tv = jnp.where(head_of == h, dot(p.astype(BF), da, TN), tv)
                ds = (p * (dp - jnp.sum(dp * p, axis=-1, keepdims=True))).astype(BF)
                tq = jnp.where(head_of == h, dot(ds, kk) * scale, tq)
                tk = jnp.where(head_of == h, dot(ds, q, TN) * scale, tk)
            gq.append(tq.astype(BF))
            gk.append(tk.astype(BF))
            gv.append(tv.astype(BF))
        low_grads = jnp.concatenate([jnp.concatenate(v, axis=0) for v in (gq, gk, gv)], axis=1)
        gqkv2[...] = both_sets(low_grads)

    def gate_up():
        gu = choose(dot(flat(n2), w[UPS][...]))
        gt[...] = gu[:, 0:fb]
        up[...] = gu[:, fb:2 * fb]

    def gate_up_back():
        active_grad = choose(dot(flat(sd), w[DOWN][...]))
        gate = gt[...]
        sig = jax.nn.sigmoid(gate)
        silu = gate * sig
        act2[...] = both_sets((silu * up[...]).astype(BF))
        gate_grad = (active_grad * up[...] * sig * (1.0 + gate * (1.0 - sig))).astype(BF)
        up_grad = (active_grad * silu).astype(BF)
        gu2[...] = both_sets(jnp.concatenate([gate_grad, up_grad], axis=1))

    def set_sums(v, at):
        three = v.reshape(half, 16, width)
        for s in range(2):
            part = (three * set_mask[s].astype(F32)[None]).reshape(rows, width)
            gain_col[z, at + s:at + s + 1, :] = jnp.sum(part, axis=0, keepdims=True)

    def norm_back(gradient, gain, unit, inverse):
        scaled = gradient * tile_rows(gain_full(gain))
        return inverse * (scaled - unit * (jnp.sum(scaled * unit, axis=-1, keepdims=True) / width))

    def second_norm(attention):
        hidden = own_rows(frames) + attention
        hid[...] = hidden
        unit, inverse, normed = normalize(hidden, gain_two)
        u_two[...] = unit
        small[2] = jnp.broadcast_to(inverse, (rows, LANES))
        n2[own_slot] = normed

    def second_norm_back(normed_two_grad):
        unit = u_two[...]
        hidden_grad = seed_rows() + norm_back(normed_two_grad, gain_two, unit, small[2][:, 0:1])
        hgrad[...] = hidden_grad
        hl[pair_slot] = hidden_grad.astype(BF)
        gain_col[z] = jnp.zeros((8, width), F32)
        set_sums(normed_two_grad * unit, 2)

    def first_norm_back(normed_one_grad):
        unit = u_one[...]
        set_sums(normed_one_grad * unit, 0)
        result = hgrad[...] + norm_back(normed_one_grad, gain_one, unit, small[0][:, 0:1])
        halves[1, mine] = result.astype(BF).reshape(half, 16, width)

    def output_rows(branch):
        halves[0, mine] = (hid[...] + branch).astype(BF).reshape(half, 16, width)

    def half_send(j):
        send(None, halves.at[j, mine], halves.at[j, mine], y_s.at[j], y_r.at[j], partner)

    def half_end(j):
        theirs = pl.ds(half * (1 - y), half)
        arrived(halves.at[j, theirs], y_r.at[j])

    place = 4 * x + 2 * c + y

    def gains_start():
        for k in (1, 2, 3):
            send(None, gain_col.at[z], gain_col.at[z], gcs.at[k], gcr.at[z], dev(hop(k), x, c, y))

    def gains_step():
        for k in (1, 2, 3):
            arrived(gain_col.at[hop(k)], gcr.at[hop(k)])
        gain_face[place] = gain_col[0] + gain_col[1] + gain_col[2] + gain_col[3]
        for k, (xx, cc, yy) in enumerate(face):
            send(None, gain_face.at[place], gain_face.at[place], gfs.at[k], gfr.at[place], dev(z, xx, cc, yy))

    def gains_end():
        for xx, cc, yy in face:
            j = 4 * xx + 2 * cc + yy
            arrived(gain_face.at[j], gfr.at[j])
        total = gain_face[0]
        for j in range(1, 8):
            total = total + gain_face[j]
        gains_out[...] = total

    counts_start()
    spread(QKV, 3)
    spread(QKV, 1)
    stage_rest()
    multicast(QKV, 0)
    multicast(QKV, 1)
    spread(QKV, 2)
    multicast(QKV, 3)
    spread(OUT, 2)
    multicast(DOWN, 0)
    pair_start(0, n1)
    spread(OUT, 1)
    spread(OUT, 3)
    spread(DOWN, 1)
    spread(DOWN, 3)
    counts_step()
    multicast(OUT, 0)
    multicast(OUT, 1)
    multicast(OUT, 2)
    spread(DOWN, 2)
    seed_here()
    gather_start(1, sd)
    forward(QKV, 0)
    multicast(QKV, 2)
    pair_step(0, n1)
    spread(UPS, 1)
    forward(QKV, 1)
    spread(UPS, 3)
    forward(OUT, 2)
    forward(OUT, 1)
    multicast(OUT, 3)
    forward(QKV, 2)
    forward(OUT, 0)
    forward(QKV, 3)
    multicast(UPS, 0)
    forward(OUT, 3)
    multicast(DOWN, 2)
    weights_here(QKV)
    pair_end(0, n1)
    spread(UPS, 2)
    multicast(DOWN, 3)
    multicast(DOWN, 1)
    project_heads()
    weights_here(OUT)
    attend()
    scatter_put(0, dot(att2[...], w[OUT][...], NT))
    pair_scatter_send(0)
    gather_step(1, sd, 1)
    pair_scatter_step(0)
    multicast(UPS, 1)
    forward(UPS, 0)
    attention = pair_scatter_end(0)
    forward(DOWN, 2)
    multicast(UPS, 3)
    second_norm(attention)
    gather_start(2, n2)
    gather_step(1, sd, 2)
    gather_step(2, n2, 1)
    forward(UPS, 1)
    multicast(UPS, 2)
    forward(DOWN, 1)
    forward(DOWN, 3)
    gather_step(1, sd, 3)
    gather_step(2, n2, 2)
    forward(DOWN, 0)
    forward(UPS, 3)
    gather_step(2, n2, 3)
    forward(UPS, 2)
    weights_here(UPS)
    weights_here(DOWN)
    gather_end(1, sd)
    gather_end(2, n2)
    gate_up()
    gate_up_back()
    scatter_put(1, dot(gu2[...], w[UPS][...], NT))
    scatter_send(1, 0)
    weight_grad(DOWN, flat(sd), act2[...])
    scatter_send(1, 2)
    scatter_send(1, 1)
    scatter_put(2, dot(act2[...], w[DOWN][...], NT))
    scatter_send(2, 0)
    reduce_across(DOWN)
    scatter_step(1, 0)
    scatter_step(1, 1)
    scatter_step(1, 6)
    scatter_send(1, 3)
    scatter_step(1, 3)
    scatter_step(1, 7)
    reduce_column(DOWN, 2)
    scatter_send(2, 1)
    scatter_step(1, 2)
    weight_grad(UPS, flat(n2), gu2[...])
    scatter_step(1, 5)
    scatter_step(1, 4)
    scatter_send(2, 2)
    reduce_across(UPS)
    scatter_step(2, 1)
    scatter_step(2, 0)
    reduce_column(DOWN, 3)
    normed_two_grad = scatter_end(1)
    second_norm_back(normed_two_grad)
    scatter_step(2, 4)
    scatter_step(2, 5)
    pair_start(3, hl)
    reduce_column(UPS, 2)
    scatter_step(2, 6)
    reduce_column(DOWN, 1)
    pair_step(3, hl)
    scatter_send(2, 3)
    scatter_step(2, 2)
    reduce_column(UPS, 3)
    pair_end(3, hl)
    attend_back()
    weight_grad(QKV, flat(n1), gqkv2[...])
    scatter_put(3, dot(gqkv2[...], w[QKV][...], NT))
    pair_scatter_send(3)
    reduce_across(QKV)
    reduce_column(UPS, 1)
    pair_scatter_step(3)
    weight_grad(OUT, flat(hl), att2[...])
    reduce_column(QKV, 2)
    reduce_across(OUT)
    normed_one_grad = pair_scatter_end(3)
    first_norm_back(normed_one_grad)
    gains_start()
    reduce_column(UPS, 0)
    reduce_column(QKV, 1)
    scatter_step(2, 7)
    scatter_step(2, 3)
    reduce_column(QKV, 3)
    reduce_column(OUT, 2)
    gains_step()
    output_rows(scatter_end(2))
    half_send(1)
    reduce_end(UPS)
    half_send(0)
    reduce_end(DOWN)
    reduce_column(OUT, 1)
    reduce_column(OUT, 3)
    reduce_column(QKV, 0)
    reduce_column(OUT, 0)
    reduce_end(QKV)
    gains_end()
    reduce_column(DOWN, 0)
    half_end(0)
    half_end(1)
    reduce_end(OUT)
    for cond, done in pending:
        if cond is None:
            done()
        else:
            pl.when(cond)(done)


def output_kernel(
    fi0, fi1, fi2, fi3, halves, gains,
    mixed, frames_grad, dq, dk, dv, do, dg, du, dd, first_gain, second_gain,
):
    inner = lax.rem(lax.axis_index("dp"), INNER)
    mixed[...] = halves[0]
    frames_grad[...] = halves[1]
    for fi, outs in ((fi0, (dq, dk, dv)), (fi1, (do,)), (fi2, (dg, du)), (fi3, (dd,))):
        cols = fi.shape[2] // (2 * len(outs))
        blocks = -(-outs[0].shape[2] // cols)
        for b in range(blocks):
            n = min(cols, outs[0].shape[2] - b * cols)
            for s in range(2):
                for j, out in enumerate(outs):
                    at = (s * len(outs) + j) * cols
                    total = fi[b, :, at:at + n].astype(F32)
                    for other in range(b + blocks, ZN, blocks):
                        total = total + fi[other, :, at:at + n].astype(F32)
                    out[s, :, b * cols:b * cols + n] = total
    width = gains.shape[1]
    share = first_gain.shape[1]
    turned = pltpu.roll(gains[...], lax.rem(width - inner * share, width), 1)
    first_gain[...] = turned[0:2, 0:share]
    second_gain[...] = turned[2:4, 0:share]


def run_layer(frames, cot, dialogue, padding, position_set, gain_one, gain_two, weights):
    wq, wk, wv, wo, wg, wu, wd = weights
    width = frames.shape[2]
    rows = frames.shape[0] * frames.shape[1] // 2
    d_rows = wq.shape[1]
    qb = wq.shape[2] // BLOCKS[QKV]
    units = wg.shape[2]
    fb = -(-units // (BLOCKS[UPS] * LANES)) * LANES
    group, pair_group = 8 * rows, 4 * rows
    dma = pltpu.SemaphoreType.DMA
    vm = pltpu.VMEM
    shape = jax.ShapeDtypeStruct
    cols = (6 * qb, 2 * qb, 4 * fb, 2 * fb)
    blocks = [(ZN, d_rows, n) for n in cols]
    block_rows = (8, rows, width)
    pair_rows = (4, rows, width)
    four = (4, 4, rows, width)
    scratch = (
        [vm((count, d_rows, n), BF) for count, n in zip(BLOCKS, cols)]
        + [vm(b, BF) for b in blocks]
        + [vm((width, n), BF) for n in cols]
        + [vm((ZN, 4, d_rows, n), BF) for n in cols]
        + [vm((2, ZN, d_rows, n), BF) for n in cols]
        + [vm((ZN, d_rows, n), BF) for n in cols] * 2
        + [vm((2, 16, width), BF)]
        + [vm(pair_rows, BF), vm(block_rows, BF), vm(block_rows, BF), vm(pair_rows, BF)] + [vm((2,) + block_rows, F32)]
        + [vm(four, BF)] * 5
        + [vm((pair_group, qb), BF)] * 3
        + [vm((pair_group, 2 * qb), BF), vm((pair_group // LANES, qb // HDIM, LANES, LANES), F32)]
        + [vm((pair_group, 6 * qb), BF)]
        + [vm((group, 2 * fb), BF), vm((group, 4 * fb), BF), vm((group, fb), F32), vm((group, fb), F32)]
        + [vm((2, 4, 8, LANES), F32), vm((ZN, 8, width), F32), vm((8, 8, width), F32)]
        + [vm((rows, width), F32)] * 4 + [vm((3, rows, LANES), F32)]
        + [dma((4, 4)), dma((4, 4)), dma((4, 4, 2)), dma((4, INNER)), dma((4, 4)), dma((4, 24, CUTS)), dma((4, 8, CUTS))]
        + [dma((4, 4, CUTS))] * 5
        + [dma((4, 2)), dma((4, 2)), dma((4, 4)), dma((4, 4)), dma((4, 4)), dma((4, 4))]
        + [dma((2, 4)), dma((2, 4)), dma((2,)), dma((2,)), dma((4,)), dma((4,)), dma((8,)), dma((8,))]
    )
    spec = pl.BlockSpec(memory_space=pltpu.VMEM)
    scalars = pl.BlockSpec(memory_space=pltpu.SMEM)
    packed = pl.pallas_call(
        layer_kernel,
        out_shape=[shape(b, BF) for b in blocks] + [shape((2,) + frames.shape, BF), shape((8, width), F32)],
        in_specs=[spec] * 2 + [scalars] * 3 + [spec] * 9,
        out_specs=[spec] * 6,
        scratch_shapes=scratch,
        compiler_params=pltpu.CompilerParams(
            collective_id=0, has_side_effects=True, vmem_limit_bytes=63 * 2**20
        ),
        cost_estimate=pl.CostEstimate(flops=10**10, bytes_accessed=10**7, transcendentals=0),
        name="layer",
    )(frames, cot, dialogue, padding, position_set, gain_one, gain_two, *weights)
    grads = [shape(v.shape, F32) for v in weights]
    return pl.pallas_call(
        output_kernel,
        out_shape=[shape(frames.shape, BF)] * 2 + grads + [shape((2, d_rows), F32)] * 2,
        in_specs=[spec] * 6,
        out_specs=[spec] * 11,
        compiler_params=pltpu.CompilerParams(vmem_limit_bytes=63 * 2**20),
        cost_estimate=pl.CostEstimate(flops=10**6, bytes_accessed=10**7, transcendentals=0),
        name="outputs",
    )(*packed)


def per_device(
    frames, cotangent, dialogue, padding, position_set,
    query_weight, key_weight, value_weight, output_weight, gate_weight, up_weight, down_weight,
    attention_gain, feedforward_gain,
):
    dp = lax.axis_size("dp")
    outer = dp // INNER
    groups = [[o * INNER + i for o in range(outer)] for i in range(INNER)]
    width = frames.shape[-1]
    turn = (False, False, False, True, False, False, True)
    weights = [query_weight, key_weight, value_weight, output_weight, gate_weight, up_weight, down_weight]
    weights = [jnp.swapaxes(v, 1, 2) if t else v for v, t in zip(weights, turn)]

    def to_kernel(v):
        if outer == 1:
            return v
        cut = v.reshape(v.shape[:-1] + (outer, INNER, width // dp))
        return jnp.swapaxes(cut, -3, -2).reshape(v.shape)

    def from_kernel(v):
        if outer == 1:
            return v
        cut = v.reshape(v.shape[:-1] + (INNER, outer, width // dp))
        return jnp.swapaxes(cut, -3, -2).reshape(v.shape)

    if outer > 1:
        weights = [lax.all_gather(v, "dp", axis=1, tiled=True, axis_index_groups=groups) for v in weights]
    mixed, frames_grad, *rest = run_layer(
        to_kernel(frames), to_kernel(cotangent), dialogue, padding, position_set,
        to_kernel(attention_gain), to_kernel(feedforward_gain), weights,
    )
    grads, gains = rest[:7], rest[7:]
    if outer > 1:
        grads = [
            lax.psum_scatter(v, "dp", scatter_dimension=1, tiled=True, axis_index_groups=groups) for v in grads
        ]
        gains = [
            lax.psum_scatter(v, "dp", scatter_dimension=1, tiled=True, axis_index_groups=groups) for v in gains
        ]
    grads = [jnp.swapaxes(v, 1, 2) if t else v for v, t in zip(grads, turn)]
    return (from_kernel(mixed), from_kernel(frames_grad), *grads, *gains)


def solution(mesh):
    column = P(None, "dp", "tensor")
    row = P(None, "tensor", "dp")
    rows = P("dp", None, None)
    in_specs = (
        rows, rows, P("dp"), P("dp"), P(),
        column, column, column, row, column, column, row, P(), P(),
    )
    out_specs = (
        rows, rows, column, column, column, row, column, column, row, P(None, "dp"), P(None, "dp"),
    )
    return jax.shard_map(per_device, mesh=mesh, in_specs=in_specs, out_specs=out_specs, check_vma=False)
```

```python
import jax
import jax.numpy as jnp
from jax import lax
from jax.experimental import pallas as pl
from jax.experimental.pallas import tpu as pltpu
from jax.sharding import PartitionSpec as P

HDIM = 64
EPSILON = 1e-05
INNER = 16
ZN = 4
LANES = 128
CUTS = 2
MESH = pl.DeviceIdType.MESH
BF = jnp.bfloat16
F32 = jnp.float32
NN = (((1,), (0,)), ((), ()))
NT = (((1,), (1,)), ((), ()))
TN = (((0,), (0,)), ((), ()))
Q, K, V, O, GT, UP, DN = range(7)
BLOCKS = (2, 2, 2, 2, 4, 4, 4)


def chip_columns(weight_columns):
    return [-(-n // (blocks * LANES)) * LANES for n, blocks in zip(weight_columns, BLOCKS)]


def dot(a, b, dims=NN):
    return lax.dot_general(a, b, dims, preferred_element_type=F32)


def layer_kernel(
    frames_in, cot_in, dialogue_in, padding_in, position_in, gain_one_in, gain_two_in, weights_in,
    grads_out, halves_out, gains_out,
    frames, cot, dialogue, padding, position_set, gain_one, gain_two, weights,
    st, ga, w, dw, rc, sx, rx, fi,
    set_mask, n1, sd, n2, hl, pf,
    sb, sr, so, ru, rd,
    heads_in, heads_grad, att2, probs, gate, up, act2, gate_grad, up_grad,
    cnt, gain_col, gain_face, gain_sum, halves,
    u_one, u_two, hid, hgrad, small,
    in_s, out_s, wt_s, sp_r, ax_r, mc_r, ag_s, ag_r, pr_r, sy_s, sy_r, py_r, sz_s, su_r, sd_r, pu_r,
    gc_s, gc_r, gx_s, gx_r, gf_s, gf_r, c_s, c_r, y_s, y_r, g_s, g_r,
):
    idx = lax.axis_index("dp")
    y = lax.axis_index("tensor")
    inner = lax.rem(idx, INNER)
    base = idx - inner
    z = lax.div(inner, 4)
    x = lax.rem(lax.div(inner, 2), 2)
    c = lax.rem(inner, 2)

    def dev(zz, xx, cc, yy):
        return (base + zz * 4 + xx * 2 + cc, yy)

    def flip(v, bit):
        return 1 - v if bit else v

    def hop(k):
        return lax.rem(z + k, ZN)

    def remote(src, dst, ssem, rsem, device):
        return pltpu.make_async_remote_copy(
            src_ref=src, dst_ref=dst, send_sem=ssem, recv_sem=rsem,
            device_id=device, device_id_type=MESH,
        )

    low = lax.rem(z, 2)
    partner = dev(z, x, c, 1 - y)
    beside = dev(z + 1 - 2 * low, x, c, y)
    sibling = dev(z, x, 1 - c, y)
    across = dev(z, 1 - x, c, y)
    above = dev(hop(1), x, c, y)
    below = dev(hop(ZN - 1), x, c, y)
    column = [dev(hop(k), x, c, y) for k in (1, 2, 3)]
    face = [
        (flip(x, a), flip(c, b), flip(y, d))
        for a in (0, 1) for b in (0, 1) for d in (0, 1) if a or b or d
    ]
    rows, width = n1.shape[1:]
    half = rows // 16
    columns = chip_columns([ref.shape[2] for ref in weights])
    d_rows = weights[0].shape[1]
    own_slot = 2 * z + y
    pair_slot = 2 * low + y
    mine = pl.ds(half * y, half)
    slice_mine = 2 * x + c

    def send(cond, src, dst, ssem, rsem, device):
        copy = remote(src, dst, ssem, rsem, device)
        if cond is None:
            copy.start()
        else:
            pl.when(cond)(copy.start)

    def sent(ref, ssem, cond=None):
        if cond is None:
            remote(ref, ref, ssem, ssem, sibling).wait_send()
        else:
            pl.when(cond)(remote(ref, ref, ssem, ssem, sibling).wait_send)

    def arrived(dst, rsem, cond=None):
        def wait():
            remote(dst, dst, rsem, rsem, sibling).wait_recv()

        if cond is None:
            wait()
        else:
            pl.when(cond)(wait)

    sources = (frames_in.at[mine], cot_in.at[mine], dialogue_in, padding_in, position_in, gain_one_in, gain_two_in)
    targets = (frames, cot, dialogue, padding, position_set, gain_one, gain_two)
    inputs = [
        pltpu.make_async_copy(src, dst, in_s.at[n])
        for n, (src, dst) in enumerate(zip(sources + tuple(weights_in), targets + tuple(weights)))
    ]
    weight_inputs = inputs[len(targets):]
    for n in (0, 4, 5):
        inputs[n].start()
    for copy in weight_inputs[:3]:
        copy.start()

    barrier = pltpu.get_barrier_semaphore()
    for d in column:
        pl.semaphore_signal(barrier, inc=1, device_id=d, device_id_type=MESH)
    for xx, cc, yy in face:
        pl.semaphore_signal(barrier, inc=1, device_id=dev(z, xx, cc, yy), device_id_type=MESH)
    for n in (2, 3, 1, 6):
        inputs[n].start()
    for copy in weight_inputs[3:]:
        copy.start()

    def stage(g):
        n, ref = columns[g], weights[g]
        for b in range(BLOCKS[g]):
            here = min(n, ref.shape[2] - b * n)
            for s in range(2):
                st[g][b, :, s * n:s * n + here] = ref[s, :, b * n:b * n + here]
                if here < n:
                    st[g][b, :, s * n + here:(s + 1) * n] = jnp.zeros((d_rows, n - here), BF)

    for g in (Q, K, V):
        weight_inputs[g].wait()
        stage(g)

    inputs[4].wait()
    row_at = lax.broadcasted_iota(jnp.int32, (16, width), 0)
    row_set = jnp.zeros((16, width), jnp.int32)
    for p in range(16):
        row_set = jnp.where(row_at == p, position_set[p], row_set)
    for s in range(2):
        set_mask[s] = jnp.where(row_set == s, 1.0, 0.0).astype(BF)

    def gain_full(gain):
        m1 = set_mask[1].astype(F32)
        return jnp.where(m1 > 0.5, gain[1:2, :], gain[0:1, :])

    def tile_rows(v):
        return jnp.broadcast_to(v[None], (half, 16, v.shape[1])).reshape(rows, v.shape[1])

    def normalize(values, gain):
        inverse = lax.rsqrt(jnp.sum(values * values, axis=-1, keepdims=True) / width + EPSILON)
        unit = values * inverse
        return unit, inverse, (unit * tile_rows(gain_full(gain))).astype(BF)

    def own_rows(ref):
        return ref[...].reshape(rows, width).astype(F32)

    def zero(ref):
        for n in (1, 2):
            ref[n] = jnp.zeros(ref.shape[1:], ref.dtype)

    inputs[0].wait()
    inputs[5].wait()
    unit, inverse, normed = normalize(own_rows(frames), gain_one)
    u_one[...] = unit
    small[0] = jnp.broadcast_to(inverse, (rows, LANES))
    n1[pair_slot] = normed
    pl.when(z == 0)(lambda: zero(ru))
    pl.when(z == ZN - 1)(lambda: zero(rd))

    inputs[2].wait()
    inputs[3].wait()
    lane = lax.broadcasted_iota(jnp.int32, (8, LANES), 1)
    table = jnp.zeros((8, LANES), F32)
    for f in range(dialogue.shape[0]):
        table = table + jnp.where(lane == dialogue[f], padding[f].astype(F32), 0.0)
    cnt[0, z] = table
    pl.semaphore_wait(barrier, len(column) + len(face))

    def spread(g, k):
        send(None, st[g].at[lax.rem(hop(k), BLOCKS[g])], ga[g].at[z], wt_s.at[g], sp_r.at[g, k - 1],
             dev(hop(k), x, c, y))

    def piece_of(g, k, xx, cc):
        piece = hop(k) * 4 + 2 * xx + cc
        return w[g].at[pl.ds(pl.multiple_of(piece * d_rows, d_rows), d_rows), :]

    def multicast(g, k):
        if k:
            arrived(ga[g].at[hop(k)], sp_r.at[g, 3 - k])
        src = ga[g].at[hop(k)] if k else st[g].at[lax.rem(z, BLOCKS[g])]
        dst = piece_of(g, k, x, c)
        send(None, src, dst, wt_s.at[g], ax_r.at[g, k], across)
        send(None, src, dst, wt_s.at[g], mc_r.at[g], sibling)
        dst[...] = src[...]

    def forward(g, k):
        dst = piece_of(g, k, 1 - x, c)
        arrived(dst, ax_r.at[g, k])
        send(None, dst, dst, wt_s.at[g], mc_r.at[g], sibling)

    def weights_here(g):
        arrived(w[g].at[pl.ds(0, 8 * d_rows), :], mc_r.at[g])

    cut_rows = rows // CUTS

    def cut(q):
        return pl.ds(q * cut_rows, cut_rows)

    def gather_sem(which, slot, q):
        return (pr_r if which in (0, 3) else ag_r).at[which // 2, slot, q]

    def gather_send(which, buf, slot, q, cond, way, device):
        src = buf.at[slot, cut(q)]
        send(cond, src, src, ag_s.at[which, min(way, 1)], gather_sem(which, slot, q), device)

    def gather_start(which, buf):
        for q in range(CUTS):
            gather_send(which, buf, own_slot, q, z < ZN - 1, 1, above)
            gather_send(which, buf, own_slot, q, z > 0, 2, below)
            gather_send(which, buf, own_slot, q, None, 0, partner)

    def gather_step(which, buf, k):
        lo = 2 * jnp.maximum(z - k, 0) + y
        hi = 2 * jnp.minimum(z + k, ZN - 1) + y
        up, down = z >= k, z + k <= ZN - 1
        for q in range(CUTS):
            arrived(buf.at[lo, cut(q)], gather_sem(which, lo, q), cond=up)
            gather_send(which, buf, lo, q, up & (z < ZN - 1), 1, above)
            gather_send(which, buf, lo, q, up, 0, partner)
            arrived(buf.at[hi, cut(q)], gather_sem(which, hi, q), cond=down)
            gather_send(which, buf, hi, q, down & (z > 0), 2, below)
            gather_send(which, buf, hi, q, down, 0, partner)

    def gather_end(which, buf):
        slot = 2 * z + 1 - y
        for q in range(CUTS):
            arrived(buf.at[slot, cut(q)], gather_sem(which, slot, q))
        for k in (1, 2, 3):
            lo = 2 * jnp.maximum(z - k, 0) + 1 - y
            hi = 2 * jnp.minimum(z + k, ZN - 1) + 1 - y
            for q in range(CUTS):
                arrived(buf.at[lo, cut(q)], gather_sem(which, lo, q), cond=z >= k)
                arrived(buf.at[hi, cut(q)], gather_sem(which, hi, q), cond=z + k <= ZN - 1)

    def pair_start(which, buf):
        for q in range(CUTS):
            gather_send(which, buf, pair_slot, q, None, 1, beside)
            gather_send(which, buf, pair_slot, q, None, 0, partner)

    def pair_step(which, buf):
        slot = 2 * (1 - low) + y
        for q in range(CUTS):
            arrived(buf.at[slot, cut(q)], gather_sem(which, slot, q))
            gather_send(which, buf, slot, q, None, 0, partner)

    def pair_end(which, buf):
        slot, far = 2 * low + 1 - y, 2 * (1 - low) + 1 - y
        for q in range(CUTS):
            arrived(buf.at[slot, cut(q)], gather_sem(which, slot, q))
            arrived(buf.at[far, cut(q)], gather_sem(which, far, q))

    def far_first(i):
        orders = ((3, 2, 1, 0), (3, 0, 2, 1), (0, 3, 1, 2), (0, 1, 2, 3))
        b = jnp.int32(0)
        for zz, order in enumerate(orders):
            b = b + jnp.where(z == zz, order[i], 0)
        return b

    def row_sem(n, b, q):
        return (py_r if n in (0, 3) else sy_r).at[n // 2, b, q]

    def scatter_put(n, partial):
        blocks = partial.shape[0] // rows
        pf[n % 2, 0:blocks] = partial.reshape(blocks, rows, width)

    def scatter_send(n, i, b=None):
        b = far_first(i) if b is None else b
        for q in range(CUTS):
            sb[n, b, cut(q), :] = pf[n % 2, 2 * b + 1 - y, cut(q), :].astype(BF)
            send(None, sb.at[n, b, cut(q)], sr.at[n, b, cut(q)], sy_s.at[n], row_sem(n, b, q), partner)

    def chip_sum(n, b, q):
        arrived(sr.at[n, b, cut(q)], row_sem(n, b, q))
        return pf[n % 2, 2 * b + y, cut(q), :] + sr[n, b, cut(q), :].astype(F32)

    plan = (
        (True, 3, z <= 1), (False, 0, z >= 2), (True, 3, z == 2), (False, 0, z == 1),
        (True, 2, z <= 1), (False, 1, z >= 2), (True, 1, z == 0), (False, 2, z == 3),
    )

    def scatter_step(n, at):
        rising, b, cond = plan[at]
        if rising:
            inflow, buf, r, target = z > 0, ru, su_r, above
        else:
            inflow, buf, r, target = z < ZN - 1, rd, sd_r, below
        for q in range(CUTS):

            def step(q=q):
                total = chip_sum(n, b, q)
                arrived(buf.at[n, b, cut(q)], r.at[n - 1, b, q], cond=inflow)
                so[n, b, cut(q), :] = (total + buf[n, b, cut(q), :].astype(F32)).astype(BF)

            pl.when(cond)(step)
            send(cond, so.at[n, b, cut(q)], buf.at[n, b, cut(q)], sz_s.at[n], r.at[n - 1, b, q], target)

    def scatter_end(n):
        totals = []
        for q in range(CUTS):
            total = chip_sum(n, z, q)
            arrived(ru.at[n, z, cut(q)], su_r.at[n - 1, z, q], cond=z > 0)
            arrived(rd.at[n, z, cut(q)], sd_r.at[n - 1, z, q], cond=z < ZN - 1)
            totals.append(total + ru[n, z, cut(q), :].astype(F32) + rd[n, z, cut(q), :].astype(F32))
        return jnp.concatenate(totals, axis=0)

    def pair_scatter_send(n):
        scatter_send(n, 2, 1 - low)
        scatter_send(n, 3, low)

    def pair_scatter_step(n):
        b = 1 - low
        for q in range(CUTS):
            so[n, b, cut(q), :] = chip_sum(n, b, q).astype(BF)
            send(None, so.at[n, b, cut(q)], ru.at[n, b, cut(q)], sz_s.at[n], pu_r.at[n // 2, q], beside)

    def pair_scatter_end(n):
        totals = []
        for q in range(CUTS):
            total = chip_sum(n, low, q)
            arrived(ru.at[n, low, cut(q)], pu_r.at[n // 2, q])
            totals.append(total + ru[n, low, cut(q), :].astype(F32))
        return jnp.concatenate(totals, axis=0)

    def both_sets(v):
        count, n = v.shape
        three = v.reshape(count // 16, 16, n)
        return jnp.concatenate([(three * set_mask[s, :, 0:n][None]).reshape(count, n) for s in range(2)], axis=1)

    def choose(v):
        count, n = v.shape[0], v.shape[1] // 2
        m = jnp.broadcast_to(set_mask[1, :, 0:n].astype(F32)[None], (count // 16, 16, n)).reshape(count, n)
        return jnp.where(m > 0.5, v[:, n:], v[:, 0:n])

    def flat(buf):
        return buf[...].reshape(buf.shape[0] * rows, width)

    def weight_grad(g, values, grads):
        dw[g][...] = dot(values, grads, TN).astype(BF).reshape(dw[g].shape)
        for xx in (1 - x, x):
            send(None, dw[g].at[:, 2 * xx + 1 - c], rc[g].at[xx], gc_s.at[g], gc_r.at[g, xx], sibling)

    def reduce_across(g):
        arrived(rc[g].at[1 - x], gc_r.at[g, 1 - x])
        for k in (2, 1, 3, 0):
            zz = hop(k)
            sx[g][zz] = (dw[g][zz, 2 * (1 - x) + c].astype(F32) + rc[g][1 - x, zz].astype(F32)).astype(BF)
            send(None, sx[g].at[zz], rx[g].at[zz], gx_s.at[g], gx_r.at[g, zz], across)

    def reduce_column(g, k):
        zz = hop(k)
        if k == 2:
            arrived(rc[g].at[x], gc_r.at[g, x])
        arrived(rx[g].at[zz], gx_r.at[g, zz])
        total = dw[g][zz, 2 * x + c].astype(F32) + rc[g][x, zz].astype(F32) + rx[g][zz].astype(F32)
        if k:
            rx[g][zz] = total.astype(BF)
            send(None, rx[g].at[zz], fi[g].at[z], gf_s.at[g], gf_r.at[g], dev(zz, x, c, y))
        else:
            fi[g][z] = total.astype(BF)

    def reduce_end(g):
        arrived(fi[g].at[pl.ds(0, 3)], gf_r.at[g])
        outputs[g].start()

    outputs = [
        pltpu.make_async_copy(src, dst, out_s.at[n])
        for n, (src, dst) in enumerate(zip(tuple(fi) + (halves, gain_sum), tuple(grads_out) + (halves_out, gains_out)))
    ]

    def counts_start():
        for k in (1, 2, 3):
            send(None, cnt.at[0, z], cnt.at[0, z], c_s.at[0], c_r.at[0], dev(hop(k), x, c, y))

    def counts_step():
        arrived(cnt.at[0, pl.ds(0, 3)], c_r.at[0])
        cnt[1, slice_mine] = cnt[0, 0] + cnt[0, 1] + cnt[0, 2] + cnt[0, 3]
        for a, b in ((0, 1), (1, 0), (1, 1)):
            send(None, cnt.at[1, slice_mine], cnt.at[1, slice_mine], c_s.at[1], c_r.at[1],
                 dev(z, flip(x, a), flip(c, b), y))

    def seed_rows():
        frame_weight = small[1, mine, :]
        weight_rows = jnp.broadcast_to(frame_weight[:, None, 0:1], (half, 16, width)).reshape(rows, width)
        return own_rows(cot) * weight_rows

    def seed_here():
        arrived(cnt.at[1, pl.ds(0, 3)], c_r.at[1])
        inputs[1].wait()
        counts = cnt[1, 0] + cnt[1, 1] + cnt[1, 2] + cnt[1, 3]
        for f in range(dialogue.shape[0]):
            found = jnp.sum(jnp.where(lane == dialogue[f], counts, 0.0), axis=1, keepdims=True)
            loss = padding[f].astype(F32) * (dialogue.shape[0] * 1.0) / (found + 1.0)
            small[1, f:f + 1, :] = jnp.broadcast_to(loss[0:1, :], (1, LANES))
        sd[own_slot] = seed_rows().astype(BF)

    def stage_rest():
        for g in (O, GT, UP, DN):
            weight_inputs[g].wait()
            stage(g)

    bl = LANES
    r_at = lax.broadcasted_iota(jnp.int32, (bl, bl), 0)
    c_at = lax.broadcasted_iota(jnp.int32, (bl, bl), 1)
    seen = (c_at <= r_at) & (lax.div(r_at, 16) == lax.div(c_at, 16))
    qb = heads_in[0].shape[1]
    heads = qb // HDIM
    head_of = lax.div(lax.broadcasted_iota(jnp.int32, (bl, qb), 1), HDIM)
    scale = HDIM ** (-0.5)

    def only(v, h):
        return jnp.where(head_of == h, v, jnp.zeros_like(v))

    def project_heads(g):
        heads_in[g][...] = choose(dot(flat(n1), w[g][...])).astype(BF)

    def attend():
        attended = []
        for t in range(att2.shape[0] // bl):
            at = pl.ds(t * bl, bl)
            q, kk, v = heads_in[Q][at, :], heads_in[K][at, :], heads_in[V][at, :]
            out = jnp.zeros((bl, qb), F32)
            for h in range(heads):
                scores = dot(only(q, h), kk, NT) * scale
                scores = jnp.where(seen, scores, -1e30)
                e = jnp.exp(scores - jnp.max(scores, axis=-1, keepdims=True))
                e = jnp.where(seen, e, 0.0)
                p = e / jnp.sum(e, axis=-1, keepdims=True)
                probs[t, h] = p
                out = jnp.where(head_of == h, dot(p.astype(BF), v), out)
            attended.append(out.astype(BF))
        att2[...] = both_sets(jnp.concatenate(attended, axis=0))

    def attend_back():
        datt = choose(dot(flat(hl), w[O][...])).astype(BF)
        gq, gk, gv = [], [], []
        for t in range(att2.shape[0] // bl):
            at = pl.ds(t * bl, bl)
            q, kk, v = heads_in[Q][at, :], heads_in[K][at, :], heads_in[V][at, :]
            da = datt[t * bl:(t + 1) * bl, :]
            tq = jnp.zeros((bl, qb), F32)
            tk, tv = tq, tq
            for h in range(heads):
                p = probs[t, h]
                dp = dot(only(da, h), v, NT)
                tv = jnp.where(head_of == h, dot(p.astype(BF), da, TN), tv)
                ds = (p * (dp - jnp.sum(dp * p, axis=-1, keepdims=True))).astype(BF)
                tq = jnp.where(head_of == h, dot(ds, kk) * scale, tq)
                tk = jnp.where(head_of == h, dot(ds, q, TN) * scale, tk)
            gq.append(tq.astype(BF))
            gk.append(tk.astype(BF))
            gv.append(tv.astype(BF))
        for g, parts in ((Q, gq), (K, gk), (V, gv)):
            heads_grad[g][...] = both_sets(jnp.concatenate(parts, axis=0))

    def heads_back():
        return sum(dot(heads_grad[g][...], w[g][...], NT) for g in (Q, K, V))

    def gate_rows():
        gate[...] = choose(dot(flat(n2), w[GT][...]))

    def up_rows():
        up[...] = choose(dot(flat(n2), w[UP][...]))

    def active_rows():
        v = gate[...]
        act2[...] = both_sets((v * jax.nn.sigmoid(v) * up[...]).astype(BF))

    def active_back():
        active_grad = choose(dot(flat(sd), w[DN][...]))
        v = gate[...]
        sig = jax.nn.sigmoid(v)
        gate_grad[...] = both_sets((active_grad * up[...] * sig * (1.0 + v * (1.0 - sig))).astype(BF))
        up_grad[...] = both_sets((active_grad * (v * sig)).astype(BF))

    def feed_back():
        return dot(gate_grad[...], w[GT][...], NT) + dot(up_grad[...], w[UP][...], NT)

    def feed_out():
        return dot(act2[...], w[DN][...], NT)

    def set_sums(v, at):
        three = v.reshape(half, 16, width)
        for s in range(2):
            part = (three * set_mask[s].astype(F32)[None]).reshape(rows, width)
            gain_col[z, at + s:at + s + 1, :] = jnp.sum(part, axis=0, keepdims=True)

    def norm_back(gradient, gain, unit, inverse):
        scaled = gradient * tile_rows(gain_full(gain))
        return inverse * (scaled - unit * (jnp.sum(scaled * unit, axis=-1, keepdims=True) / width))

    def second_norm(attention):
        inputs[6].wait()
        hidden = own_rows(frames) + attention
        hid[...] = hidden
        unit, inverse, normed = normalize(hidden, gain_two)
        u_two[...] = unit
        small[2] = jnp.broadcast_to(inverse, (rows, LANES))
        n2[own_slot] = normed

    def second_norm_back(normed_two_grad):
        unit = u_two[...]
        hidden_grad = seed_rows() + norm_back(normed_two_grad, gain_two, unit, small[2][:, 0:1])
        hgrad[...] = hidden_grad
        hl[pair_slot] = hidden_grad.astype(BF)
        gain_col[z] = jnp.zeros((8, width), F32)
        set_sums(normed_two_grad * unit, 2)

    def first_norm_back(normed_one_grad):
        unit = u_one[...]
        set_sums(normed_one_grad * unit, 0)
        result = hgrad[...] + norm_back(normed_one_grad, gain_one, unit, small[0][:, 0:1])
        halves[1, mine] = result.astype(BF).reshape(half, 16, width)

    def output_rows(branch):
        halves[0, mine] = (hid[...] + branch).astype(BF).reshape(half, 16, width)

    def half_send(j):
        send(None, halves.at[j, mine], halves.at[j, mine], y_s.at[j], y_r.at[j], partner)

    def half_end(j):
        theirs = pl.ds(half * (1 - y), half)
        arrived(halves.at[j, theirs], y_r.at[j])

    place = 4 * x + 2 * c + y

    def gains_start():
        for k in (1, 2, 3):
            send(None, gain_col.at[z], gain_col.at[z], g_s.at[0], g_r.at[0], dev(hop(k), x, c, y))

    def gains_step():
        arrived(gain_col.at[pl.ds(0, 3)], g_r.at[0])
        gain_face[place] = gain_col[0] + gain_col[1] + gain_col[2] + gain_col[3]
        for xx, cc, yy in face:
            send(None, gain_face.at[place], gain_face.at[place], g_s.at[1], g_r.at[1], dev(z, xx, cc, yy))

    def gains_end():
        arrived(gain_face.at[pl.ds(0, 7)], g_r.at[1])
        total = gain_face[0]
        for j in range(1, 8):
            total = total + gain_face[j]
        gain_sum[...] = total
        outputs[8].start()

    counts_start()
    spread(K, 2)
    stage_rest()
    spread(V, 1)
    spread(V, 3)
    multicast(GT, 0)
    spread(O, 2)
    spread(O, 1)
    multicast(V, 0)
    multicast(O, 0)
    spread(Q, 3)
    spread(Q, 1)
    spread(K, 1)
    spread(K, 3)
    pair_start(0, n1)
    multicast(Q, 0)
    multicast(K, 2)
    counts_step()
    multicast(DN, 0)
    multicast(V, 1)
    spread(O, 3)
    spread(GT, 1)
    multicast(K, 0)
    multicast(K, 3)
    spread(V, 2)
    multicast(O, 3)
    multicast(K, 1)
    multicast(O, 1)
    spread(GT, 3)
    pair_step(0, n1)
    spread(Q, 2)
    spread(UP, 3)
    multicast(GT, 3)
    multicast(Q, 3)
    forward(O, 3)
    multicast(V, 3)
    spread(UP, 1)
    forward(GT, 0)
    multicast(O, 2)
    forward(K, 2)
    multicast(V, 2)
    forward(V, 0)
    forward(K, 0)
    seed_here()
    multicast(Q, 1)
    forward(O, 1)
    gather_start(1, sd)
    forward(O, 2)
    forward(K, 3)
    multicast(Q, 2)
    spread(UP, 2)
    forward(Q, 3)
    pair_end(0, n1)
    multicast(UP, 0)
    forward(V, 3)
    forward(K, 1)
    forward(O, 0)
    multicast(UP, 3)
    forward(DN, 0)
    forward(Q, 0)
    weights_here(K)
    forward(V, 2)
    forward(V, 1)
    spread(DN, 1)
    forward(Q, 1)
    forward(Q, 2)
    spread(DN, 3)
    multicast(GT, 1)
    project_heads(K)
    weights_here(O)
    weights_here(Q)
    forward(GT, 3)
    spread(DN, 2)
    weights_here(V)
    project_heads(V)
    project_heads(Q)
    attend()
    scatter_put(0, dot(att2[...], w[O][...], NT))
    pair_scatter_send(0)
    multicast(UP, 1)
    pair_scatter_step(0)
    gather_step(1, sd, 1)
    attention = pair_scatter_end(0)
    second_norm(attention)
    forward(UP, 0)
    multicast(DN, 1)
    forward(UP, 1)
    gather_start(2, n2)
    forward(UP, 3)
    multicast(UP, 2)
    gather_step(2, n2, 1)
    multicast(DN, 3)
    forward(DN, 1)
    spread(GT, 2)
    gather_step(2, n2, 2)
    multicast(DN, 2)
    gather_step(2, n2, 3)
    forward(DN, 3)
    gather_step(1, sd, 2)
    forward(UP, 2)
    forward(DN, 2)
    multicast(GT, 2)
    weights_here(UP)
    weights_here(DN)
    gather_end(2, n2)
    up_rows()
    forward(GT, 1)
    gather_step(1, sd, 3)
    forward(GT, 2)
    weights_here(GT)
    gate_rows()
    active_rows()
    scatter_put(2, feed_out())
    scatter_send(2, 0)
    gather_end(1, sd)
    active_back()
    scatter_put(1, feed_back())
    scatter_send(1, 0)
    scatter_send(1, 1)
    scatter_step(2, 0)
    weight_grad(GT, flat(n2), gate_grad[...])
    scatter_send(1, 2)
    scatter_step(1, 0)
    scatter_step(2, 1)
    reduce_across(GT)
    scatter_step(1, 1)
    scatter_send(2, 1)
    weight_grad(DN, flat(sd), act2[...])
    scatter_send(1, 3)
    scatter_step(1, 4)
    reduce_column(GT, 2)
    scatter_send(2, 2)
    scatter_step(1, 2)
    scatter_step(1, 5)
    scatter_send(2, 3)
    reduce_across(DN)
    weight_grad(UP, flat(n2), up_grad[...])
    scatter_step(1, 3)
    scatter_step(1, 7)
    scatter_step(1, 6)
    scatter_step(2, 4)
    reduce_column(DN, 2)
    normed_two_grad = scatter_end(1)
    scatter_step(2, 5)
    second_norm_back(normed_two_grad)
    pair_start(3, hl)
    reduce_column(GT, 1)
    reduce_across(UP)
    reduce_column(GT, 3)
    reduce_column(DN, 1)
    scatter_step(2, 6)
    pair_step(3, hl)
    reduce_column(UP, 2)
    pair_end(3, hl)
    scatter_step(2, 3)
    reduce_column(UP, 1)
    weight_grad(O, flat(hl), att2[...])
    attend_back()
    weight_grad(V, flat(n1), heads_grad[V][...])
    reduce_column(UP, 3)
    scatter_put(3, heads_back())
    reduce_across(V)
    scatter_step(2, 2)
    reduce_column(DN, 3)
    pair_scatter_send(3)
    weight_grad(Q, flat(n1), heads_grad[Q][...])
    weight_grad(K, flat(n1), heads_grad[K][...])
    reduce_column(V, 2)
    reduce_column(DN, 0)
    reduce_across(K)
    reduce_across(Q)
    pair_scatter_step(3)
    reduce_column(V, 1)
    reduce_column(K, 2)
    reduce_column(K, 1)
    scatter_step(2, 7)
    reduce_column(V, 3)
    reduce_column(Q, 2)
    reduce_column(GT, 0)
    reduce_across(O)
    normed_one_grad = pair_scatter_end(3)
    first_norm_back(normed_one_grad)
    gains_start()
    reduce_column(UP, 0)
    reduce_end(UP)
    reduce_column(K, 3)
    reduce_column(V, 0)
    reduce_end(V)
    reduce_column(O, 2)
    half_send(1)
    reduce_column(Q, 1)
    output_rows(scatter_end(2))
    reduce_column(Q, 3)
    reduce_column(K, 0)
    reduce_end(K)
    half_send(0)
    reduce_column(O, 1)
    gains_step()
    reduce_column(O, 3)
    reduce_end(GT)
    half_end(1)
    half_end(0)
    reduce_end(DN)
    reduce_column(Q, 0)
    reduce_end(Q)
    gains_end()
    reduce_column(O, 0)
    reduce_end(O)
    outputs[7].start()
    for g in range(len(weights)):
        sent(w[g].at[pl.ds(0, 15 * d_rows), :], wt_s.at[g])
        sent(dw[g].at[:, pl.ds(0, 2)], gc_s.at[g])
        sent(sx[g], gx_s.at[g])
        sent(rx[g].at[pl.ds(0, 3)], gf_s.at[g])
    for which, buf in ((1, sd), (2, n2)):
        sent(buf.at[pl.ds(0, 4)], ag_s.at[which, 0])
        sent(buf.at[pl.ds(0, 1)], ag_s.at[which, 1], cond=(z == 0) | (z == ZN - 1))
        sent(buf.at[pl.ds(0, 5)], ag_s.at[which, 1], cond=(z > 0) & (z < ZN - 1))
        sent(sb.at[which], sy_s.at[which])
        sent(so.at[which, pl.ds(0, 3)], sz_s.at[which])
    for which, buf in ((0, n1), (3, hl)):
        sent(buf.at[pl.ds(0, 2)], ag_s.at[which, 0])
        sent(buf.at[pl.ds(0, 1)], ag_s.at[which, 1])
        sent(sb.at[which, pl.ds(0, 2)], sy_s.at[which])
        sent(so.at[which, pl.ds(0, 1)], sz_s.at[which])
    for j in (0, 1):
        sent(cnt.at[j, pl.ds(0, 3)], c_s.at[j])
        sent(halves.at[j, mine], y_s.at[j])
    sent(gain_col.at[pl.ds(0, 3)], g_s.at[0])
    sent(gain_face.at[pl.ds(0, 7)], g_s.at[1])
    for copy in outputs:
        copy.wait()


def output_kernel(
    fi, halves, gains,
    mixed, frames_grad, dq, dk, dv, do, dg, du, dd, first_gain, second_gain,
):
    inner = lax.rem(lax.axis_index("dp"), INNER)
    mixed[...] = halves[0]
    frames_grad[...] = halves[1]
    outs = (dq, dk, dv, do, dg, du, dd)
    for g, n in enumerate(chip_columns([ref.shape[2] for ref in outs])):
        for b in range(BLOCKS[g]):
            here = min(n, outs[g].shape[2] - b * n)
            for s in range(2):
                lanes = slice(s * n, s * n + here)
                parts = [fi[g][other, :, lanes].astype(F32) for other in range(b, ZN, BLOCKS[g])]
                outs[g][s, :, b * n:b * n + here] = sum(parts)
    width = gains.shape[1]
    share = first_gain.shape[1]
    turned = pltpu.roll(gains[...], lax.rem(width - inner * share, width), 1)
    first_gain[...] = turned[0:2, 0:share]
    second_gain[...] = turned[2:4, 0:share]


def run_layer(frames, cot, dialogue, padding, position_set, gain_one, gain_two, weights):
    width = frames.shape[2]
    rows = frames.shape[0] * frames.shape[1] // 2
    d_rows = weights[0].shape[1]
    sizes = chip_columns([v.shape[2] for v in weights])
    count = len(sizes)
    group, pair_group = 8 * rows, 4 * rows
    dma = pltpu.SemaphoreType.DMA
    vm = pltpu.VMEM
    shape = jax.ShapeDtypeStruct
    block_rows, pair_rows = (8, rows, width), (4, rows, width)
    four = (4, 4, rows, width)
    own = [(ZN, d_rows, 2 * n) for n in sizes]
    qb, fb = sizes[Q], sizes[GT]
    own_frames = (frames.shape[0] // 2,) + frames.shape[1:]
    scratch = (
        [vm(own_frames, BF)] * 2
        + [pltpu.SMEM(v.shape, v.dtype) for v in (dialogue, padding, position_set)]
        + [vm(gain_one.shape, F32)] * 2
        + [[vm(v.shape, BF) for v in weights]]
        + [[vm((blocks, d_rows, 2 * n), BF) for blocks, n in zip(BLOCKS, sizes)]]
        + [[vm(v, BF) for v in own]]
        + [[vm((width, 2 * n), BF) for n in sizes]]
        + [[vm((ZN, 4, d_rows, 2 * n), BF) for n in sizes]]
        + [[vm((2, ZN, d_rows, 2 * n), BF) for n in sizes]]
        + [[vm(v, BF) for v in own]] * 3
        + [vm((2, 16, width), BF)]
        + [vm(pair_rows, BF), vm(block_rows, BF), vm(block_rows, BF), vm(pair_rows, BF)] + [vm((2,) + block_rows, F32)]
        + [vm(four, BF)] * 5
        + [[vm((pair_group, qb), BF)] * 3, [vm((pair_group, 2 * qb), BF)] * 3, vm((pair_group, 2 * qb), BF)]
        + [vm((pair_group // LANES, qb // HDIM, LANES, LANES), F32)]
        + [vm((group, fb), F32)] * 2
        + [vm((group, 2 * fb), BF)] * 3
        + [vm((2, 4, 8, LANES), F32), vm((ZN, 8, width), F32), vm((8, 8, width), F32), vm((8, width), F32)]
        + [vm((2,) + frames.shape, BF)]
        + [vm((rows, width), F32)] * 4 + [vm((3, rows, LANES), F32)]
        + [dma((7 + count,)), dma((2 + count,))]
        + [dma((count,)), dma((count, 3)), dma((count, 4)), dma((count,))]
        + [dma((4, 2)), dma((2, 8, CUTS)), dma((2, 4, CUTS))]
        + [dma((4,)), dma((2, 4, CUTS)), dma((2, 2, CUTS)), dma((4,)), dma((2, 4, CUTS)), dma((2, 4, CUTS)), dma((2, CUTS))]
        + [dma((count,)), dma((count, 2)), dma((count,)), dma((count, 4)), dma((count,)), dma((count,))]
        + [dma((2,))] * 6
    )
    any_place = pl.BlockSpec(memory_space=pl.ANY)
    spec = pl.BlockSpec(memory_space=pltpu.VMEM)
    packed = pl.pallas_call(
        layer_kernel,
        out_shape=[[shape(v, BF) for v in own], shape((2,) + frames.shape, BF), shape((8, width), F32)],
        in_specs=[any_place] * 7 + [[any_place] * count],
        out_specs=[[any_place] * count, any_place, any_place],
        scratch_shapes=scratch,
        compiler_params=pltpu.CompilerParams(
            collective_id=0, has_side_effects=True, vmem_limit_bytes=63 * 2**20
        ),
        cost_estimate=pl.CostEstimate(flops=10**10, bytes_accessed=10**7, transcendentals=0),
        name="layer",
    )(frames, cot, dialogue, padding, position_set, gain_one, gain_two, list(weights))
    grads = [shape(v.shape, F32) for v in weights]
    return pl.pallas_call(
        output_kernel,
        out_shape=[shape(frames.shape, BF)] * 2 + grads + [shape((2, d_rows), F32)] * 2,
        in_specs=[[spec] * count, spec, spec],
        out_specs=[spec] * 11,
        compiler_params=pltpu.CompilerParams(vmem_limit_bytes=63 * 2**20),
        cost_estimate=pl.CostEstimate(flops=10**6, bytes_accessed=10**7, transcendentals=0),
        name="outputs",
    )(*packed)


def per_device(
    frames, cotangent, dialogue, padding, position_set,
    query_weight, key_weight, value_weight, output_weight, gate_weight, up_weight, down_weight,
    attention_gain, feedforward_gain,
):
    dp = lax.axis_size("dp")
    outer = dp // INNER
    groups = [[o * INNER + i for o in range(outer)] for i in range(INNER)]
    width = frames.shape[-1]
    turn = (False, False, False, True, False, False, True)
    weights = [query_weight, key_weight, value_weight, output_weight, gate_weight, up_weight, down_weight]
    weights = [jnp.swapaxes(v, 1, 2) if t else v for v, t in zip(weights, turn)]

    def to_kernel(v):
        if outer == 1:
            return v
        cut = v.reshape(v.shape[:-1] + (outer, INNER, width // dp))
        return jnp.swapaxes(cut, -3, -2).reshape(v.shape)

    def from_kernel(v):
        if outer == 1:
            return v
        cut = v.reshape(v.shape[:-1] + (INNER, outer, width // dp))
        return jnp.swapaxes(cut, -3, -2).reshape(v.shape)

    if outer > 1:
        weights = [lax.all_gather(v, "dp", axis=1, tiled=True, axis_index_groups=groups) for v in weights]
    mixed, frames_grad, *rest = run_layer(
        to_kernel(frames), to_kernel(cotangent), dialogue, padding, position_set,
        to_kernel(attention_gain), to_kernel(feedforward_gain), weights,
    )
    grads, gains = rest[:7], rest[7:]
    if outer > 1:
        grads = [
            lax.psum_scatter(v, "dp", scatter_dimension=1, tiled=True, axis_index_groups=groups) for v in grads
        ]
        gains = [
            lax.psum_scatter(v, "dp", scatter_dimension=1, tiled=True, axis_index_groups=groups) for v in gains
        ]
    grads = [jnp.swapaxes(v, 1, 2) if t else v for v, t in zip(grads, turn)]
    return (from_kernel(mixed), from_kernel(frames_grad), *grads, *gains)


def solution(mesh):
    column = P(None, "dp", "tensor")
    row = P(None, "tensor", "dp")
    rows = P("dp", None, None)
    in_specs = (
        rows, rows, P("dp"), P("dp"), P(),
        column, column, column, row, column, column, row, P(), P(),
    )
    out_specs = (
        rows, rows, column, column, column, row, column, column, row, P(None, "dp"), P(None, "dp"),
    )
    return jax.shard_map(per_device, mesh=mesh, in_specs=in_specs, out_specs=out_specs, check_vma=False)
```

```python
import jax
import jax.numpy as jnp
from jax import lax
from jax.experimental import pallas as pl
from jax.experimental.pallas import tpu as pltpu
from jax.sharding import PartitionSpec as P

HDIM = 64
EPSILON = 1e-05
INNER = 16
ZN = 4
LANES = 128
CUTS = 2
MESH = pl.DeviceIdType.MESH
BF = jnp.bfloat16
F32 = jnp.float32
NN = (((1,), (0,)), ((), ()))
NT = (((1,), (1,)), ((), ()))
TN = (((0,), (0,)), ((), ()))
Q, K, V, O, GA, UA, DA, B1, B2 = range(9)
FEED = (4, 5, 6)
ATTENTION_BLOCKS, TAIL = 2, 64


def feed_columns(units):
    part = units // (ZN * LANES) * LANES
    assert units == ZN * part + ZN * TAIL + ZN // 2 * TAIL
    return part, ZN * part, ZN * (part + TAIL)


def group_lanes(attention_columns, units):
    chip = attention_columns // ATTENTION_BLOCKS
    return [2 * chip] * 4 + [2 * feed_columns(units)[0]] * 3 + [2 * TAIL * len(FEED)] * 2


def swap_halves(v):
    return pltpu.roll(v.astype(F32), TAIL, 1).astype(v.dtype)


def lower_lanes(v):
    return lax.broadcasted_iota(jnp.int32, v.shape, 1) < TAIL


def dot(a, b, dims=NN):
    return lax.dot_general(a, b, dims, preferred_element_type=F32)


def layer_kernel(
    frames_in, cot_in, dialogue_in, padding_in, position_in, gain_one_in, gain_two_in, weights_in,
    grads_out, halves_out, gains_out,
    frames, cot, dialogue, padding, position_set, gain_one, gain_two, weights,
    st, ga, w, dw, rc, sx, rx, fi,
    set_mask, n1, sd, n2, hl, pf,
    sb, sr, so, ru, rd,
    heads_in, heads_grad, att2, probs, gate, up, active_grad, act2, gate_grad, up_grad, tail_gate_up, tail_act,
    cnt, gain_col, gain_face, gain_sum, halves,
    u_one, u_two, hid, hgrad, small,
    in_s, out_s, wt_s, sp_r, ax_r, mc_r, ag_s, ag_r, pr_r, sy_s, sy_r, py_r, sz_s, su_r, sd_r, pu_r,
    gc_s, gc_r, gx_s, gx_r, gf_s, gf_r, c_s, c_r, y_s, y_r, g_s, g_r,
):
    idx = lax.axis_index("dp")
    y = lax.axis_index("tensor")
    inner = lax.rem(idx, INNER)
    base = idx - inner
    z = lax.div(inner, 4)
    x = lax.rem(lax.div(inner, 2), 2)
    c = lax.rem(inner, 2)

    def dev(zz, xx, cc, yy):
        return (base + zz * 4 + xx * 2 + cc, yy)

    def flip(v, bit):
        return 1 - v if bit else v

    def hop(k):
        return lax.rem(z + k, ZN)

    def remote(src, dst, ssem, rsem, device):
        return pltpu.make_async_remote_copy(
            src_ref=src, dst_ref=dst, send_sem=ssem, recv_sem=rsem,
            device_id=device, device_id_type=MESH,
        )

    low = lax.rem(z, 2)
    partner = dev(z, x, c, 1 - y)
    beside = dev(z + 1 - 2 * low, x, c, y)
    sibling = dev(z, x, 1 - c, y)
    across = dev(z, 1 - x, c, y)
    above = dev(hop(1), x, c, y)
    below = dev(hop(ZN - 1), x, c, y)
    column = [dev(hop(k), x, c, y) for k in (1, 2, 3)]
    face = [
        (flip(x, a), flip(c, b), flip(y, d))
        for a in (0, 1) for b in (0, 1) for d in (0, 1) if a or b or d
    ]
    rows, width = n1.shape[1:]
    half = rows // 16
    units = weights[FEED[0]].shape[2]
    part, first_b1, first_b2 = feed_columns(units)
    even = low == 0
    d_rows = weights[0].shape[1]
    own_slot = 2 * z + y
    pair_slot = 2 * low + y
    mine = pl.ds(half * y, half)
    slice_mine = 2 * x + c

    def send(cond, src, dst, ssem, rsem, device):
        copy = remote(src, dst, ssem, rsem, device)
        if cond is None:
            copy.start()
        else:
            pl.when(cond)(copy.start)

    def sent(ref, ssem, cond=None):
        if cond is None:
            remote(ref, ref, ssem, ssem, sibling).wait_send()
        else:
            pl.when(cond)(remote(ref, ref, ssem, ssem, sibling).wait_send)

    def arrived(dst, rsem, cond=None):
        def wait():
            remote(dst, dst, rsem, rsem, sibling).wait_recv()

        if cond is None:
            wait()
        else:
            pl.when(cond)(wait)

    sources = (frames_in.at[mine], cot_in.at[mine], dialogue_in, padding_in, position_in, gain_one_in, gain_two_in)
    targets = (frames, cot, dialogue, padding, position_set, gain_one, gain_two)
    inputs = [
        pltpu.make_async_copy(src, dst, in_s.at[n])
        for n, (src, dst) in enumerate(zip(sources + tuple(weights_in), targets + tuple(weights)))
    ]
    weight_inputs = inputs[len(targets):]
    for n in (0, 4, 5):
        inputs[n].start()
    for copy in weight_inputs[:3]:
        copy.start()

    barrier = pltpu.get_barrier_semaphore()
    for d in column:
        pl.semaphore_signal(barrier, inc=1, device_id=d, device_id_type=MESH)
    for xx, cc, yy in face:
        pl.semaphore_signal(barrier, inc=1, device_id=dev(z, xx, cc, yy), device_id_type=MESH)
    for n in (2, 3, 1, 6):
        inputs[n].start()
    for copy in weight_inputs[3:]:
        copy.start()

    def blocks_of(g):
        return ATTENTION_BLOCKS if g <= O else ZN

    def stage(g):
        n = st[g].shape[2] // 2
        for b in range(blocks_of(g)):
            for s in range(2):
                st[g][b, :, s * n:(s + 1) * n] = weights[g][s, :, b * n:(b + 1) * n]

    def stage_tail(g, first, b):
        at = first + (b // 2 if g == B2 else b) * TAIL
        tile = at // LANES * LANES
        for m, weight in enumerate(FEED):
            both = [weights[weight][s, :, tile:tile + LANES] for s in range(2)]
            if at == tile:
                here = jnp.where(lower_lanes(both[0]), both[0], swap_halves(both[1]))
            else:
                here = jnp.where(lower_lanes(both[0]), swap_halves(both[0]), both[1])
            st[g][b, :, m * LANES:(m + 1) * LANES] = here

    for g in (Q, K, V):
        weight_inputs[g].wait()
        stage(g)

    inputs[4].wait()
    row_at = lax.broadcasted_iota(jnp.int32, (16, width), 0)
    row_set = jnp.zeros((16, width), jnp.int32)
    for p in range(16):
        row_set = jnp.where(row_at == p, position_set[p], row_set)
    for s in range(2):
        set_mask[s] = jnp.where(row_set == s, 1.0, 0.0).astype(BF)

    def gain_full(gain):
        m1 = set_mask[1].astype(F32)
        return jnp.where(m1 > 0.5, gain[1:2, :], gain[0:1, :])

    def tile_rows(v):
        return jnp.broadcast_to(v[None], (half, 16, v.shape[1])).reshape(rows, v.shape[1])

    def normalize(values, gain):
        inverse = lax.rsqrt(jnp.sum(values * values, axis=-1, keepdims=True) / width + EPSILON)
        unit = values * inverse
        return unit, inverse, (unit * tile_rows(gain_full(gain))).astype(BF)

    def own_rows(ref):
        return ref[...].reshape(rows, width).astype(F32)

    def zero(ref):
        for n in (1, 2):
            ref[n] = jnp.zeros(ref.shape[1:], ref.dtype)

    inputs[0].wait()
    inputs[5].wait()
    unit, inverse, normed = normalize(own_rows(frames), gain_one)
    u_one[...] = unit
    small[0] = jnp.broadcast_to(inverse, (rows, LANES))
    n1[pair_slot] = normed
    pl.when(z == 0)(lambda: zero(ru))
    pl.when(z == ZN - 1)(lambda: zero(rd))

    inputs[2].wait()
    inputs[3].wait()
    lane = lax.broadcasted_iota(jnp.int32, (8, LANES), 1)
    table = jnp.zeros((8, LANES), F32)
    for f in range(dialogue.shape[0]):
        table = table + jnp.where(lane == dialogue[f], padding[f].astype(F32), 0.0)
    cnt[0, z] = table
    pl.semaphore_wait(barrier, len(column) + len(face))

    def used(g, k=0):
        if g != B2:
            return None
        return even if k % 2 == 0 else jnp.logical_not(even)

    def spread(g, k):
        send(used(g, k), st[g].at[lax.rem(hop(k), blocks_of(g))], ga[g].at[z], wt_s.at[g], sp_r.at[g, k - 1],
             dev(hop(k), x, c, y))

    def piece_of(g, k, xx, cc):
        piece = hop(k) * 4 + 2 * xx + cc
        return w[g].at[pl.ds(pl.multiple_of(piece * d_rows, d_rows), d_rows), :]

    def where_used(g, action):
        if used(g) is None:
            action()
        else:
            pl.when(used(g))(action)

    def multicast(g, k):
        def action():
            if k:
                arrived(ga[g].at[hop(k)], sp_r.at[g, 3 - k])
            src = ga[g].at[hop(k)] if k else st[g].at[lax.rem(z, blocks_of(g))]
            dst = piece_of(g, k, x, c)
            send(None, src, dst, wt_s.at[g], ax_r.at[g, k], across)
            send(None, src, dst, wt_s.at[g], mc_r.at[g], sibling)
            dst[...] = src[...]

        where_used(g, action)

    def forward(g, k):
        def action():
            dst = piece_of(g, k, 1 - x, c)
            arrived(dst, ax_r.at[g, k])
            send(None, dst, dst, wt_s.at[g], mc_r.at[g], sibling)

        where_used(g, action)

    def weights_here(g):
        arrived(w[g].at[pl.ds(0, 8 * d_rows), :], mc_r.at[g], cond=used(g))

    cut_rows = rows // CUTS

    def cut(q):
        return pl.ds(q * cut_rows, cut_rows)

    def gather_sem(which, slot, q):
        return (pr_r if which in (0, 3) else ag_r).at[which // 2, slot, q]

    def gather_send(which, buf, slot, q, cond, way, device):
        src = buf.at[slot, cut(q)]
        send(cond, src, src, ag_s.at[which, min(way, 1)], gather_sem(which, slot, q), device)

    def gather_start(which, buf):
        for q in range(CUTS):
            gather_send(which, buf, own_slot, q, z < ZN - 1, 1, above)
            gather_send(which, buf, own_slot, q, z > 0, 2, below)
            gather_send(which, buf, own_slot, q, None, 0, partner)

    def gather_step(which, buf, k):
        lo = 2 * jnp.maximum(z - k, 0) + y
        hi = 2 * jnp.minimum(z + k, ZN - 1) + y
        up, down = z >= k, z + k <= ZN - 1
        for q in range(CUTS):
            arrived(buf.at[lo, cut(q)], gather_sem(which, lo, q), cond=up)
            gather_send(which, buf, lo, q, up & (z < ZN - 1), 1, above)
            gather_send(which, buf, lo, q, up, 0, partner)
            arrived(buf.at[hi, cut(q)], gather_sem(which, hi, q), cond=down)
            gather_send(which, buf, hi, q, down & (z > 0), 2, below)
            gather_send(which, buf, hi, q, down, 0, partner)

    def gather_end(which, buf):
        slot = 2 * z + 1 - y
        for q in range(CUTS):
            arrived(buf.at[slot, cut(q)], gather_sem(which, slot, q))
        for k in (1, 2, 3):
            lo = 2 * jnp.maximum(z - k, 0) + 1 - y
            hi = 2 * jnp.minimum(z + k, ZN - 1) + 1 - y
            for q in range(CUTS):
                arrived(buf.at[lo, cut(q)], gather_sem(which, lo, q), cond=z >= k)
                arrived(buf.at[hi, cut(q)], gather_sem(which, hi, q), cond=z + k <= ZN - 1)

    def pair_start(which, buf):
        for q in range(CUTS):
            gather_send(which, buf, pair_slot, q, None, 1, beside)
            gather_send(which, buf, pair_slot, q, None, 0, partner)

    def pair_step(which, buf):
        slot = 2 * (1 - low) + y
        for q in range(CUTS):
            arrived(buf.at[slot, cut(q)], gather_sem(which, slot, q))
            gather_send(which, buf, slot, q, None, 0, partner)

    def pair_end(which, buf):
        slot, far = 2 * low + 1 - y, 2 * (1 - low) + 1 - y
        for q in range(CUTS):
            arrived(buf.at[slot, cut(q)], gather_sem(which, slot, q))
            arrived(buf.at[far, cut(q)], gather_sem(which, far, q))

    def far_first(i):
        orders = ((3, 2, 1, 0), (3, 0, 2, 1), (0, 3, 1, 2), (0, 1, 2, 3))
        b = jnp.int32(0)
        for zz, order in enumerate(orders):
            b = b + jnp.where(z == zz, order[i], 0)
        return b

    def row_sem(n, b, q):
        return (py_r if n in (0, 3) else sy_r).at[n // 2, b, q]

    def scatter_put(n, partial):
        blocks = partial.shape[0] // rows
        pf[n % 2, 0:blocks] = partial.reshape(blocks, rows, width)

    def scatter_add(n, partial):
        blocks = partial.shape[0] // rows
        pf[n % 2, 0:blocks] += partial.reshape(blocks, rows, width)

    def scatter_send(n, i, b=None):
        b = far_first(i) if b is None else b
        for q in range(CUTS):
            sb[n, b, cut(q), :] = pf[n % 2, 2 * b + 1 - y, cut(q), :].astype(BF)
            send(None, sb.at[n, b, cut(q)], sr.at[n, b, cut(q)], sy_s.at[n], row_sem(n, b, q), partner)

    def chip_sum(n, b, q):
        arrived(sr.at[n, b, cut(q)], row_sem(n, b, q))
        return pf[n % 2, 2 * b + y, cut(q), :] + sr[n, b, cut(q), :].astype(F32)

    plan = (
        (True, 3, z <= 1), (False, 0, z >= 2), (True, 3, z == 2), (False, 0, z == 1),
        (True, 2, z <= 1), (False, 1, z >= 2), (True, 1, z == 0), (False, 2, z == 3),
    )

    def scatter_step(n, at):
        rising, b, cond = plan[at]
        if rising:
            inflow, buf, r, target = z > 0, ru, su_r, above
        else:
            inflow, buf, r, target = z < ZN - 1, rd, sd_r, below
        for q in range(CUTS):

            def step(q=q):
                total = chip_sum(n, b, q)
                arrived(buf.at[n, b, cut(q)], r.at[n - 1, b, q], cond=inflow)
                so[n, b, cut(q), :] = (total + buf[n, b, cut(q), :].astype(F32)).astype(BF)

            pl.when(cond)(step)
            send(cond, so.at[n, b, cut(q)], buf.at[n, b, cut(q)], sz_s.at[n], r.at[n - 1, b, q], target)

    def scatter_end(n):
        totals = []
        for q in range(CUTS):
            total = chip_sum(n, z, q)
            arrived(ru.at[n, z, cut(q)], su_r.at[n - 1, z, q], cond=z > 0)
            arrived(rd.at[n, z, cut(q)], sd_r.at[n - 1, z, q], cond=z < ZN - 1)
            totals.append(total + ru[n, z, cut(q), :].astype(F32) + rd[n, z, cut(q), :].astype(F32))
        return jnp.concatenate(totals, axis=0)

    def pair_scatter_send(n):
        scatter_send(n, 2, 1 - low)
        scatter_send(n, 3, low)

    def pair_scatter_step(n):
        b = 1 - low
        for q in range(CUTS):
            so[n, b, cut(q), :] = chip_sum(n, b, q).astype(BF)
            send(None, so.at[n, b, cut(q)], ru.at[n, b, cut(q)], sz_s.at[n], pu_r.at[n // 2, q], beside)

    def pair_scatter_end(n):
        totals = []
        for q in range(CUTS):
            total = chip_sum(n, low, q)
            arrived(ru.at[n, low, cut(q)], pu_r.at[n // 2, q])
            totals.append(total + ru[n, low, cut(q), :].astype(F32))
        return jnp.concatenate(totals, axis=0)

    def both_sets(v):
        count, n = v.shape
        three = v.reshape(count // 16, 16, n)
        return jnp.concatenate([(three * set_mask[s, :, 0:n][None]).reshape(count, n) for s in range(2)], axis=1)

    def choose(v):
        count, n = v.shape[0], v.shape[1] // 2
        m = jnp.broadcast_to(set_mask[1, :, 0:n].astype(F32)[None], (count // 16, 16, n)).reshape(count, n)
        return jnp.where(m > 0.5, v[:, n:], v[:, 0:n])

    def flat(buf):
        return buf[...].reshape(buf.shape[0] * rows, width)

    def weight_grad(g, values, grads):
        dw[g][...] = dot(values, grads, TN).astype(BF).reshape(dw[g].shape)
        weight_grad_send(g)

    def tail_grad(h):
        g = (B1, B2)[h]
        n = 2 * LANES
        dw[g][:, :, :, 0:n] = dot(flat(n2), tail_gate_up[h][...], TN).astype(BF).reshape(ZN, 4, d_rows, n)
        dw[g][:, :, :, n:] = dot(flat(sd), tail_act[h][...], TN).astype(BF).reshape(ZN, 4, d_rows, LANES)
        weight_grad_send(g)

    def weight_grad_send(g):
        for xx in (1 - x, x):
            send(used(g), dw[g].at[:, 2 * xx + 1 - c], rc[g].at[xx], gc_s.at[g], gc_r.at[g, xx], sibling)

    def reduce_across(g):
        def action():
            arrived(rc[g].at[1 - x], gc_r.at[g, 1 - x])
            for k in (2, 1, 3, 0):
                zz = hop(k)
                sx[g][zz] = (dw[g][zz, 2 * (1 - x) + c].astype(F32) + rc[g][1 - x, zz].astype(F32)).astype(BF)
                send(None, sx[g].at[zz], rx[g].at[zz], gx_s.at[g], gx_r.at[g, zz], across)

        where_used(g, action)

    def reduce_column(g, k):
        def action():
            zz = hop(k)
            if k == 2:
                arrived(rc[g].at[x], gc_r.at[g, x])
            arrived(rx[g].at[zz], gx_r.at[g, zz])
            total = dw[g][zz, 2 * x + c].astype(F32) + rc[g][x, zz].astype(F32) + rx[g][zz].astype(F32)
            if k:
                rx[g][zz] = total.astype(BF)
                send(None, rx[g].at[zz], fi[g].at[z], gf_s.at[g], gf_r.at[g], dev(zz, x, c, y))
            else:
                fi[g][z] = total.astype(BF)

        where_used(g, action)

    def reduce_end(g):
        if g == B2:
            arrived(fi[g].at[pl.ds(0, 1)], gf_r.at[g], cond=even)
            arrived(fi[g].at[pl.ds(0, 2)], gf_r.at[g], cond=jnp.logical_not(even))
        else:
            arrived(fi[g].at[pl.ds(0, 3)], gf_r.at[g])
        outputs[g].start()

    outputs = [
        pltpu.make_async_copy(src, dst, out_s.at[n])
        for n, (src, dst) in enumerate(zip(tuple(fi) + (halves, gain_sum), tuple(grads_out) + (halves_out, gains_out)))
    ]

    def counts_start():
        for k in (1, 2, 3):
            send(None, cnt.at[0, z], cnt.at[0, z], c_s.at[0], c_r.at[0], dev(hop(k), x, c, y))

    def counts_step():
        arrived(cnt.at[0, pl.ds(0, 3)], c_r.at[0])
        cnt[1, slice_mine] = cnt[0, 0] + cnt[0, 1] + cnt[0, 2] + cnt[0, 3]
        for a, b in ((0, 1), (1, 0), (1, 1)):
            send(None, cnt.at[1, slice_mine], cnt.at[1, slice_mine], c_s.at[1], c_r.at[1],
                 dev(z, flip(x, a), flip(c, b), y))

    def seed_rows():
        frame_weight = small[1, mine, :]
        weight_rows = jnp.broadcast_to(frame_weight[:, None, 0:1], (half, 16, width)).reshape(rows, width)
        return own_rows(cot) * weight_rows

    def seed_here():
        arrived(cnt.at[1, pl.ds(0, 3)], c_r.at[1])
        inputs[1].wait()
        counts = cnt[1, 0] + cnt[1, 1] + cnt[1, 2] + cnt[1, 3]
        for f in range(dialogue.shape[0]):
            found = jnp.sum(jnp.where(lane == dialogue[f], counts, 0.0), axis=1, keepdims=True)
            loss = padding[f].astype(F32) * (dialogue.shape[0] * 1.0) / (found + 1.0)
            small[1, f:f + 1, :] = jnp.broadcast_to(loss[0:1, :], (1, LANES))
        sd[own_slot] = seed_rows().astype(BF)

    def stage_rest():
        for copy in weight_inputs[O:]:
            copy.wait()
        for g in (O, GA, UA, DA):
            stage(g)
        for b in range(ZN):
            stage_tail(B1, first_b1, b)
        for b in (0, 2):
            stage_tail(B2, first_b2, b)
        zero_unused()

    def zero_unused():
        def zero_weights():
            w[B2][...] = jnp.zeros_like(w[B2])

        pl.when(jnp.logical_not(even))(zero_weights)
        for b in (1, 3):
            fi[B2][b] = jnp.zeros(fi[B2].shape[1:], BF)

    bl = LANES
    r_at = lax.broadcasted_iota(jnp.int32, (bl, bl), 0)
    c_at = lax.broadcasted_iota(jnp.int32, (bl, bl), 1)
    seen = (c_at <= r_at) & (lax.div(r_at, 16) == lax.div(c_at, 16))
    qb = heads_in[0].shape[1]
    heads = qb // HDIM
    head_of = lax.div(lax.broadcasted_iota(jnp.int32, (bl, qb), 1), HDIM)
    scale = HDIM ** (-0.5)

    def only(v, h):
        return jnp.where(head_of == h, v, jnp.zeros_like(v))

    def project_heads(g):
        heads_in[g][...] = choose(dot(flat(n1), w[g][...])).astype(BF)

    def attend():
        attended = []
        for t in range(att2.shape[0] // bl):
            at = pl.ds(t * bl, bl)
            q, kk, v = heads_in[Q][at, :], heads_in[K][at, :], heads_in[V][at, :]
            out = jnp.zeros((bl, qb), F32)
            for h in range(heads):
                scores = dot(only(q, h), kk, NT) * scale
                scores = jnp.where(seen, scores, -1e30)
                e = jnp.exp(scores - jnp.max(scores, axis=-1, keepdims=True))
                e = jnp.where(seen, e, 0.0)
                p = e / jnp.sum(e, axis=-1, keepdims=True)
                probs[t, h] = p
                out = jnp.where(head_of == h, dot(p.astype(BF), v), out)
            attended.append(out.astype(BF))
        att2[...] = both_sets(jnp.concatenate(attended, axis=0))

    def attend_back():
        datt = choose(dot(flat(hl), w[O][...])).astype(BF)
        gq, gk, gv = [], [], []
        for t in range(att2.shape[0] // bl):
            at = pl.ds(t * bl, bl)
            q, kk, v = heads_in[Q][at, :], heads_in[K][at, :], heads_in[V][at, :]
            da = datt[t * bl:(t + 1) * bl, :]
            tq = jnp.zeros((bl, qb), F32)
            tk, tv = tq, tq
            for h in range(heads):
                p = probs[t, h]
                dp = dot(only(da, h), v, NT)
                tv = jnp.where(head_of == h, dot(p.astype(BF), da, TN), tv)
                ds = (p * (dp - jnp.sum(dp * p, axis=-1, keepdims=True))).astype(BF)
                tq = jnp.where(head_of == h, dot(ds, kk) * scale, tq)
                tk = jnp.where(head_of == h, dot(ds, q, TN) * scale, tk)
            gq.append(tq.astype(BF))
            gk.append(tk.astype(BF))
            gv.append(tv.astype(BF))
        for g, parts in ((Q, gq), (K, gk), (V, gv)):
            heads_grad[g][...] = both_sets(jnp.concatenate(parts, axis=0))

    def heads_back():
        return sum(dot(heads_grad[g][...], w[g][...], NT) for g in (Q, K, V))

    def choose_tail(one, two):
        count = one.shape[0]
        m = jnp.broadcast_to(set_mask[1, :, 0:LANES].astype(F32)[None], (count // 16, 16, LANES)).reshape(count, LANES)
        first = jnp.where(lower_lanes(one), one, swap_halves(two))
        second = jnp.where(lower_lanes(one), swap_halves(one), two)
        return jnp.where(m > 0.5, second, first)

    def split_tail(v):
        count = v.shape[0]
        turned = swap_halves(v)
        m0, m1 = [
            jnp.broadcast_to(set_mask[s, :, 0:LANES].astype(F32)[None], (count // 16, 16, LANES)).reshape(count, LANES)
            for s in range(2)
        ]
        one = jnp.where(lower_lanes(v), v * m0, turned * m1)
        two = jnp.where(lower_lanes(v), turned * m0, v * m1)
        return one.astype(BF), two.astype(BF)

    def gate_up_rows():
        gate[0][...] = choose(dot(flat(n2), w[GA][...]))
        up[0][...] = choose(dot(flat(n2), w[UA][...]))

    def gate_up_tail():
        one = dot(flat(n2), w[B1][:, 0:2 * LANES])
        two = dot(flat(n2), w[B2][:, 0:2 * LANES])
        gate[1][...] = choose_tail(one[:, 0:LANES], two[:, 0:LANES])
        up[1][...] = choose_tail(one[:, LANES:], two[:, LANES:])

    def active_rows():
        v = gate[0][...]
        act2[...] = both_sets((v * jax.nn.sigmoid(v) * up[0][...]).astype(BF))

    def active_tail():
        v = gate[1][...]
        for h, tile in enumerate(split_tail(v * jax.nn.sigmoid(v) * up[1][...])):
            tail_act[h][...] = tile

    def active_dot():
        active_grad[0][...] = choose(dot(flat(sd), w[DA][...]))

    def active_dot_tail():
        active_grad[1][...] = choose_tail(dot(flat(sd), w[B1][:, 2 * LANES:]), dot(flat(sd), w[B2][:, 2 * LANES:]))

    def gate_up_grads(h):
        v = gate[h][...]
        sig = jax.nn.sigmoid(v)
        g = active_grad[h][...]
        return g * up[h][...] * sig * (1.0 + v * (1.0 - sig)), g * (v * sig)

    def active_back():
        first, second = gate_up_grads(0)
        gate_grad[...] = both_sets(first.astype(BF))
        up_grad[...] = both_sets(second.astype(BF))

    def active_back_tail():
        first, second = gate_up_grads(1)
        for h, (g_tile, u_tile) in enumerate(zip(split_tail(first), split_tail(second))):
            tail_gate_up[h][:, 0:LANES] = g_tile
            tail_gate_up[h][:, LANES:] = u_tile

    def feed_back():
        return dot(gate_grad[...], w[GA][...], NT) + dot(up_grad[...], w[UA][...], NT)

    def feed_back_tail():
        return sum(dot(tail_gate_up[h][...], w[g][:, 0:2 * LANES], NT) for h, g in enumerate((B1, B2)))

    def feed_out():
        tail = sum(dot(tail_act[h][...], w[g][:, 2 * LANES:], NT) for h, g in enumerate((B1, B2)))
        return dot(act2[...], w[DA][...], NT) + tail

    def set_sums(v, at):
        three = v.reshape(half, 16, width)
        for s in range(2):
            part = (three * set_mask[s].astype(F32)[None]).reshape(rows, width)
            total = jnp.sum(part, axis=0, keepdims=True)
            for side in range(2):
                gain_col[z, 4 * side + at + s:4 * side + at + s + 1, :] = total[:, side * width // 2:(side + 1) * width // 2]

    def norm_back(gradient, gain, unit, inverse):
        scaled = gradient * tile_rows(gain_full(gain))
        return inverse * (scaled - unit * (jnp.sum(scaled * unit, axis=-1, keepdims=True) / width))

    def second_norm(attention):
        inputs[6].wait()
        hidden = own_rows(frames) + attention
        hid[...] = hidden
        unit, inverse, normed = normalize(hidden, gain_two)
        u_two[...] = unit
        small[2] = jnp.broadcast_to(inverse, (rows, LANES))
        n2[own_slot] = normed

    def second_norm_back(normed_two_grad):
        unit = u_two[...]
        hidden_grad = seed_rows() + norm_back(normed_two_grad, gain_two, unit, small[2][:, 0:1])
        hgrad[...] = hidden_grad
        hl[pair_slot] = hidden_grad.astype(BF)
        set_sums(normed_two_grad * unit, 2)

    def first_norm_back(normed_one_grad):
        unit = u_one[...]
        set_sums(normed_one_grad * unit, 0)
        result = hgrad[...] + norm_back(normed_one_grad, gain_one, unit, small[0][:, 0:1])
        halves[1, mine] = result.astype(BF).reshape(half, 16, width)

    def output_rows(branch):
        halves[0, mine] = (hid[...] + branch).astype(BF).reshape(half, 16, width)

    def half_send(j):
        send(None, halves.at[j, mine], halves.at[j, mine], y_s.at[j], y_r.at[j], partner)

    def half_end(j):
        theirs = pl.ds(half * (1 - y), half)
        arrived(halves.at[j, theirs], y_r.at[j])

    place = 4 * x + 2 * c + y

    def gains_start():
        for k in (1, 2, 3):
            send(None, gain_col.at[z], gain_col.at[z], g_s.at[0], g_r.at[0], dev(hop(k), x, c, y))

    def gains_step():
        arrived(gain_col.at[pl.ds(0, 3)], g_r.at[0])
        gain_face[place] = gain_col[0] + gain_col[1] + gain_col[2] + gain_col[3]
        for xx, cc, yy in face:
            send(None, gain_face.at[place], gain_face.at[place], g_s.at[1], g_r.at[1], dev(z, xx, cc, yy))

    def gains_end():
        arrived(gain_face.at[pl.ds(0, 7)], g_r.at[1])
        total = gain_face[0]
        for j in range(1, 8):
            total = total + gain_face[j]
        gain_sum[...] = total
        outputs[len(st) + 1].start()

    counts_start()
    spread(K, 1)
    spread(Q, 3)
    spread(Q, 2)
    spread(K, 3)
    spread(V, 2)
    pair_start(0, n1)
    stage_rest()
    spread(Q, 1)
    multicast(V, 0)
    multicast(Q, 0)
    spread(B2, 3)
    spread(O, 2)
    spread(O, 1)
    spread(V, 1)
    spread(B1, 1)
    counts_step()
    multicast(O, 0)
    multicast(Q, 1)
    multicast(Q, 2)
    multicast(V, 2)
    spread(K, 2)
    spread(DA, 1)
    multicast(K, 0)
    multicast(B2, 1)
    forward(V, 2)
    forward(K, 0)
    multicast(Q, 3)
    forward(Q, 0)
    multicast(K, 1)
    multicast(O, 3)
    spread(V, 3)
    multicast(B2, 0)
    forward(Q, 3)
    forward(Q, 2)
    multicast(O, 2)
    pair_step(0, n1)
    multicast(V, 3)
    forward(V, 0)
    forward(Q, 1)
    spread(O, 3)
    spread(UA, 1)
    seed_here()
    multicast(DA, 3)
    forward(K, 1)
    multicast(K, 2)
    spread(DA, 3)
    multicast(V, 1)
    forward(B2, 1)
    gather_start(1, sd)
    multicast(K, 3)
    multicast(O, 1)
    weights_here(Q)
    forward(DA, 3)
    spread(GA, 3)
    forward(O, 0)
    spread(UA, 2)
    forward(V, 1)
    spread(B2, 2)
    multicast(B1, 3)
    pair_end(0, n1)
    spread(GA, 1)
    multicast(UA, 0)
    spread(B1, 3)
    forward(V, 3)
    multicast(B1, 0)
    gather_step(1, sd, 1)
    spread(UA, 3)
    multicast(DA, 1)
    spread(B2, 1)
    multicast(DA, 0)
    forward(O, 3)
    forward(O, 2)
    weights_here(V)
    forward(B2, 0)
    multicast(GA, 0)
    forward(K, 3)
    forward(K, 2)
    project_heads(Q)
    weights_here(K)
    forward(O, 1)
    project_heads(K)
    weights_here(O)
    project_heads(V)
    attend()
    scatter_put(0, dot(att2[...], w[O][...], NT))
    pair_scatter_send(0)
    multicast(B2, 2)
    multicast(GA, 3)
    spread(GA, 2)
    pair_scatter_step(0)
    multicast(GA, 1)
    multicast(UA, 3)
    multicast(B1, 1)
    forward(B1, 0)
    spread(DA, 2)
    gather_step(1, sd, 2)
    attention = pair_scatter_end(0)
    forward(DA, 0)
    second_norm(attention)
    gather_start(2, n2)
    multicast(GA, 2)
    gather_step(1, sd, 3)
    multicast(B2, 3)
    multicast(UA, 1)
    spread(B1, 2)
    forward(GA, 1)
    multicast(UA, 2)
    forward(UA, 0)
    forward(B1, 1)
    forward(B2, 2)
    forward(B2, 3)
    gather_step(2, n2, 1)
    forward(UA, 3)
    forward(GA, 3)
    multicast(DA, 2)
    forward(DA, 1)
    weights_here(B2)
    forward(UA, 1)
    forward(GA, 2)
    multicast(B1, 2)
    forward(UA, 2)
    forward(B1, 3)
    gather_step(2, n2, 2)
    forward(DA, 2)
    forward(GA, 0)
    gather_end(1, sd)
    forward(B1, 2)
    gather_step(2, n2, 3)
    weights_here(B1)
    weights_here(GA)
    active_dot_tail()
    weights_here(DA)
    weights_here(UA)
    active_dot()
    gather_end(2, n2)
    gate_up_tail()
    gate_up_rows()
    active_rows()
    active_tail()
    active_back()
    active_back_tail()
    scatter_put(1, feed_back())
    scatter_add(1, feed_back_tail())
    scatter_send(1, 0)
    scatter_send(1, 1)
    weight_grad(GA, flat(n2), gate_grad[...])
    scatter_put(2, feed_out())
    reduce_across(GA)
    scatter_send(1, 2)
    scatter_step(1, 0)
    scatter_send(1, 3)
    scatter_step(1, 1)
    scatter_send(2, 0)
    weight_grad(UA, flat(n2), up_grad[...])
    scatter_step(1, 5)
    scatter_send(2, 3)
    scatter_step(1, 4)
    scatter_step(1, 3)
    scatter_step(1, 2)
    reduce_column(GA, 2)
    reduce_across(UA)
    scatter_step(1, 6)
    scatter_step(1, 7)
    tail_grad(1)
    weight_grad(DA, flat(sd), act2[...])
    reduce_column(UA, 2)
    scatter_send(2, 1)
    reduce_across(DA)
    scatter_step(2, 1)
    scatter_step(2, 0)
    normed_two_grad = scatter_end(1)
    second_norm_back(normed_two_grad)
    pair_start(3, hl)
    reduce_column(GA, 1)
    reduce_column(GA, 3)
    reduce_column(DA, 2)
    scatter_send(2, 2)
    tail_grad(0)
    reduce_across(B1)
    reduce_column(UA, 1)
    reduce_across(B2)
    pair_step(3, hl)
    reduce_column(B1, 2)
    scatter_step(2, 3)
    scatter_step(2, 5)
    scatter_step(2, 4)
    reduce_column(B1, 3)
    scatter_step(2, 7)
    reduce_column(B1, 0)
    reduce_column(UA, 3)
    pair_end(3, hl)
    reduce_column(B2, 2)
    reduce_column(DA, 3)
    scatter_step(2, 2)
    weight_grad(O, flat(hl), att2[...])
    reduce_column(B2, 3)
    reduce_column(B1, 1)
    reduce_across(O)
    attend_back()
    weight_grad(V, flat(n1), heads_grad[V][...])
    weight_grad(K, flat(n1), heads_grad[K][...])
    scatter_step(2, 6)
    reduce_column(O, 2)
    scatter_put(3, heads_back())
    reduce_across(V)
    reduce_column(O, 3)
    reduce_column(O, 1)
    pair_scatter_send(3)
    output_rows(scatter_end(2))
    reduce_column(V, 2)
    weight_grad(Q, flat(n1), heads_grad[Q][...])
    reduce_across(K)
    pair_scatter_step(3)
    half_send(0)
    reduce_column(DA, 1)
    reduce_column(B2, 1)
    reduce_column(DA, 0)
    reduce_column(V, 1)
    reduce_column(GA, 0)
    normed_one_grad = pair_scatter_end(3)
    first_norm_back(normed_one_grad)
    reduce_column(K, 2)
    reduce_column(V, 3)
    reduce_column(B2, 0)
    reduce_column(K, 3)
    reduce_across(Q)
    reduce_column(UA, 0)
    gains_start()
    reduce_end(UA)
    reduce_end(DA)
    half_end(0)
    reduce_end(GA)
    reduce_column(V, 0)
    reduce_end(B1)
    reduce_column(K, 1)
    half_send(1)
    reduce_column(O, 0)
    reduce_column(Q, 2)
    reduce_column(Q, 3)
    reduce_end(V)
    reduce_column(Q, 1)
    reduce_column(Q, 0)
    reduce_column(K, 0)
    half_end(1)
    reduce_end(B2)
    reduce_end(O)
    gains_step()
    gains_end()
    reduce_end(K)
    reduce_end(Q)
    outputs[len(st)].start()
    for g in range(len(st)):
        if g == B2:
            sent(w[g].at[pl.ds(0, 13 * d_rows), :], wt_s.at[g], cond=even)
            sent(w[g].at[pl.ds(0, 2 * d_rows), :], wt_s.at[g], cond=jnp.logical_not(even))
        else:
            sent(w[g].at[pl.ds(0, 15 * d_rows), :], wt_s.at[g])
        sent(dw[g].at[:, pl.ds(0, 2)], gc_s.at[g], cond=used(g))
        sent(sx[g], gx_s.at[g], cond=used(g))
        sent(rx[g].at[pl.ds(0, 3)], gf_s.at[g], cond=used(g))
    for which, buf in ((1, sd), (2, n2)):
        sent(buf.at[pl.ds(0, 4)], ag_s.at[which, 0])
        sent(buf.at[pl.ds(0, 1)], ag_s.at[which, 1], cond=(z == 0) | (z == ZN - 1))
        sent(buf.at[pl.ds(0, 5)], ag_s.at[which, 1], cond=(z > 0) & (z < ZN - 1))
        sent(sb.at[which], sy_s.at[which])
        sent(so.at[which, pl.ds(0, 3)], sz_s.at[which])
    for which, buf in ((0, n1), (3, hl)):
        sent(buf.at[pl.ds(0, 2)], ag_s.at[which, 0])
        sent(buf.at[pl.ds(0, 1)], ag_s.at[which, 1])
        sent(sb.at[which, pl.ds(0, 2)], sy_s.at[which])
        sent(so.at[which, pl.ds(0, 1)], sz_s.at[which])
    for j in (0, 1):
        sent(cnt.at[j, pl.ds(0, 3)], c_s.at[j])
        sent(halves.at[j, mine], y_s.at[j])
    sent(gain_col.at[pl.ds(0, 3)], g_s.at[0])
    sent(gain_face.at[pl.ds(0, 7)], g_s.at[1])
    for copy in outputs:
        copy.wait()


def output_kernel(
    fi_in, halves_in, gains_in,
    mixed_out, frames_grad_out, grads_out, first_out, second_out,
    fi, halves, gains, grads, first_gain, second_gain, in_s, out_s,
):
    inner = lax.rem(lax.axis_index("dp"), INNER)
    order = (B1, B2, GA, UA, DA, Q, K, V, O)
    copies = {
        g: pltpu.make_async_copy(src, dst, in_s.at[g])
        for g, (src, dst) in enumerate(zip(tuple(fi_in) + (halves_in, gains_in), tuple(fi) + (halves, gains)))
    }
    for g in order + (len(order), len(order) + 1):
        copies[g].start()
    leaving = []

    def leave(src, dst):
        leaving.append(pltpu.make_async_copy(src, dst, out_s.at[len(leaving)]))
        leaving[-1].start()

    units = grads[FEED[0]].shape[2]
    _, first_b1, first_b2 = feed_columns(units)
    copies[B1].wait()
    copies[B2].wait()
    for g, weight in ((GA, 4), (UA, 5), (DA, 6), (Q, 0), (K, 1), (V, 2), (O, 3)):
        copies[g].wait()
        out = grads[weight]
        blocks = ATTENTION_BLOCKS if g <= O else ZN
        n = fi[g].shape[2] // 2
        for b in range(blocks):
            for s in range(2):
                parts = [fi[g][other, :, s * n:(s + 1) * n].astype(F32) for other in range(b, ZN, blocks)]
                out[s, :, b * n:(b + 1) * n] = sum(parts)
        if weight in FEED:
            m = FEED.index(weight)
            lanes = slice(m * LANES, (m + 1) * LANES)
            for tail, first, pair in ((B1, first_b1, (0, 1)), (B1, first_b1 + LANES, (2, 3)), (B2, first_b2, (0, 2))):
                one, two = [fi[tail][b, :, lanes].astype(F32) for b in pair]
                out[0, :, first:first + LANES] = jnp.where(lower_lanes(one), one, swap_halves(two))
                out[1, :, first:first + LANES] = jnp.where(lower_lanes(one), swap_halves(one), two)
        leave(out, grads_out[weight])
    copies[len(order)].wait()
    leave(halves.at[0], mixed_out)
    leave(halves.at[1], frames_grad_out)
    copies[len(order) + 1].wait()
    width = 2 * gains.shape[1]
    share = first_gain.shape[1]
    whole = jnp.concatenate([gains[0:4, :], gains[4:8, :]], axis=1)
    turned = pltpu.roll(whole, lax.rem(width - inner * share, width), 1)
    first_gain[...] = turned[0:2, 0:share]
    second_gain[...] = turned[2:4, 0:share]
    leave(first_gain, first_out)
    leave(second_gain, second_out)
    for copy in leaving:
        copy.wait()


def run_layer(frames, cot, dialogue, padding, position_set, gain_one, gain_two, weights):
    width = frames.shape[2]
    rows = frames.shape[0] * frames.shape[1] // 2
    d_rows = weights[0].shape[1]
    lanes = group_lanes(weights[0].shape[2], weights[FEED[0]].shape[2])
    count = len(lanes)
    group, pair_group = 8 * rows, 4 * rows
    dma = pltpu.SemaphoreType.DMA
    vm = pltpu.VMEM
    shape = jax.ShapeDtypeStruct
    block_rows, pair_rows = (8, rows, width), (4, rows, width)
    four = (4, 4, rows, width)
    own = [(ZN, d_rows, n) for n in lanes]
    qb, part = lanes[Q] // 2, lanes[GA] // 2
    own_frames = (frames.shape[0] // 2,) + frames.shape[1:]
    scratch = (
        [vm(own_frames, BF)] * 2
        + [pltpu.SMEM(v.shape, v.dtype) for v in (dialogue, padding, position_set)]
        + [vm(gain_one.shape, F32)] * 2
        + [[vm(v.shape, BF) for v in weights]]
        + [[vm((ATTENTION_BLOCKS if g <= O else ZN, d_rows, n), BF) for g, n in enumerate(lanes)]]
        + [[vm(v, BF) for v in own]]
        + [[vm((width, n), BF) for n in lanes]]
        + [[vm((ZN, 4, d_rows, n), BF) for n in lanes]]
        + [[vm((2, ZN, d_rows, n), BF) for n in lanes]]
        + [[vm(v, BF) for v in own]] * 3
        + [vm((2, 16, width), BF)]
        + [vm(pair_rows, BF), vm(block_rows, BF), vm(block_rows, BF), vm(pair_rows, BF)] + [vm((2,) + block_rows, F32)]
        + [vm(four, BF)] * 5
        + [[vm((pair_group, qb), BF)] * 3, [vm((pair_group, 2 * qb), BF)] * 3, vm((pair_group, 2 * qb), BF)]
        + [vm((pair_group // LANES, qb // HDIM, LANES, LANES), F32)]
        + [[vm((group, n), F32) for n in (part, LANES)]] * 3
        + [vm((group, 2 * part), BF)] * 3
        + [[vm((group, 2 * LANES), BF)] * 2, [vm((group, LANES), BF)] * 2]
        + [vm((2, 4, 8, LANES), F32), vm((ZN, 8, width // 2), F32), vm((8, 8, width // 2), F32), vm((8, width // 2), F32)]
        + [vm((2,) + frames.shape, BF)]
        + [vm((rows, width), F32)] * 4 + [vm((3, rows, LANES), F32)]
        + [dma((7 + len(weights),)), dma((2 + count,))]
        + [dma((count,)), dma((count, 3)), dma((count, 4)), dma((count,))]
        + [dma((4, 2)), dma((2, 8, CUTS)), dma((2, 4, CUTS))]
        + [dma((4,)), dma((2, 4, CUTS)), dma((2, 2, CUTS)), dma((4,)), dma((2, 4, CUTS)), dma((2, 4, CUTS)), dma((2, CUTS))]
        + [dma((count,)), dma((count, 2)), dma((count,)), dma((count, 4)), dma((count,)), dma((count,))]
        + [dma((2,))] * 6
    )
    any_place = pl.BlockSpec(memory_space=pl.ANY)
    packed = pl.pallas_call(
        layer_kernel,
        out_shape=[[shape(v, BF) for v in own], shape((2,) + frames.shape, BF), shape((8, width // 2), F32)],
        in_specs=[any_place] * 7 + [[any_place] * len(weights)],
        out_specs=[[any_place] * count, any_place, any_place],
        scratch_shapes=scratch,
        compiler_params=pltpu.CompilerParams(
            collective_id=0, has_side_effects=True, vmem_limit_bytes=63 * 2**20
        ),
        cost_estimate=pl.CostEstimate(flops=10**10, bytes_accessed=10**7, transcendentals=0),
        name="layer",
    )(frames, cot, dialogue, padding, position_set, gain_one, gain_two, list(weights))
    grads = [shape(v.shape, F32) for v in weights]
    gain = shape((2, d_rows), F32)
    mixed, frames_grad, grads, first_gain, second_gain = pl.pallas_call(
        output_kernel,
        out_shape=[shape(frames.shape, BF), shape(frames.shape, BF), grads, gain, gain],
        in_specs=[[any_place] * count, any_place, any_place],
        out_specs=[any_place, any_place, [any_place] * len(grads), any_place, any_place],
        scratch_shapes=[
            [vm(v, BF) for v in own], vm((2,) + frames.shape, BF), vm((8, width // 2), F32),
            [vm(v.shape, F32) for v in weights], vm(gain.shape, F32), vm(gain.shape, F32),
            dma((count + 2,)), dma((len(grads) + 4,)),
        ],
        compiler_params=pltpu.CompilerParams(vmem_limit_bytes=63 * 2**20),
        cost_estimate=pl.CostEstimate(flops=10**6, bytes_accessed=10**7, transcendentals=0),
        name="outputs",
    )(*packed)
    return mixed, frames_grad, *grads, first_gain, second_gain


def per_device(
    frames, cotangent, dialogue, padding, position_set,
    query_weight, key_weight, value_weight, output_weight, gate_weight, up_weight, down_weight,
    attention_gain, feedforward_gain,
):
    dp = lax.axis_size("dp")
    outer = dp // INNER
    groups = [[o * INNER + i for o in range(outer)] for i in range(INNER)]
    width = frames.shape[-1]
    turn = (False, False, False, True, False, False, True)
    weights = [query_weight, key_weight, value_weight, output_weight, gate_weight, up_weight, down_weight]
    weights = [jnp.swapaxes(v, 1, 2) if t else v for v, t in zip(weights, turn)]

    def to_kernel(v):
        if outer == 1:
            return v
        cut = v.reshape(v.shape[:-1] + (outer, INNER, width // dp))
        return jnp.swapaxes(cut, -3, -2).reshape(v.shape)

    def from_kernel(v):
        if outer == 1:
            return v
        cut = v.reshape(v.shape[:-1] + (INNER, outer, width // dp))
        return jnp.swapaxes(cut, -3, -2).reshape(v.shape)

    if outer > 1:
        weights = [lax.all_gather(v, "dp", axis=1, tiled=True, axis_index_groups=groups) for v in weights]
    mixed, frames_grad, *rest = run_layer(
        to_kernel(frames), to_kernel(cotangent), dialogue, padding, position_set,
        to_kernel(attention_gain), to_kernel(feedforward_gain), weights,
    )
    grads, gains = rest[:7], rest[7:]
    if outer > 1:
        grads = [
            lax.psum_scatter(v, "dp", scatter_dimension=1, tiled=True, axis_index_groups=groups) for v in grads
        ]
        gains = [
            lax.psum_scatter(v, "dp", scatter_dimension=1, tiled=True, axis_index_groups=groups) for v in gains
        ]
    grads = [jnp.swapaxes(v, 1, 2) if t else v for v, t in zip(grads, turn)]
    return (from_kernel(mixed), from_kernel(frames_grad), *grads, *gains)


def solution(mesh):
    column = P(None, "dp", "tensor")
    row = P(None, "tensor", "dp")
    rows = P("dp", None, None)
    in_specs = (
        rows, rows, P("dp"), P("dp"), P(),
        column, column, column, row, column, column, row, P(), P(),
    )
    out_specs = (
        rows, rows, column, column, column, row, column, column, row, P(None, "dp"), P(None, "dp"),
    )
    return jax.shard_map(per_device, mesh=mesh, in_specs=in_specs, out_specs=out_specs, check_vma=False)
```

```python
import jax
import jax.numpy as jnp
from jax import lax
from jax.experimental import pallas as pl
from jax.experimental.pallas import tpu as pltpu
from jax.sharding import PartitionSpec as P

HDIM = 64
EPSILON = 1e-05
INNER = 16
ZN = 4
LANES = 128
CUTS = 2
MESH = pl.DeviceIdType.MESH
BF = jnp.bfloat16
F32 = jnp.float32
NN = (((1,), (0,)), ((), ()))
NT = (((1,), (1,)), ((), ()))
TN = (((0,), (0,)), ((), ()))
Q, K, V, O, GA, UA, DA, B1, B2 = range(9)
FEED = (4, 5, 6)
ATTENTION_BLOCKS, TAIL = 2, 64


def feed_columns(units):
    part = units // (ZN * LANES) * LANES
    assert units == ZN * part + ZN * TAIL + ZN // 2 * TAIL
    return part, ZN * part, ZN * (part + TAIL)


def group_lanes(attention_columns, units):
    chip = attention_columns // ATTENTION_BLOCKS
    return [2 * chip] * 4 + [2 * feed_columns(units)[0]] * 3 + [2 * TAIL * len(FEED)] * 2


def swap_halves(v):
    return pltpu.roll(v.astype(F32), TAIL, 1).astype(v.dtype)


def lower_lanes(v):
    return lax.broadcasted_iota(jnp.int32, v.shape, 1) < TAIL


def dot(a, b, dims=NN):
    return lax.dot_general(a, b, dims, preferred_element_type=F32)


def layer_kernel(
    frames_in, cot_in, dialogue_in, padding_in, position_in, gain_one_in, gain_two_in, weights_in,
    grads_out, halves_out, gains_out,
    frames, cot, dialogue, padding, position_set, gain_one, gain_two, weights,
    st, ga, w, dw, rc, sx, rx, fi,
    set_mask, n1, sd, n2, hl, pf,
    sb, sr, so, ru, rd,
    heads_in, heads_grad, att2, probs, gate, up, active_grad, act2, gate_grad, up_grad, tail_gate_up, tail_act,
    cnt, gain_col, gain_face, gain_sum, halves,
    u_one, u_two, hid, hgrad, small,
    in_s, out_s, wt_s, sp_r, ax_r, mc_r, ag_s, ag_r, pr_r, sy_s, sy_r, py_r, sz_s, su_r, sd_r, pu_r,
    gc_s, gc_r, gx_s, gx_r, gf_s, gf_r, c_s, c_r, y_s, y_r, g_s, g_r,
):
    idx = lax.axis_index("dp")
    y = lax.axis_index("tensor")
    inner = lax.rem(idx, INNER)
    base = idx - inner
    z = lax.div(inner, 4)
    x = lax.rem(lax.div(inner, 2), 2)
    c = lax.rem(inner, 2)

    def dev(zz, xx, cc, yy):
        return (base + zz * 4 + xx * 2 + cc, yy)

    def flip(v, bit):
        return 1 - v if bit else v

    def hop(k):
        return lax.rem(z + k, ZN)

    def remote(src, dst, ssem, rsem, device):
        return pltpu.make_async_remote_copy(
            src_ref=src, dst_ref=dst, send_sem=ssem, recv_sem=rsem,
            device_id=device, device_id_type=MESH,
        )

    low = lax.rem(z, 2)
    partner = dev(z, x, c, 1 - y)
    beside = dev(z + 1 - 2 * low, x, c, y)
    sibling = dev(z, x, 1 - c, y)
    across = dev(z, 1 - x, c, y)
    above = dev(hop(1), x, c, y)
    below = dev(hop(ZN - 1), x, c, y)
    column = [dev(hop(k), x, c, y) for k in (1, 2, 3)]
    face = [
        (flip(x, a), flip(c, b), flip(y, d))
        for a in (0, 1) for b in (0, 1) for d in (0, 1) if a or b or d
    ]
    rows, width = n1.shape[1:]
    half = rows // 16
    units = weights[FEED[0]].shape[2]
    part, first_b1, first_b2 = feed_columns(units)
    even = low == 0
    d_rows = weights[0].shape[1]
    own_slot = 2 * z + y
    pair_slot = 2 * low + y
    mine = pl.ds(half * y, half)
    slice_mine = 2 * x + c

    def send(cond, src, dst, ssem, rsem, device):
        copy = remote(src, dst, ssem, rsem, device)
        if cond is None:
            copy.start()
        else:
            pl.when(cond)(copy.start)

    def sent(ref, ssem, cond=None):
        if cond is None:
            remote(ref, ref, ssem, ssem, sibling).wait_send()
        else:
            pl.when(cond)(remote(ref, ref, ssem, ssem, sibling).wait_send)

    def arrived(dst, rsem, cond=None):
        def wait():
            remote(dst, dst, rsem, rsem, sibling).wait_recv()

        if cond is None:
            wait()
        else:
            pl.when(cond)(wait)

    sources = (frames_in.at[mine], cot_in.at[mine], dialogue_in, padding_in, position_in, gain_one_in, gain_two_in)
    targets = (frames, cot, dialogue, padding, position_set, gain_one, gain_two)
    inputs = [
        pltpu.make_async_copy(src, dst, in_s.at[n])
        for n, (src, dst) in enumerate(zip(sources + tuple(weights_in), targets + tuple(weights)))
    ]
    weight_inputs = inputs[len(targets):]
    for n in (0, 4, 5):
        inputs[n].start()
    for copy in weight_inputs[:3]:
        copy.start()

    barrier = pltpu.get_barrier_semaphore()
    for d in column:
        pl.semaphore_signal(barrier, inc=1, device_id=d, device_id_type=MESH)
    for xx, cc, yy in face:
        pl.semaphore_signal(barrier, inc=1, device_id=dev(z, xx, cc, yy), device_id_type=MESH)
    for n in (2, 3, 1, 6):
        inputs[n].start()
    for copy in weight_inputs[3:]:
        copy.start()

    def blocks_of(g):
        return ATTENTION_BLOCKS if g <= O else ZN

    def stage(g):
        n = st[g].shape[2] // 2
        for b in range(blocks_of(g)):
            for s in range(2):
                st[g][b, :, s * n:(s + 1) * n] = weights[g][s, :, b * n:(b + 1) * n]

    def stage_tail(g, first, b):
        at = first + (b // 2 if g == B2 else b) * TAIL
        tile = at // LANES * LANES
        for m, weight in enumerate(FEED):
            both = [weights[weight][s, :, tile:tile + LANES] for s in range(2)]
            if at == tile:
                here = jnp.where(lower_lanes(both[0]), both[0], swap_halves(both[1]))
            else:
                here = jnp.where(lower_lanes(both[0]), swap_halves(both[0]), both[1])
            st[g][b, :, m * LANES:(m + 1) * LANES] = here

    for g in (Q, K, V):
        weight_inputs[g].wait()
        stage(g)

    inputs[4].wait()
    row_at = lax.broadcasted_iota(jnp.int32, (16, width), 0)
    row_set = jnp.zeros((16, width), jnp.int32)
    for p in range(16):
        row_set = jnp.where(row_at == p, position_set[p], row_set)
    for s in range(2):
        set_mask[s] = jnp.where(row_set == s, 1.0, 0.0).astype(BF)

    def gain_full(gain):
        m1 = set_mask[1].astype(F32)
        return jnp.where(m1 > 0.5, gain[1:2, :], gain[0:1, :])

    def tile_rows(v):
        return jnp.broadcast_to(v[None], (half, 16, v.shape[1])).reshape(rows, v.shape[1])

    def normalize(values, gain):
        inverse = lax.rsqrt(jnp.sum(values * values, axis=-1, keepdims=True) / width + EPSILON)
        unit = values * inverse
        return unit, inverse, (unit * tile_rows(gain_full(gain))).astype(BF)

    def own_rows(ref):
        return ref[...].reshape(rows, width).astype(F32)

    def zero(ref):
        for n in (1, 2):
            ref[n] = jnp.zeros(ref.shape[1:], ref.dtype)

    inputs[0].wait()
    inputs[5].wait()
    unit, inverse, normed = normalize(own_rows(frames), gain_one)
    u_one[...] = unit
    small[0] = jnp.broadcast_to(inverse, (rows, LANES))
    n1[pair_slot] = normed
    pl.when(z == 0)(lambda: zero(ru))
    pl.when(z == ZN - 1)(lambda: zero(rd))

    inputs[2].wait()
    inputs[3].wait()
    lane = lax.broadcasted_iota(jnp.int32, (8, LANES), 1)
    table = jnp.zeros((8, LANES), F32)
    for f in range(dialogue.shape[0]):
        table = table + jnp.where(lane == dialogue[f], padding[f].astype(F32), 0.0)
    cnt[0, z] = table
    pl.semaphore_wait(barrier, len(column) + len(face))

    def used(g, k=0):
        if g != B2:
            return None
        return even if k % 2 == 0 else jnp.logical_not(even)

    def spread(g, k):
        send(used(g, k), st[g].at[lax.rem(hop(k), blocks_of(g))], ga[g].at[z], wt_s.at[g], sp_r.at[g, k - 1],
             dev(hop(k), x, c, y))

    def piece_of(g, k, xx, cc):
        piece = hop(k) * 4 + 2 * xx + cc
        return w[g].at[pl.ds(pl.multiple_of(piece * d_rows, d_rows), d_rows), :]

    def where_used(g, action):
        if used(g) is None:
            action()
        else:
            pl.when(used(g))(action)

    def multicast(g, k):
        def action():
            if k:
                arrived(ga[g].at[hop(k)], sp_r.at[g, 3 - k])
            src = ga[g].at[hop(k)] if k else st[g].at[lax.rem(z, blocks_of(g))]
            dst = piece_of(g, k, x, c)
            send(None, src, dst, wt_s.at[g], ax_r.at[g, k], across)
            send(None, src, dst, wt_s.at[g], mc_r.at[g], sibling)
            dst[...] = src[...]

        where_used(g, action)

    def forward(g, k):
        def action():
            dst = piece_of(g, k, 1 - x, c)
            arrived(dst, ax_r.at[g, k])
            send(None, dst, dst, wt_s.at[g], mc_r.at[g], sibling)

        where_used(g, action)

    def weights_here(g):
        arrived(w[g].at[pl.ds(0, 8 * d_rows), :], mc_r.at[g], cond=used(g))

    cut_rows = rows // CUTS

    def cut(q):
        return pl.ds(q * cut_rows, cut_rows)

    def gather_sem(which, slot, q):
        return (pr_r if which in (0, 3) else ag_r).at[which // 2, slot, q]

    def gather_send(which, buf, slot, q, cond, way, device):
        src = buf.at[slot, cut(q)]
        send(cond, src, src, ag_s.at[which, min(way, 1)], gather_sem(which, slot, q), device)

    def gather_start(which, buf):
        for q in range(CUTS):
            gather_send(which, buf, own_slot, q, z < ZN - 1, 1, above)
            gather_send(which, buf, own_slot, q, z > 0, 2, below)
            gather_send(which, buf, own_slot, q, None, 0, partner)

    def gather_step(which, buf, k):
        lo = 2 * jnp.maximum(z - k, 0) + y
        hi = 2 * jnp.minimum(z + k, ZN - 1) + y
        up, down = z >= k, z + k <= ZN - 1
        for q in range(CUTS):
            arrived(buf.at[lo, cut(q)], gather_sem(which, lo, q), cond=up)
            gather_send(which, buf, lo, q, up & (z < ZN - 1), 1, above)
            gather_send(which, buf, lo, q, up, 0, partner)
            arrived(buf.at[hi, cut(q)], gather_sem(which, hi, q), cond=down)
            gather_send(which, buf, hi, q, down & (z > 0), 2, below)
            gather_send(which, buf, hi, q, down, 0, partner)

    def gather_end(which, buf):
        slot = 2 * z + 1 - y
        for q in range(CUTS):
            arrived(buf.at[slot, cut(q)], gather_sem(which, slot, q))
        for k in (1, 2, 3):
            lo = 2 * jnp.maximum(z - k, 0) + 1 - y
            hi = 2 * jnp.minimum(z + k, ZN - 1) + 1 - y
            for q in range(CUTS):
                arrived(buf.at[lo, cut(q)], gather_sem(which, lo, q), cond=z >= k)
                arrived(buf.at[hi, cut(q)], gather_sem(which, hi, q), cond=z + k <= ZN - 1)

    def pair_start(which, buf):
        for q in range(CUTS):
            gather_send(which, buf, pair_slot, q, None, 1, beside)
            gather_send(which, buf, pair_slot, q, None, 0, partner)

    def pair_step(which, buf):
        slot = 2 * (1 - low) + y
        for q in range(CUTS):
            arrived(buf.at[slot, cut(q)], gather_sem(which, slot, q))
            gather_send(which, buf, slot, q, None, 0, partner)

    def pair_end(which, buf):
        slot, far = 2 * low + 1 - y, 2 * (1 - low) + 1 - y
        for q in range(CUTS):
            arrived(buf.at[slot, cut(q)], gather_sem(which, slot, q))
            arrived(buf.at[far, cut(q)], gather_sem(which, far, q))

    def far_first(i):
        orders = ((3, 2, 1, 0), (3, 0, 2, 1), (0, 3, 1, 2), (0, 1, 2, 3))
        b = jnp.int32(0)
        for zz, order in enumerate(orders):
            b = b + jnp.where(z == zz, order[i], 0)
        return b

    def row_sem(n, b, q):
        return (py_r if n in (0, 3) else sy_r).at[n // 2, b, q]

    def scatter_put(n, partial):
        blocks = partial.shape[0] // rows
        pf[n % 2, 0:blocks] = partial.reshape(blocks, rows, width)

    def scatter_add(n, partial):
        blocks = partial.shape[0] // rows
        pf[n % 2, 0:blocks] += partial.reshape(blocks, rows, width)

    def scatter_send(n, i, b=None):
        b = far_first(i) if b is None else b
        for q in range(CUTS):
            sb[n, b, cut(q), :] = pf[n % 2, 2 * b + 1 - y, cut(q), :].astype(BF)
            send(None, sb.at[n, b, cut(q)], sr.at[n, b, cut(q)], sy_s.at[n], row_sem(n, b, q), partner)

    def chip_sum(n, b, q):
        arrived(sr.at[n, b, cut(q)], row_sem(n, b, q))
        return pf[n % 2, 2 * b + y, cut(q), :] + sr[n, b, cut(q), :].astype(F32)

    plan = (
        (True, 3, z <= 1), (False, 0, z >= 2), (True, 3, z == 2), (False, 0, z == 1),
        (True, 2, z <= 1), (False, 1, z >= 2), (True, 1, z == 0), (False, 2, z == 3),
    )

    def scatter_step(n, at):
        rising, b, cond = plan[at]
        if rising:
            inflow, buf, r, target = z > 0, ru, su_r, above
        else:
            inflow, buf, r, target = z < ZN - 1, rd, sd_r, below
        for q in range(CUTS):

            def step(q=q):
                total = chip_sum(n, b, q)
                arrived(buf.at[n, b, cut(q)], r.at[n - 1, b, q], cond=inflow)
                so[n, b, cut(q), :] = (total + buf[n, b, cut(q), :].astype(F32)).astype(BF)

            pl.when(cond)(step)
            send(cond, so.at[n, b, cut(q)], buf.at[n, b, cut(q)], sz_s.at[n], r.at[n - 1, b, q], target)

    def scatter_end(n):
        totals = []
        for q in range(CUTS):
            total = chip_sum(n, z, q)
            arrived(ru.at[n, z, cut(q)], su_r.at[n - 1, z, q], cond=z > 0)
            arrived(rd.at[n, z, cut(q)], sd_r.at[n - 1, z, q], cond=z < ZN - 1)
            totals.append(total + ru[n, z, cut(q), :].astype(F32) + rd[n, z, cut(q), :].astype(F32))
        return jnp.concatenate(totals, axis=0)

    def pair_scatter_send(n):
        scatter_send(n, 2, 1 - low)
        scatter_send(n, 3, low)

    def pair_scatter_step(n):
        b = 1 - low
        for q in range(CUTS):
            so[n, b, cut(q), :] = chip_sum(n, b, q).astype(BF)
            send(None, so.at[n, b, cut(q)], ru.at[n, b, cut(q)], sz_s.at[n], pu_r.at[n // 2, q], beside)

    def pair_scatter_end(n):
        totals = []
        for q in range(CUTS):
            total = chip_sum(n, low, q)
            arrived(ru.at[n, low, cut(q)], pu_r.at[n // 2, q])
            totals.append(total + ru[n, low, cut(q), :].astype(F32))
        return jnp.concatenate(totals, axis=0)

    def both_sets(v):
        count, n = v.shape
        three = v.reshape(count // 16, 16, n)
        return jnp.concatenate([(three * set_mask[s, :, 0:n][None]).reshape(count, n) for s in range(2)], axis=1)

    def choose(v):
        count, n = v.shape[0], v.shape[1] // 2
        m = jnp.broadcast_to(set_mask[1, :, 0:n].astype(F32)[None], (count // 16, 16, n)).reshape(count, n)
        return jnp.where(m > 0.5, v[:, n:], v[:, 0:n])

    def flat(buf):
        return buf[...].reshape(buf.shape[0] * rows, width)

    def weight_grad(g, values, grads):
        dw[g][...] = dot(values, grads, TN).astype(BF).reshape(dw[g].shape)
        weight_grad_send(g)

    def tail_grad(h):
        g = (B1, B2)[h]
        n = 2 * LANES
        dw[g][:, :, :, 0:n] = dot(flat(n2), tail_gate_up[h][...], TN).astype(BF).reshape(ZN, 4, d_rows, n)
        dw[g][:, :, :, n:] = dot(flat(sd), tail_act[h][...], TN).astype(BF).reshape(ZN, 4, d_rows, LANES)
        weight_grad_send(g)

    def weight_grad_send(g):
        for xx in (1 - x, x):
            send(used(g), dw[g].at[:, 2 * xx + 1 - c], rc[g].at[xx], gc_s.at[g], gc_r.at[g, xx], sibling)

    def reduce_across(g):
        def action():
            arrived(rc[g].at[1 - x], gc_r.at[g, 1 - x])
            for k in (2, 1, 3, 0):
                zz = hop(k)
                sx[g][zz] = (dw[g][zz, 2 * (1 - x) + c].astype(F32) + rc[g][1 - x, zz].astype(F32)).astype(BF)
                send(None, sx[g].at[zz], rx[g].at[zz], gx_s.at[g], gx_r.at[g, zz], across)

        where_used(g, action)

    def reduce_column(g, k):
        def action():
            zz = hop(k)
            if k == 2:
                arrived(rc[g].at[x], gc_r.at[g, x])
            arrived(rx[g].at[zz], gx_r.at[g, zz])
            total = dw[g][zz, 2 * x + c].astype(F32) + rc[g][x, zz].astype(F32) + rx[g][zz].astype(F32)
            if k:
                rx[g][zz] = total.astype(BF)
                send(None, rx[g].at[zz], fi[g].at[z], gf_s.at[g], gf_r.at[g], dev(zz, x, c, y))
            else:
                fi[g][z] = total.astype(BF)

        where_used(g, action)

    def reduce_end(g):
        if g == B2:
            arrived(fi[g].at[pl.ds(0, 1)], gf_r.at[g], cond=even)
            arrived(fi[g].at[pl.ds(0, 2)], gf_r.at[g], cond=jnp.logical_not(even))
        else:
            arrived(fi[g].at[pl.ds(0, 3)], gf_r.at[g])
        outputs[g].start()

    outputs = [
        pltpu.make_async_copy(src, dst, out_s.at[n])
        for n, (src, dst) in enumerate(zip(tuple(fi) + (halves, gain_sum), tuple(grads_out) + (halves_out, gains_out)))
    ]

    def counts_start():
        for k in (1, 2, 3):
            send(None, cnt.at[0, z], cnt.at[0, z], c_s.at[0], c_r.at[0], dev(hop(k), x, c, y))

    def counts_step():
        arrived(cnt.at[0, pl.ds(0, 3)], c_r.at[0])
        cnt[1, slice_mine] = cnt[0, 0] + cnt[0, 1] + cnt[0, 2] + cnt[0, 3]
        for a, b in ((0, 1), (1, 0), (1, 1)):
            send(None, cnt.at[1, slice_mine], cnt.at[1, slice_mine], c_s.at[1], c_r.at[1],
                 dev(z, flip(x, a), flip(c, b), y))

    def seed_rows():
        frame_weight = small[1, mine, :]
        weight_rows = jnp.broadcast_to(frame_weight[:, None, 0:1], (half, 16, width)).reshape(rows, width)
        return own_rows(cot) * weight_rows

    def seed_here():
        arrived(cnt.at[1, pl.ds(0, 3)], c_r.at[1])
        inputs[1].wait()
        counts = cnt[1, 0] + cnt[1, 1] + cnt[1, 2] + cnt[1, 3]
        for f in range(dialogue.shape[0]):
            found = jnp.sum(jnp.where(lane == dialogue[f], counts, 0.0), axis=1, keepdims=True)
            loss = padding[f].astype(F32) * (dialogue.shape[0] * 1.0) / (found + 1.0)
            small[1, f:f + 1, :] = jnp.broadcast_to(loss[0:1, :], (1, LANES))
        sd[own_slot] = seed_rows().astype(BF)

    def stage_rest():
        for copy in weight_inputs[O:]:
            copy.wait()
        for g in (O, GA, UA, DA):
            stage(g)
        for b in range(ZN):
            stage_tail(B1, first_b1, b)
        for b in (0, 2):
            stage_tail(B2, first_b2, b)
        zero_unused()

    def zero_unused():
        def zero_weights():
            w[B2][...] = jnp.zeros_like(w[B2])

        pl.when(jnp.logical_not(even))(zero_weights)
        for b in (1, 3):
            fi[B2][b] = jnp.zeros(fi[B2].shape[1:], BF)

    bl = LANES
    r_at = lax.broadcasted_iota(jnp.int32, (bl, bl), 0)
    c_at = lax.broadcasted_iota(jnp.int32, (bl, bl), 1)
    seen = (c_at <= r_at) & (lax.div(r_at, 16) == lax.div(c_at, 16))
    qb = heads_in[0].shape[1]
    heads = qb // HDIM
    head_of = lax.div(lax.broadcasted_iota(jnp.int32, (bl, qb), 1), HDIM)
    scale = HDIM ** (-0.5)

    def only(v, h):
        return jnp.where(head_of == h, v, jnp.zeros_like(v))

    def project_heads(g):
        heads_in[g][...] = choose(dot(flat(n1), w[g][...])).astype(BF)

    def attend():
        attended = []
        for t in range(att2.shape[0] // bl):
            at = pl.ds(t * bl, bl)
            q, kk, v = heads_in[Q][at, :], heads_in[K][at, :], heads_in[V][at, :]
            out = jnp.zeros((bl, qb), F32)
            for h in range(heads):
                scores = dot(only(q, h), kk, NT) * scale
                scores = jnp.where(seen, scores, -1e30)
                e = jnp.exp(scores - jnp.max(scores, axis=-1, keepdims=True))
                e = jnp.where(seen, e, 0.0)
                p = e / jnp.sum(e, axis=-1, keepdims=True)
                probs[t, h] = p
                out = jnp.where(head_of == h, dot(p.astype(BF), v), out)
            attended.append(out.astype(BF))
        att2[...] = both_sets(jnp.concatenate(attended, axis=0))

    def attend_back():
        datt = choose(dot(flat(hl), w[O][...])).astype(BF)
        gq, gk, gv = [], [], []
        for t in range(att2.shape[0] // bl):
            at = pl.ds(t * bl, bl)
            q, kk, v = heads_in[Q][at, :], heads_in[K][at, :], heads_in[V][at, :]
            da = datt[t * bl:(t + 1) * bl, :]
            tq = jnp.zeros((bl, qb), F32)
            tk, tv = tq, tq
            for h in range(heads):
                p = probs[t, h]
                dp = dot(only(da, h), v, NT)
                tv = jnp.where(head_of == h, dot(p.astype(BF), da, TN), tv)
                ds = (p * (dp - jnp.sum(dp * p, axis=-1, keepdims=True))).astype(BF)
                tq = jnp.where(head_of == h, dot(ds, kk) * scale, tq)
                tk = jnp.where(head_of == h, dot(ds, q, TN) * scale, tk)
            gq.append(tq.astype(BF))
            gk.append(tk.astype(BF))
            gv.append(tv.astype(BF))
        for g, parts in ((Q, gq), (K, gk), (V, gv)):
            heads_grad[g][...] = both_sets(jnp.concatenate(parts, axis=0))

    def heads_back():
        return sum(dot(heads_grad[g][...], w[g][...], NT) for g in (Q, K, V))

    def choose_tail(one, two):
        count = one.shape[0]
        m = jnp.broadcast_to(set_mask[1, :, 0:LANES].astype(F32)[None], (count // 16, 16, LANES)).reshape(count, LANES)
        first = jnp.where(lower_lanes(one), one, swap_halves(two))
        second = jnp.where(lower_lanes(one), swap_halves(one), two)
        return jnp.where(m > 0.5, second, first)

    def split_tail(v):
        count = v.shape[0]
        turned = swap_halves(v)
        m0, m1 = [
            jnp.broadcast_to(set_mask[s, :, 0:LANES].astype(F32)[None], (count // 16, 16, LANES)).reshape(count, LANES)
            for s in range(2)
        ]
        one = jnp.where(lower_lanes(v), v * m0, turned * m1)
        two = jnp.where(lower_lanes(v), turned * m0, v * m1)
        return one.astype(BF), two.astype(BF)

    def gate_up_rows():
        gate[0][...] = choose(dot(flat(n2), w[GA][...]))
        up[0][...] = choose(dot(flat(n2), w[UA][...]))

    def gate_up_tail():
        one = dot(flat(n2), w[B1][:, 0:2 * LANES])
        two = dot(flat(n2), w[B2][:, 0:2 * LANES])
        gate[1][...] = choose_tail(one[:, 0:LANES], two[:, 0:LANES])
        up[1][...] = choose_tail(one[:, LANES:], two[:, LANES:])

    def active_rows():
        v = gate[0][...]
        act2[...] = both_sets((v * jax.nn.sigmoid(v) * up[0][...]).astype(BF))

    def active_tail():
        v = gate[1][...]
        for h, tile in enumerate(split_tail(v * jax.nn.sigmoid(v) * up[1][...])):
            tail_act[h][...] = tile

    def active_dot():
        active_grad[0][...] = choose(dot(flat(sd), w[DA][...]))

    def active_dot_tail():
        active_grad[1][...] = choose_tail(dot(flat(sd), w[B1][:, 2 * LANES:]), dot(flat(sd), w[B2][:, 2 * LANES:]))

    def gate_up_grads(h):
        v = gate[h][...]
        sig = jax.nn.sigmoid(v)
        g = active_grad[h][...]
        return g * up[h][...] * sig * (1.0 + v * (1.0 - sig)), g * (v * sig)

    def active_back():
        first, second = gate_up_grads(0)
        gate_grad[...] = both_sets(first.astype(BF))
        up_grad[...] = both_sets(second.astype(BF))

    def active_back_tail():
        first, second = gate_up_grads(1)
        for h, (g_tile, u_tile) in enumerate(zip(split_tail(first), split_tail(second))):
            tail_gate_up[h][:, 0:LANES] = g_tile
            tail_gate_up[h][:, LANES:] = u_tile

    def feed_back():
        return dot(gate_grad[...], w[GA][...], NT) + dot(up_grad[...], w[UA][...], NT)

    def feed_back_tail():
        return sum(dot(tail_gate_up[h][...], w[g][:, 0:2 * LANES], NT) for h, g in enumerate((B1, B2)))

    def feed_out():
        tail = sum(dot(tail_act[h][...], w[g][:, 2 * LANES:], NT) for h, g in enumerate((B1, B2)))
        return dot(act2[...], w[DA][...], NT) + tail

    def set_sums(v, at):
        three = v.reshape(half, 16, width)
        for s in range(2):
            part = (three * set_mask[s].astype(F32)[None]).reshape(rows, width)
            total = jnp.sum(part, axis=0, keepdims=True)
            for side in range(2):
                gain_col[z, 4 * side + at + s:4 * side + at + s + 1, :] = total[:, side * width // 2:(side + 1) * width // 2]

    def norm_back(gradient, gain, unit, inverse):
        scaled = gradient * tile_rows(gain_full(gain))
        return inverse * (scaled - unit * (jnp.sum(scaled * unit, axis=-1, keepdims=True) / width))

    def second_norm(attention):
        inputs[6].wait()
        hidden = own_rows(frames) + attention
        hid[...] = hidden
        unit, inverse, normed = normalize(hidden, gain_two)
        u_two[...] = unit
        small[2] = jnp.broadcast_to(inverse, (rows, LANES))
        n2[own_slot] = normed

    def second_norm_back(normed_two_grad):
        unit = u_two[...]
        hidden_grad = seed_rows() + norm_back(normed_two_grad, gain_two, unit, small[2][:, 0:1])
        hgrad[...] = hidden_grad
        hl[pair_slot] = hidden_grad.astype(BF)
        set_sums(normed_two_grad * unit, 2)

    def first_norm_back(normed_one_grad):
        unit = u_one[...]
        set_sums(normed_one_grad * unit, 0)
        result = hgrad[...] + norm_back(normed_one_grad, gain_one, unit, small[0][:, 0:1])
        halves[1, mine] = result.astype(BF).reshape(half, 16, width)

    def output_rows(branch):
        halves[0, mine] = (hid[...] + branch).astype(BF).reshape(half, 16, width)

    def half_send(j):
        send(None, halves.at[j, mine], halves.at[j, mine], y_s.at[j], y_r.at[j], partner)

    def half_end(j):
        theirs = pl.ds(half * (1 - y), half)
        arrived(halves.at[j, theirs], y_r.at[j])

    place = 4 * x + 2 * c + y

    def gains_start():
        for k in (1, 2, 3):
            send(None, gain_col.at[z], gain_col.at[z], g_s.at[0], g_r.at[0], dev(hop(k), x, c, y))

    def gains_step():
        arrived(gain_col.at[pl.ds(0, 3)], g_r.at[0])
        gain_face[place] = gain_col[0] + gain_col[1] + gain_col[2] + gain_col[3]
        for xx, cc, yy in face:
            send(None, gain_face.at[place], gain_face.at[place], g_s.at[1], g_r.at[1], dev(z, xx, cc, yy))

    def gains_end():
        arrived(gain_face.at[pl.ds(0, 7)], g_r.at[1])
        total = gain_face[0]
        for j in range(1, 8):
            total = total + gain_face[j]
        gain_sum[...] = total
        outputs[len(st) + 1].start()

    counts_start()
    spread(Q, 1)
    spread(Q, 2)
    stage_rest()
    spread(K, 1)
    spread(K, 3)
    multicast(Q, 3)
    counts_step()
    spread(O, 3)
    multicast(Q, 0)
    multicast(K, 0)
    multicast(DA, 0)
    spread(K, 2)
    spread(V, 1)
    pair_start(0, n1)
    spread(V, 2)
    multicast(V, 0)
    forward(Q, 0)
    spread(O, 1)
    multicast(O, 1)
    spread(B2, 3)
    forward(DA, 0)
    multicast(B1, 0)
    seed_here()
    multicast(K, 1)
    spread(Q, 3)
    spread(O, 2)
    forward(Q, 3)
    spread(V, 3)
    forward(V, 0)
    forward(O, 1)
    pair_step(0, n1)
    gather_start(1, sd)
    multicast(K, 3)
    multicast(K, 2)
    spread(UA, 3)
    multicast(Q, 2)
    multicast(V, 2)
    forward(K, 3)
    spread(B2, 1)
    multicast(Q, 1)
    multicast(O, 0)
    multicast(O, 2)
    forward(K, 0)
    spread(B2, 2)
    spread(GA, 1)
    spread(DA, 3)
    forward(K, 2)
    multicast(O, 3)
    multicast(B2, 0)
    forward(V, 2)
    spread(B1, 3)
    multicast(V, 3)
    forward(K, 1)
    spread(DA, 1)
    forward(Q, 2)
    forward(Q, 1)
    multicast(V, 1)
    weights_here(Q)
    pair_end(0, n1)
    spread(B1, 2)
    forward(O, 2)
    spread(UA, 1)
    gather_step(1, sd, 1)
    forward(B1, 0)
    project_heads(Q)
    forward(O, 3)
    multicast(UA, 1)
    weights_here(K)
    forward(O, 0)
    forward(V, 3)
    forward(V, 1)
    project_heads(K)
    weights_here(V)
    project_heads(V)
    spread(GA, 3)
    attend()
    spread(GA, 2)
    spread(B1, 1)
    weights_here(O)
    multicast(B2, 2)
    multicast(DA, 1)
    multicast(UA, 0)
    scatter_put(0, dot(att2[...], w[O][...], NT))
    multicast(GA, 0)
    pair_scatter_send(0)
    pair_scatter_step(0)
    forward(B2, 0)
    multicast(B2, 3)
    forward(UA, 1)
    multicast(B1, 1)
    multicast(B2, 1)
    spread(DA, 2)
    multicast(B1, 2)
    gather_step(1, sd, 2)
    attention = pair_scatter_end(0)
    forward(B1, 1)
    second_norm(attention)
    multicast(UA, 3)
    multicast(DA, 3)
    gather_start(2, n2)
    spread(UA, 2)
    multicast(GA, 2)
    forward(B2, 3)
    multicast(GA, 1)
    forward(DA, 1)
    gather_step(1, sd, 3)
    multicast(B1, 3)
    forward(UA, 0)
    multicast(GA, 3)
    multicast(DA, 2)
    gather_step(2, n2, 1)
    forward(GA, 2)
    forward(B1, 2)
    multicast(UA, 2)
    forward(B2, 1)
    forward(B2, 2)
    forward(B1, 3)
    gather_step(2, n2, 2)
    gather_end(1, sd)
    forward(DA, 3)
    forward(DA, 2)
    forward(GA, 0)
    forward(GA, 3)
    gather_step(2, n2, 3)
    forward(UA, 2)
    weights_here(B2)
    weights_here(B1)
    forward(GA, 1)
    weights_here(DA)
    active_dot()
    forward(UA, 3)
    active_dot_tail()
    weights_here(GA)
    weights_here(UA)
    gather_end(2, n2)
    gate_up_rows()
    gate_up_tail()
    active_tail()
    active_back_tail()
    active_rows()
    active_back()
    scatter_put(1, feed_back())
    scatter_add(1, feed_back_tail())
    scatter_send(1, 0)
    scatter_send(1, 1)
    scatter_send(1, 2)
    weight_grad(DA, flat(sd), act2[...])
    scatter_put(2, feed_out())
    reduce_across(DA)
    scatter_send(1, 3)
    scatter_step(1, 1)
    scatter_step(1, 0)
    tail_grad(1)
    scatter_send(2, 0)
    scatter_step(1, 2)
    scatter_step(1, 3)
    scatter_step(1, 4)
    scatter_step(1, 5)
    reduce_across(B2)
    scatter_send(2, 2)
    reduce_column(DA, 2)
    reduce_column(DA, 1)
    tail_grad(0)
    weight_grad(UA, flat(n2), up_grad[...])
    scatter_step(1, 7)
    reduce_across(B1)
    scatter_step(1, 6)
    reduce_across(UA)
    scatter_step(2, 0)
    reduce_column(B2, 2)
    scatter_step(2, 1)
    normed_two_grad = scatter_end(1)
    scatter_send(2, 1)
    second_norm_back(normed_two_grad)
    reduce_column(B1, 2)
    pair_start(3, hl)
    weight_grad(GA, flat(n2), gate_grad[...])
    reduce_column(UA, 2)
    scatter_step(2, 2)
    reduce_column(B1, 3)
    reduce_column(UA, 3)
    reduce_across(GA)
    pair_step(3, hl)
    scatter_step(2, 4)
    reduce_column(GA, 2)
    reduce_column(B2, 3)
    scatter_send(2, 3)
    scatter_step(2, 5)
    reduce_column(UA, 1)
    reduce_column(B1, 1)
    scatter_step(2, 7)
    pair_end(3, hl)
    weight_grad(O, flat(hl), att2[...])
    reduce_column(GA, 1)
    attend_back()
    reduce_column(GA, 3)
    scatter_step(2, 6)
    reduce_across(O)
    scatter_put(3, heads_back())
    weight_grad(V, flat(n1), heads_grad[V][...])
    reduce_column(B1, 0)
    pair_scatter_send(3)
    reduce_column(O, 2)
    reduce_column(DA, 3)
    reduce_column(UA, 0)
    reduce_across(V)
    scatter_step(2, 3)
    pair_scatter_step(3)
    weight_grad(Q, flat(n1), heads_grad[Q][...])
    reduce_column(O, 1)
    reduce_column(O, 3)
    reduce_column(V, 2)
    reduce_across(Q)
    reduce_column(Q, 2)
    reduce_column(V, 3)
    reduce_column(B2, 1)
    reduce_column(O, 0)
    normed_one_grad = pair_scatter_end(3)
    weight_grad(K, flat(n1), heads_grad[K][...])
    first_norm_back(normed_one_grad)
    reduce_column(B2, 0)
    reduce_column(GA, 0)
    reduce_column(Q, 1)
    gains_start()
    output_rows(scatter_end(2))
    reduce_across(K)
    reduce_column(K, 2)
    reduce_column(V, 0)
    reduce_column(Q, 0)
    reduce_column(DA, 0)
    reduce_end(UA)
    reduce_end(B1)
    reduce_column(V, 1)
    half_send(0)
    reduce_column(Q, 3)
    reduce_end(O)
    reduce_end(GA)
    reduce_column(K, 3)
    half_send(1)
    reduce_column(K, 1)
    reduce_end(B2)
    gains_step()
    reduce_column(K, 0)
    half_end(0)
    half_end(1)
    reduce_end(Q)
    gains_end()
    reduce_end(DA)
    reduce_end(V)
    reduce_end(K)
    outputs[len(st)].start()
    for g in range(len(st)):
        if g == B2:
            sent(w[g].at[pl.ds(0, 13 * d_rows), :], wt_s.at[g], cond=even)
            sent(w[g].at[pl.ds(0, 2 * d_rows), :], wt_s.at[g], cond=jnp.logical_not(even))
        else:
            sent(w[g].at[pl.ds(0, 15 * d_rows), :], wt_s.at[g])
        sent(dw[g].at[:, pl.ds(0, 2)], gc_s.at[g], cond=used(g))
        sent(sx[g], gx_s.at[g], cond=used(g))
        sent(rx[g].at[pl.ds(0, 3)], gf_s.at[g], cond=used(g))
    for which, buf in ((1, sd), (2, n2)):
        sent(buf.at[pl.ds(0, 4)], ag_s.at[which, 0])
        sent(buf.at[pl.ds(0, 1)], ag_s.at[which, 1], cond=(z == 0) | (z == ZN - 1))
        sent(buf.at[pl.ds(0, 5)], ag_s.at[which, 1], cond=(z > 0) & (z < ZN - 1))
        sent(sb.at[which], sy_s.at[which])
        sent(so.at[which, pl.ds(0, 3)], sz_s.at[which])
    for which, buf in ((0, n1), (3, hl)):
        sent(buf.at[pl.ds(0, 2)], ag_s.at[which, 0])
        sent(buf.at[pl.ds(0, 1)], ag_s.at[which, 1])
        sent(sb.at[which, pl.ds(0, 2)], sy_s.at[which])
        sent(so.at[which, pl.ds(0, 1)], sz_s.at[which])
    for j in (0, 1):
        sent(cnt.at[j, pl.ds(0, 3)], c_s.at[j])
        sent(halves.at[j, mine], y_s.at[j])
    sent(gain_col.at[pl.ds(0, 3)], g_s.at[0])
    sent(gain_face.at[pl.ds(0, 7)], g_s.at[1])
    for copy in outputs:
        copy.wait()


def output_kernel(
    fi_in, halves_in, gains_in,
    mixed_out, frames_grad_out, grads_out, first_out, second_out,
    fi, halves, gains, grads, first_gain, second_gain, in_s, out_s,
):
    inner = lax.rem(lax.axis_index("dp"), INNER)
    order = (B1, B2, GA, UA, DA, Q, K, V, O)
    copies = {
        g: pltpu.make_async_copy(src, dst, in_s.at[g])
        for g, (src, dst) in enumerate(zip(tuple(fi_in) + (halves_in, gains_in), tuple(fi) + (halves, gains)))
    }
    for g in order + (len(order), len(order) + 1):
        copies[g].start()
    leaving = []

    def leave(src, dst):
        leaving.append(pltpu.make_async_copy(src, dst, out_s.at[len(leaving)]))
        leaving[-1].start()

    units = grads[FEED[0]].shape[2]
    _, first_b1, first_b2 = feed_columns(units)
    copies[B1].wait()
    copies[B2].wait()
    for g, weight in ((GA, 4), (UA, 5), (DA, 6), (Q, 0), (K, 1), (V, 2), (O, 3)):
        copies[g].wait()
        out = grads[weight]
        blocks = ATTENTION_BLOCKS if g <= O else ZN
        n = fi[g].shape[2] // 2
        for b in range(blocks):
            for s in range(2):
                parts = [fi[g][other, :, s * n:(s + 1) * n].astype(F32) for other in range(b, ZN, blocks)]
                out[s, :, b * n:(b + 1) * n] = sum(parts)
        if weight in FEED:
            m = FEED.index(weight)
            lanes = slice(m * LANES, (m + 1) * LANES)
            for tail, first, pair in ((B1, first_b1, (0, 1)), (B1, first_b1 + LANES, (2, 3)), (B2, first_b2, (0, 2))):
                one, two = [fi[tail][b, :, lanes].astype(F32) for b in pair]
                out[0, :, first:first + LANES] = jnp.where(lower_lanes(one), one, swap_halves(two))
                out[1, :, first:first + LANES] = jnp.where(lower_lanes(one), swap_halves(one), two)
        leave(out, grads_out[weight])
    copies[len(order)].wait()
    leave(halves.at[0], mixed_out)
    leave(halves.at[1], frames_grad_out)
    copies[len(order) + 1].wait()
    width = 2 * gains.shape[1]
    share = first_gain.shape[1]
    whole = jnp.concatenate([gains[0:4, :], gains[4:8, :]], axis=1)
    turned = pltpu.roll(whole, lax.rem(width - inner * share, width), 1)
    first_gain[...] = turned[0:2, 0:share]
    second_gain[...] = turned[2:4, 0:share]
    leave(first_gain, first_out)
    leave(second_gain, second_out)
    for copy in leaving:
        copy.wait()


def run_layer(frames, cot, dialogue, padding, position_set, gain_one, gain_two, weights):
    width = frames.shape[2]
    rows = frames.shape[0] * frames.shape[1] // 2
    d_rows = weights[0].shape[1]
    lanes = group_lanes(weights[0].shape[2], weights[FEED[0]].shape[2])
    count = len(lanes)
    group, pair_group = 8 * rows, 4 * rows
    dma = pltpu.SemaphoreType.DMA
    vm = pltpu.VMEM
    shape = jax.ShapeDtypeStruct
    block_rows, pair_rows = (8, rows, width), (4, rows, width)
    four = (4, 4, rows, width)
    own = [(ZN, d_rows, n) for n in lanes]
    qb, part = lanes[Q] // 2, lanes[GA] // 2
    own_frames = (frames.shape[0] // 2,) + frames.shape[1:]
    scratch = (
        [vm(own_frames, BF)] * 2
        + [pltpu.SMEM(v.shape, v.dtype) for v in (dialogue, padding, position_set)]
        + [vm(gain_one.shape, F32)] * 2
        + [[vm(v.shape, BF) for v in weights]]
        + [[vm((ATTENTION_BLOCKS if g <= O else ZN, d_rows, n), BF) for g, n in enumerate(lanes)]]
        + [[vm(v, BF) for v in own]]
        + [[vm((width, n), BF) for n in lanes]]
        + [[vm((ZN, 4, d_rows, n), BF) for n in lanes]]
        + [[vm((2, ZN, d_rows, n), BF) for n in lanes]]
        + [[vm(v, BF) for v in own]] * 3
        + [vm((2, 16, width), BF)]
        + [vm(pair_rows, BF), vm(block_rows, BF), vm(block_rows, BF), vm(pair_rows, BF)] + [vm((2,) + block_rows, F32)]
        + [vm(four, BF)] * 5
        + [[vm((pair_group, qb), BF)] * 3, [vm((pair_group, 2 * qb), BF)] * 3, vm((pair_group, 2 * qb), BF)]
        + [vm((pair_group // LANES, qb // HDIM, LANES, LANES), F32)]
        + [[vm((group, n), F32) for n in (part, LANES)]] * 3
        + [vm((group, 2 * part), BF)] * 3
        + [[vm((group, 2 * LANES), BF)] * 2, [vm((group, LANES), BF)] * 2]
        + [vm((2, 4, 8, LANES), F32), vm((ZN, 8, width // 2), F32), vm((8, 8, width // 2), F32), vm((8, width // 2), F32)]
        + [vm((2,) + frames.shape, BF)]
        + [vm((rows, width), F32)] * 4 + [vm((3, rows, LANES), F32)]
        + [dma((7 + len(weights),)), dma((2 + count,))]
        + [dma((count,)), dma((count, 3)), dma((count, 4)), dma((count,))]
        + [dma((4, 2)), dma((2, 8, CUTS)), dma((2, 4, CUTS))]
        + [dma((4,)), dma((2, 4, CUTS)), dma((2, 2, CUTS)), dma((4,)), dma((2, 4, CUTS)), dma((2, 4, CUTS)), dma((2, CUTS))]
        + [dma((count,)), dma((count, 2)), dma((count,)), dma((count, 4)), dma((count,)), dma((count,))]
        + [dma((2,))] * 6
    )
    any_place = pl.BlockSpec(memory_space=pl.ANY)
    packed = pl.pallas_call(
        layer_kernel,
        out_shape=[[shape(v, BF) for v in own], shape((2,) + frames.shape, BF), shape((8, width // 2), F32)],
        in_specs=[any_place] * 7 + [[any_place] * len(weights)],
        out_specs=[[any_place] * count, any_place, any_place],
        scratch_shapes=scratch,
        compiler_params=pltpu.CompilerParams(
            collective_id=0, has_side_effects=True, vmem_limit_bytes=63 * 2**20
        ),
        cost_estimate=pl.CostEstimate(flops=10**10, bytes_accessed=10**7, transcendentals=0),
        name="layer",
    )(frames, cot, dialogue, padding, position_set, gain_one, gain_two, list(weights))
    grads = [shape(v.shape, F32) for v in weights]
    gain = shape((2, d_rows), F32)
    mixed, frames_grad, grads, first_gain, second_gain = pl.pallas_call(
        output_kernel,
        out_shape=[shape(frames.shape, BF), shape(frames.shape, BF), grads, gain, gain],
        in_specs=[[any_place] * count, any_place, any_place],
        out_specs=[any_place, any_place, [any_place] * len(grads), any_place, any_place],
        scratch_shapes=[
            [vm(v, BF) for v in own], vm((2,) + frames.shape, BF), vm((8, width // 2), F32),
            [vm(v.shape, F32) for v in weights], vm(gain.shape, F32), vm(gain.shape, F32),
            dma((count + 2,)), dma((len(grads) + 4,)),
        ],
        compiler_params=pltpu.CompilerParams(vmem_limit_bytes=63 * 2**20),
        cost_estimate=pl.CostEstimate(flops=10**6, bytes_accessed=10**7, transcendentals=0),
        name="outputs",
    )(*packed)
    return mixed, frames_grad, *grads, first_gain, second_gain


def per_device(
    frames, cotangent, dialogue, padding, position_set,
    query_weight, key_weight, value_weight, output_weight, gate_weight, up_weight, down_weight,
    attention_gain, feedforward_gain,
):
    dp = lax.axis_size("dp")
    outer = dp // INNER
    groups = [[o * INNER + i for o in range(outer)] for i in range(INNER)]
    width = frames.shape[-1]
    turn = (False, False, False, True, False, False, True)
    weights = [query_weight, key_weight, value_weight, output_weight, gate_weight, up_weight, down_weight]
    weights = [jnp.swapaxes(v, 1, 2) if t else v for v, t in zip(weights, turn)]

    def to_kernel(v):
        if outer == 1:
            return v
        cut = v.reshape(v.shape[:-1] + (outer, INNER, width // dp))
        return jnp.swapaxes(cut, -3, -2).reshape(v.shape)

    def from_kernel(v):
        if outer == 1:
            return v
        cut = v.reshape(v.shape[:-1] + (INNER, outer, width // dp))
        return jnp.swapaxes(cut, -3, -2).reshape(v.shape)

    if outer > 1:
        weights = [lax.all_gather(v, "dp", axis=1, tiled=True, axis_index_groups=groups) for v in weights]
    mixed, frames_grad, *rest = run_layer(
        to_kernel(frames), to_kernel(cotangent), dialogue, padding, position_set,
        to_kernel(attention_gain), to_kernel(feedforward_gain), weights,
    )
    grads, gains = rest[:7], rest[7:]
    if outer > 1:
        grads = [
            lax.psum_scatter(v, "dp", scatter_dimension=1, tiled=True, axis_index_groups=groups) for v in grads
        ]
        gains = [
            lax.psum_scatter(v, "dp", scatter_dimension=1, tiled=True, axis_index_groups=groups) for v in gains
        ]
    grads = [jnp.swapaxes(v, 1, 2) if t else v for v, t in zip(grads, turn)]
    return (from_kernel(mixed), from_kernel(frames_grad), *grads, *gains)


def solution(mesh):
    column = P(None, "dp", "tensor")
    row = P(None, "tensor", "dp")
    rows = P("dp", None, None)
    in_specs = (
        rows, rows, P("dp"), P("dp"), P(),
        column, column, column, row, column, column, row, P(), P(),
    )
    out_specs = (
        rows, rows, column, column, column, row, column, column, row, P(None, "dp"), P(None, "dp"),
    )
    return jax.shard_map(per_device, mesh=mesh, in_specs=in_specs, out_specs=out_specs, check_vma=False)
```

```python
import jax
import jax.numpy as jnp
from jax import lax
from jax.experimental import pallas as pl
from jax.experimental.pallas import tpu as pltpu
from jax.sharding import PartitionSpec as P

HDIM = 64
EPSILON = 1e-05
INNER = 16
ZN = 4
LANES = 128
CUTS = 4
MESH = pl.DeviceIdType.MESH
BF = jnp.bfloat16
F32 = jnp.float32
NN = (((1,), (0,)), ((), ()))
NT = (((1,), (1,)), ((), ()))
TN = (((0,), (0,)), ((), ()))
Q, K, V, O, GA, UA, DA, B1, B2 = range(9)
FEED = (4, 5, 6)
ATTENTION_BLOCKS, TAIL = 2, 64


def feed_columns(units):
    part = units // (ZN * LANES) * LANES
    assert units == ZN * part + ZN * TAIL + ZN // 2 * TAIL
    return part, ZN * part, ZN * (part + TAIL)


def group_lanes(attention_columns, units):
    chip = attention_columns // ATTENTION_BLOCKS
    return [2 * chip] * 4 + [2 * feed_columns(units)[0]] * 3 + [2 * TAIL * len(FEED)] * 2


def swap_halves(v):
    return pltpu.roll(v.astype(F32), TAIL, 1).astype(v.dtype)


def lower_lanes(v):
    return lax.broadcasted_iota(jnp.int32, v.shape, 1) < TAIL


def dot(a, b, dims=NN):
    return lax.dot_general(a, b, dims, preferred_element_type=F32)


def layer_kernel(
    frames_in, cot_in, dialogue_in, padding_in, position_in, gain_one_in, gain_two_in, weights_in,
    grads_out, halves_out, gains_out,
    frames, cot, dialogue, padding, position_set, gain_one, gain_two, weights,
    st, ga, w, dw, rc, sx, rx, fi,
    set_mask, n1, sd, n2, hl, pf,
    sb, sr, so, ru, rd,
    heads_in, heads_grad, att2, probs, gate, up, active_grad, act2, gate_grad, up_grad, tail_gate_up, tail_act,
    cnt, gain_col, gain_face, gain_sum, halves,
    u_one, u_two, hid, hgrad, small,
    in_s, out_s, wt_s, sp_r, ax_r, mc_r, ag_s, ag_r, pr_r, sy_s, sy_r, py_r, sz_s, su_r, sd_r, pu_r,
    gc_s, gc_r, gx_s, gx_r, gf_s, gf_r, c_s, c_r, y_s, y_r, g_s, g_r,
):
    idx = lax.axis_index("dp")
    y = lax.axis_index("tensor")
    inner = lax.rem(idx, INNER)
    base = idx - inner
    z = lax.div(inner, 4)
    x = lax.rem(lax.div(inner, 2), 2)
    c = lax.rem(inner, 2)

    def dev(zz, xx, cc, yy):
        return (base + zz * 4 + xx * 2 + cc, yy)

    def flip(v, bit):
        return 1 - v if bit else v

    def hop(k):
        return lax.rem(z + k, ZN)

    def remote(src, dst, ssem, rsem, device):
        return pltpu.make_async_remote_copy(
            src_ref=src, dst_ref=dst, send_sem=ssem, recv_sem=rsem,
            device_id=device, device_id_type=MESH,
        )

    low = lax.rem(z, 2)
    partner = dev(z, x, c, 1 - y)
    beside = dev(z + 1 - 2 * low, x, c, y)
    sibling = dev(z, x, 1 - c, y)
    across = dev(z, 1 - x, c, y)
    above = dev(hop(1), x, c, y)
    below = dev(hop(ZN - 1), x, c, y)
    column = [dev(hop(k), x, c, y) for k in (1, 2, 3)]
    face = [
        (flip(x, a), flip(c, b), flip(y, d))
        for a in (0, 1) for b in (0, 1) for d in (0, 1) if a or b or d
    ]
    rows, width = n1.shape[1:]
    half = rows // 16
    units = weights[FEED[0]].shape[2]
    part, first_b1, first_b2 = feed_columns(units)
    even = low == 0
    d_rows = weights[0].shape[1]
    own_slot = 2 * z + y
    pair_slot = 2 * low + y
    mine = pl.ds(half * y, half)
    slice_mine = 2 * x + c

    def send(cond, src, dst, ssem, rsem, device):
        copy = remote(src, dst, ssem, rsem, device)
        if cond is None:
            copy.start()
        else:
            pl.when(cond)(copy.start)

    def sent(ref, ssem, cond=None):
        if cond is None:
            remote(ref, ref, ssem, ssem, sibling).wait_send()
        else:
            pl.when(cond)(remote(ref, ref, ssem, ssem, sibling).wait_send)

    def arrived(dst, rsem, cond=None):
        def wait():
            remote(dst, dst, rsem, rsem, sibling).wait_recv()

        if cond is None:
            wait()
        else:
            pl.when(cond)(wait)

    sources = (frames_in.at[mine], cot_in.at[mine], dialogue_in, padding_in, position_in, gain_one_in, gain_two_in)
    targets = (frames, cot, dialogue, padding, position_set, gain_one, gain_two)
    inputs = [
        pltpu.make_async_copy(src, dst, in_s.at[n])
        for n, (src, dst) in enumerate(zip(sources + tuple(weights_in), targets + tuple(weights)))
    ]
    weight_inputs = inputs[len(targets):]
    for n in (0, 4, 5):
        inputs[n].start()
    for copy in weight_inputs[:3]:
        copy.start()

    barrier = pltpu.get_barrier_semaphore()
    for d in column:
        pl.semaphore_signal(barrier, inc=1, device_id=d, device_id_type=MESH)
    for xx, cc, yy in face:
        pl.semaphore_signal(barrier, inc=1, device_id=dev(z, xx, cc, yy), device_id_type=MESH)
    for n in (2, 3, 1, 6):
        inputs[n].start()
    for copy in weight_inputs[3:]:
        copy.start()

    def blocks_of(g):
        return ATTENTION_BLOCKS if g <= O else ZN

    def stage(g):
        n = st[g].shape[2] // 2
        for b in range(blocks_of(g)):
            for s in range(2):
                st[g][b, :, s * n:(s + 1) * n] = weights[g][s, :, b * n:(b + 1) * n]

    def stage_tail(g, first, b):
        at = first + (b // 2 if g == B2 else b) * TAIL
        tile = at // LANES * LANES
        for m, weight in enumerate(FEED):
            both = [weights[weight][s, :, tile:tile + LANES] for s in range(2)]
            if at == tile:
                here = jnp.where(lower_lanes(both[0]), both[0], swap_halves(both[1]))
            else:
                here = jnp.where(lower_lanes(both[0]), swap_halves(both[0]), both[1])
            st[g][b, :, m * LANES:(m + 1) * LANES] = here

    for g in (Q, K, V):
        weight_inputs[g].wait()
        stage(g)

    inputs[4].wait()
    row_at = lax.broadcasted_iota(jnp.int32, (16, width), 0)
    row_set = jnp.zeros((16, width), jnp.int32)
    for p in range(16):
        row_set = jnp.where(row_at == p, position_set[p], row_set)
    for s in range(2):
        set_mask[s] = jnp.where(row_set == s, 1.0, 0.0).astype(BF)

    def gain_full(gain):
        m1 = set_mask[1].astype(F32)
        return jnp.where(m1 > 0.5, gain[1:2, :], gain[0:1, :])

    def tile_rows(v):
        return jnp.broadcast_to(v[None], (half, 16, v.shape[1])).reshape(rows, v.shape[1])

    def normalize(values, gain):
        inverse = lax.rsqrt(jnp.sum(values * values, axis=-1, keepdims=True) / width + EPSILON)
        unit = values * inverse
        return unit, inverse, (unit * tile_rows(gain_full(gain))).astype(BF)

    def own_rows(ref):
        return ref[...].reshape(rows, width).astype(F32)

    def zero(ref):
        for n in (1, 2):
            ref[n] = jnp.zeros(ref.shape[1:], ref.dtype)

    inputs[0].wait()
    inputs[5].wait()
    unit, inverse, normed = normalize(own_rows(frames), gain_one)
    u_one[...] = unit
    small[0] = jnp.broadcast_to(inverse, (rows, LANES))
    n1[pair_slot] = normed
    pl.when(z == 0)(lambda: zero(ru))
    pl.when(z == ZN - 1)(lambda: zero(rd))

    inputs[2].wait()
    inputs[3].wait()
    lane = lax.broadcasted_iota(jnp.int32, (8, LANES), 1)
    table = jnp.zeros((8, LANES), F32)
    for f in range(dialogue.shape[0]):
        table = table + jnp.where(lane == dialogue[f], padding[f].astype(F32), 0.0)
    cnt[0, z] = table
    pl.semaphore_wait(barrier, len(column) + len(face))

    def used(g, k=0):
        if g != B2:
            return None
        return even if k % 2 == 0 else jnp.logical_not(even)

    def spread(g, k):
        send(used(g, k), st[g].at[lax.rem(hop(k), blocks_of(g))], ga[g].at[z], wt_s.at[g], sp_r.at[g, k - 1],
             dev(hop(k), x, c, y))

    def piece_of(g, k, xx, cc):
        piece = hop(k) * 4 + 2 * xx + cc
        return w[g].at[pl.ds(pl.multiple_of(piece * d_rows, d_rows), d_rows), :]

    def where_used(g, action):
        if used(g) is None:
            action()
        else:
            pl.when(used(g))(action)

    def multicast(g, k):
        def action():
            if k:
                arrived(ga[g].at[hop(k)], sp_r.at[g, 3 - k])
            src = ga[g].at[hop(k)] if k else st[g].at[lax.rem(z, blocks_of(g))]
            dst = piece_of(g, k, x, c)
            send(None, src, dst, wt_s.at[g], ax_r.at[g, k], across)
            send(None, src, dst, wt_s.at[g], mc_r.at[g], sibling)
            dst[...] = src[...]

        where_used(g, action)

    def forward(g, k):
        def action():
            dst = piece_of(g, k, 1 - x, c)
            arrived(dst, ax_r.at[g, k])
            send(None, dst, dst, wt_s.at[g], mc_r.at[g], sibling)

        where_used(g, action)

    def weights_here(g):
        arrived(w[g].at[pl.ds(0, 8 * d_rows), :], mc_r.at[g], cond=used(g))

    cut_rows = rows // CUTS

    def cut(q):
        return pl.ds(q * cut_rows, cut_rows)

    def gather_sem(which, slot, q):
        return (pr_r if which in (0, 3) else ag_r).at[which // 2, slot, q]

    def gather_send(which, buf, slot, q, cond, way, device):
        src = buf.at[slot, cut(q)]
        send(cond, src, src, ag_s.at[which, min(way, 1)], gather_sem(which, slot, q), device)

    def gather_start(which, buf):
        for q in range(CUTS):
            gather_send(which, buf, own_slot, q, z < ZN - 1, 1, above)
            gather_send(which, buf, own_slot, q, z > 0, 2, below)
            gather_send(which, buf, own_slot, q, None, 0, partner)

    def gather_step(which, buf, k):
        lo = 2 * jnp.maximum(z - k, 0) + y
        hi = 2 * jnp.minimum(z + k, ZN - 1) + y
        up, down = z >= k, z + k <= ZN - 1
        for q in range(CUTS):
            arrived(buf.at[lo, cut(q)], gather_sem(which, lo, q), cond=up)
            gather_send(which, buf, lo, q, up & (z < ZN - 1), 1, above)
            gather_send(which, buf, lo, q, up, 0, partner)
            arrived(buf.at[hi, cut(q)], gather_sem(which, hi, q), cond=down)
            gather_send(which, buf, hi, q, down & (z > 0), 2, below)
            gather_send(which, buf, hi, q, down, 0, partner)

    def gather_end(which, buf):
        slot = 2 * z + 1 - y
        for q in range(CUTS):
            arrived(buf.at[slot, cut(q)], gather_sem(which, slot, q))
        for k in (1, 2, 3):
            lo = 2 * jnp.maximum(z - k, 0) + 1 - y
            hi = 2 * jnp.minimum(z + k, ZN - 1) + 1 - y
            for q in range(CUTS):
                arrived(buf.at[lo, cut(q)], gather_sem(which, lo, q), cond=z >= k)
                arrived(buf.at[hi, cut(q)], gather_sem(which, hi, q), cond=z + k <= ZN - 1)

    def pair_start(which, buf):
        for q in range(CUTS):
            gather_send(which, buf, pair_slot, q, None, 1, beside)
            gather_send(which, buf, pair_slot, q, None, 0, partner)

    def pair_step(which, buf):
        slot = 2 * (1 - low) + y
        for q in range(CUTS):
            arrived(buf.at[slot, cut(q)], gather_sem(which, slot, q))
            gather_send(which, buf, slot, q, None, 0, partner)

    def pair_end(which, buf):
        slot, far = 2 * low + 1 - y, 2 * (1 - low) + 1 - y
        for q in range(CUTS):
            arrived(buf.at[slot, cut(q)], gather_sem(which, slot, q))
            arrived(buf.at[far, cut(q)], gather_sem(which, far, q))

    def far_first(i):
        orders = ((3, 2, 1, 0), (3, 0, 2, 1), (0, 3, 1, 2), (0, 1, 2, 3))
        b = jnp.int32(0)
        for zz, order in enumerate(orders):
            b = b + jnp.where(z == zz, order[i], 0)
        return b

    def row_sem(n, b, q):
        return (py_r if n in (0, 3) else sy_r).at[n // 2, b, q]

    def scatter_put(n, partial):
        blocks = partial.shape[0] // rows
        pf[n % 2, 0:blocks] = partial.reshape(blocks, rows, width)

    def scatter_add(n, partial):
        blocks = partial.shape[0] // rows
        pf[n % 2, 0:blocks] += partial.reshape(blocks, rows, width)

    def scatter_send(n, i, b=None):
        b = far_first(i) if b is None else b
        for q in range(CUTS):
            sb[n, b, cut(q), :] = pf[n % 2, 2 * b + 1 - y, cut(q), :].astype(BF)
            send(None, sb.at[n, b, cut(q)], sr.at[n, b, cut(q)], sy_s.at[n], row_sem(n, b, q), partner)

    def chip_sum(n, b, q):
        arrived(sr.at[n, b, cut(q)], row_sem(n, b, q))
        return pf[n % 2, 2 * b + y, cut(q), :] + sr[n, b, cut(q), :].astype(F32)

    plan = (
        (True, 3, z <= 1), (False, 0, z >= 2), (True, 3, z == 2), (False, 0, z == 1),
        (True, 2, z <= 1), (False, 1, z >= 2), (True, 1, z == 0), (False, 2, z == 3),
    )

    def scatter_step(n, at):
        rising, b, cond = plan[at]
        if rising:
            inflow, buf, r, target = z > 0, ru, su_r, above
        else:
            inflow, buf, r, target = z < ZN - 1, rd, sd_r, below
        for q in range(CUTS):

            def step(q=q):
                total = chip_sum(n, b, q)
                arrived(buf.at[n, b, cut(q)], r.at[n - 1, b, q], cond=inflow)
                so[n, b, cut(q), :] = (total + buf[n, b, cut(q), :].astype(F32)).astype(BF)

            pl.when(cond)(step)
            send(cond, so.at[n, b, cut(q)], buf.at[n, b, cut(q)], sz_s.at[n], r.at[n - 1, b, q], target)

    def scatter_end(n):
        totals = []
        for q in range(CUTS):
            total = chip_sum(n, z, q)
            arrived(ru.at[n, z, cut(q)], su_r.at[n - 1, z, q], cond=z > 0)
            arrived(rd.at[n, z, cut(q)], sd_r.at[n - 1, z, q], cond=z < ZN - 1)
            totals.append(total + ru[n, z, cut(q), :].astype(F32) + rd[n, z, cut(q), :].astype(F32))
        return jnp.concatenate(totals, axis=0)

    def pair_scatter_send(n):
        scatter_send(n, 2, 1 - low)
        scatter_send(n, 3, low)

    def pair_scatter_step(n):
        b = 1 - low
        for q in range(CUTS):
            so[n, b, cut(q), :] = chip_sum(n, b, q).astype(BF)
            send(None, so.at[n, b, cut(q)], ru.at[n, b, cut(q)], sz_s.at[n], pu_r.at[n // 2, q], beside)

    def pair_scatter_end(n):
        totals = []
        for q in range(CUTS):
            total = chip_sum(n, low, q)
            arrived(ru.at[n, low, cut(q)], pu_r.at[n // 2, q])
            totals.append(total + ru[n, low, cut(q), :].astype(F32))
        return jnp.concatenate(totals, axis=0)

    def both_sets(v):
        count, n = v.shape
        three = v.reshape(count // 16, 16, n)
        return jnp.concatenate([(three * set_mask[s, :, 0:n][None]).reshape(count, n) for s in range(2)], axis=1)

    def choose(v):
        count, n = v.shape[0], v.shape[1] // 2
        m = jnp.broadcast_to(set_mask[1, :, 0:n].astype(F32)[None], (count // 16, 16, n)).reshape(count, n)
        return jnp.where(m > 0.5, v[:, n:], v[:, 0:n])

    def flat(buf):
        return buf[...].reshape(buf.shape[0] * rows, width)

    def weight_grad(g, values, grads):
        dw[g][...] = dot(values, grads, TN).astype(BF).reshape(dw[g].shape)
        weight_grad_send(g)

    def tail_grad(h):
        g = (B1, B2)[h]
        n = 2 * LANES
        dw[g][:, :, :, 0:n] = dot(flat(n2), tail_gate_up[h][...], TN).astype(BF).reshape(ZN, 4, d_rows, n)
        dw[g][:, :, :, n:] = dot(flat(sd), tail_act[h][...], TN).astype(BF).reshape(ZN, 4, d_rows, LANES)
        weight_grad_send(g)

    def weight_grad_send(g):
        for xx in (1 - x, x):
            send(used(g), dw[g].at[:, 2 * xx + 1 - c], rc[g].at[xx], gc_s.at[g], gc_r.at[g, xx], sibling)

    def reduce_across(g):
        def action():
            arrived(rc[g].at[1 - x], gc_r.at[g, 1 - x])
            for k in (2, 1, 3, 0):
                zz = hop(k)
                sx[g][zz] = (dw[g][zz, 2 * (1 - x) + c].astype(F32) + rc[g][1 - x, zz].astype(F32)).astype(BF)
                send(None, sx[g].at[zz], rx[g].at[zz], gx_s.at[g], gx_r.at[g, zz], across)

        where_used(g, action)

    def reduce_column(g, k):
        def action():
            zz = hop(k)
            if k == 2:
                arrived(rc[g].at[x], gc_r.at[g, x])
            arrived(rx[g].at[zz], gx_r.at[g, zz])
            total = dw[g][zz, 2 * x + c].astype(F32) + rc[g][x, zz].astype(F32) + rx[g][zz].astype(F32)
            if k:
                rx[g][zz] = total.astype(BF)
                send(None, rx[g].at[zz], fi[g].at[z], gf_s.at[g], gf_r.at[g], dev(zz, x, c, y))
            else:
                fi[g][z] = total.astype(BF)

        where_used(g, action)

    def reduce_end(g):
        if g == B2:
            arrived(fi[g].at[pl.ds(0, 1)], gf_r.at[g], cond=even)
            arrived(fi[g].at[pl.ds(0, 2)], gf_r.at[g], cond=jnp.logical_not(even))
        else:
            arrived(fi[g].at[pl.ds(0, 3)], gf_r.at[g])
        outputs[g].start()

    outputs = [
        pltpu.make_async_copy(src, dst, out_s.at[n])
        for n, (src, dst) in enumerate(zip(tuple(fi) + (halves, gain_sum), tuple(grads_out) + (halves_out, gains_out)))
    ]

    def counts_start():
        for k in (1, 2, 3):
            send(None, cnt.at[0, z], cnt.at[0, z], c_s.at[0], c_r.at[0], dev(hop(k), x, c, y))

    def counts_step():
        arrived(cnt.at[0, pl.ds(0, 3)], c_r.at[0])
        cnt[1, slice_mine] = cnt[0, 0] + cnt[0, 1] + cnt[0, 2] + cnt[0, 3]
        for a, b in ((0, 1), (1, 0), (1, 1)):
            send(None, cnt.at[1, slice_mine], cnt.at[1, slice_mine], c_s.at[1], c_r.at[1],
                 dev(z, flip(x, a), flip(c, b), y))

    def seed_rows():
        frame_weight = small[1, mine, :]
        weight_rows = jnp.broadcast_to(frame_weight[:, None, 0:1], (half, 16, width)).reshape(rows, width)
        return own_rows(cot) * weight_rows

    def seed_here():
        arrived(cnt.at[1, pl.ds(0, 3)], c_r.at[1])
        inputs[1].wait()
        counts = cnt[1, 0] + cnt[1, 1] + cnt[1, 2] + cnt[1, 3]
        for f in range(dialogue.shape[0]):
            found = jnp.sum(jnp.where(lane == dialogue[f], counts, 0.0), axis=1, keepdims=True)
            loss = padding[f].astype(F32) * (dialogue.shape[0] * 1.0) / (found + 1.0)
            small[1, f:f + 1, :] = jnp.broadcast_to(loss[0:1, :], (1, LANES))
        sd[own_slot] = seed_rows().astype(BF)

    def stage_rest():
        for copy in weight_inputs[O:]:
            copy.wait()
        for g in (O, GA, UA, DA):
            stage(g)
        for b in range(ZN):
            stage_tail(B1, first_b1, b)
        for b in (0, 2):
            stage_tail(B2, first_b2, b)
        zero_unused()

    def zero_unused():
        def zero_weights():
            w[B2][...] = jnp.zeros_like(w[B2])

        pl.when(jnp.logical_not(even))(zero_weights)
        for b in (1, 3):
            fi[B2][b] = jnp.zeros(fi[B2].shape[1:], BF)

    bl = LANES
    r_at = lax.broadcasted_iota(jnp.int32, (bl, bl), 0)
    c_at = lax.broadcasted_iota(jnp.int32, (bl, bl), 1)
    seen = (c_at <= r_at) & (lax.div(r_at, 16) == lax.div(c_at, 16))
    qb = heads_in[0].shape[1]
    heads = qb // HDIM
    head_of = lax.div(lax.broadcasted_iota(jnp.int32, (bl, qb), 1), HDIM)
    scale = HDIM ** (-0.5)

    def only(v, h):
        return jnp.where(head_of == h, v, jnp.zeros_like(v))

    def project_heads(g):
        heads_in[g][...] = choose(dot(flat(n1), w[g][...])).astype(BF)

    def attend():
        attended = []
        for t in range(att2.shape[0] // bl):
            at = pl.ds(t * bl, bl)
            q, kk, v = heads_in[Q][at, :], heads_in[K][at, :], heads_in[V][at, :]
            out = jnp.zeros((bl, qb), F32)
            for h in range(heads):
                scores = dot(only(q, h), kk, NT) * scale
                scores = jnp.where(seen, scores, -1e30)
                e = jnp.exp(scores - jnp.max(scores, axis=-1, keepdims=True))
                e = jnp.where(seen, e, 0.0)
                p = e / jnp.sum(e, axis=-1, keepdims=True)
                probs[t, h] = p
                out = jnp.where(head_of == h, dot(p.astype(BF), v), out)
            attended.append(out.astype(BF))
        att2[...] = both_sets(jnp.concatenate(attended, axis=0))

    def attend_back():
        datt = choose(dot(flat(hl), w[O][...])).astype(BF)
        gq, gk, gv = [], [], []
        for t in range(att2.shape[0] // bl):
            at = pl.ds(t * bl, bl)
            q, kk, v = heads_in[Q][at, :], heads_in[K][at, :], heads_in[V][at, :]
            da = datt[t * bl:(t + 1) * bl, :]
            tq = jnp.zeros((bl, qb), F32)
            tk, tv = tq, tq
            for h in range(heads):
                p = probs[t, h]
                dp = dot(only(da, h), v, NT)
                tv = jnp.where(head_of == h, dot(p.astype(BF), da, TN), tv)
                ds = (p * (dp - jnp.sum(dp * p, axis=-1, keepdims=True))).astype(BF)
                tq = jnp.where(head_of == h, dot(ds, kk) * scale, tq)
                tk = jnp.where(head_of == h, dot(ds, q, TN) * scale, tk)
            gq.append(tq.astype(BF))
            gk.append(tk.astype(BF))
            gv.append(tv.astype(BF))
        for g, parts in ((Q, gq), (K, gk), (V, gv)):
            heads_grad[g][...] = both_sets(jnp.concatenate(parts, axis=0))

    def heads_back():
        return sum(dot(heads_grad[g][...], w[g][...], NT) for g in (Q, K, V))

    def choose_tail(one, two):
        count = one.shape[0]
        m = jnp.broadcast_to(set_mask[1, :, 0:LANES].astype(F32)[None], (count // 16, 16, LANES)).reshape(count, LANES)
        first = jnp.where(lower_lanes(one), one, swap_halves(two))
        second = jnp.where(lower_lanes(one), swap_halves(one), two)
        return jnp.where(m > 0.5, second, first)

    def split_tail(v):
        count = v.shape[0]
        turned = swap_halves(v)
        m0, m1 = [
            jnp.broadcast_to(set_mask[s, :, 0:LANES].astype(F32)[None], (count // 16, 16, LANES)).reshape(count, LANES)
            for s in range(2)
        ]
        one = jnp.where(lower_lanes(v), v * m0, turned * m1)
        two = jnp.where(lower_lanes(v), turned * m0, v * m1)
        return one.astype(BF), two.astype(BF)

    def gate_up_rows():
        gate[0][...] = choose(dot(flat(n2), w[GA][...]))
        up[0][...] = choose(dot(flat(n2), w[UA][...]))

    def gate_up_tail():
        one = dot(flat(n2), w[B1][:, 0:2 * LANES])
        two = dot(flat(n2), w[B2][:, 0:2 * LANES])
        gate[1][...] = choose_tail(one[:, 0:LANES], two[:, 0:LANES])
        up[1][...] = choose_tail(one[:, LANES:], two[:, LANES:])

    def active_rows():
        v = gate[0][...]
        act2[...] = both_sets((v * jax.nn.sigmoid(v) * up[0][...]).astype(BF))

    def active_tail():
        v = gate[1][...]
        for h, tile in enumerate(split_tail(v * jax.nn.sigmoid(v) * up[1][...])):
            tail_act[h][...] = tile

    def active_dot():
        active_grad[0][...] = choose(dot(flat(sd), w[DA][...]))

    def active_dot_tail():
        active_grad[1][...] = choose_tail(dot(flat(sd), w[B1][:, 2 * LANES:]), dot(flat(sd), w[B2][:, 2 * LANES:]))

    def gate_up_grads(h):
        v = gate[h][...]
        sig = jax.nn.sigmoid(v)
        g = active_grad[h][...]
        return g * up[h][...] * sig * (1.0 + v * (1.0 - sig)), g * (v * sig)

    def active_back():
        first, second = gate_up_grads(0)
        gate_grad[...] = both_sets(first.astype(BF))
        up_grad[...] = both_sets(second.astype(BF))

    def active_back_tail():
        first, second = gate_up_grads(1)
        for h, (g_tile, u_tile) in enumerate(zip(split_tail(first), split_tail(second))):
            tail_gate_up[h][:, 0:LANES] = g_tile
            tail_gate_up[h][:, LANES:] = u_tile

    def feed_back():
        return dot(gate_grad[...], w[GA][...], NT) + dot(up_grad[...], w[UA][...], NT)

    def feed_back_tail():
        return sum(dot(tail_gate_up[h][...], w[g][:, 0:2 * LANES], NT) for h, g in enumerate((B1, B2)))

    def feed_out():
        tail = sum(dot(tail_act[h][...], w[g][:, 2 * LANES:], NT) for h, g in enumerate((B1, B2)))
        return dot(act2[...], w[DA][...], NT) + tail

    def set_sums(v, at):
        three = v.reshape(half, 16, width)
        for s in range(2):
            part = (three * set_mask[s].astype(F32)[None]).reshape(rows, width)
            total = jnp.sum(part, axis=0, keepdims=True)
            for side in range(2):
                gain_col[z, 4 * side + at + s:4 * side + at + s + 1, :] = total[:, side * width // 2:(side + 1) * width // 2]

    def norm_back(gradient, gain, unit, inverse):
        scaled = gradient * tile_rows(gain_full(gain))
        return inverse * (scaled - unit * (jnp.sum(scaled * unit, axis=-1, keepdims=True) / width))

    def second_norm(attention):
        inputs[6].wait()
        hidden = own_rows(frames) + attention
        hid[...] = hidden
        unit, inverse, normed = normalize(hidden, gain_two)
        u_two[...] = unit
        small[2] = jnp.broadcast_to(inverse, (rows, LANES))
        n2[own_slot] = normed

    def second_norm_back(normed_two_grad):
        unit = u_two[...]
        hidden_grad = seed_rows() + norm_back(normed_two_grad, gain_two, unit, small[2][:, 0:1])
        hgrad[...] = hidden_grad
        hl[pair_slot] = hidden_grad.astype(BF)
        set_sums(normed_two_grad * unit, 2)

    def first_norm_back(normed_one_grad):
        unit = u_one[...]
        set_sums(normed_one_grad * unit, 0)
        result = hgrad[...] + norm_back(normed_one_grad, gain_one, unit, small[0][:, 0:1])
        halves[1, mine] = result.astype(BF).reshape(half, 16, width)

    def output_rows(branch):
        halves[0, mine] = (hid[...] + branch).astype(BF).reshape(half, 16, width)

    def half_send(j):
        send(None, halves.at[j, mine], halves.at[j, mine], y_s.at[j], y_r.at[j], partner)

    def half_end(j):
        theirs = pl.ds(half * (1 - y), half)
        arrived(halves.at[j, theirs], y_r.at[j])

    place = 4 * x + 2 * c + y

    def gains_start():
        for k in (1, 2, 3):
            send(None, gain_col.at[z], gain_col.at[z], g_s.at[0], g_r.at[0], dev(hop(k), x, c, y))

    def gains_step():
        arrived(gain_col.at[pl.ds(0, 3)], g_r.at[0])
        gain_face[place] = gain_col[0] + gain_col[1] + gain_col[2] + gain_col[3]
        for xx, cc, yy in face:
            send(None, gain_face.at[place], gain_face.at[place], g_s.at[1], g_r.at[1], dev(z, xx, cc, yy))

    def gains_end():
        arrived(gain_face.at[pl.ds(0, 7)], g_r.at[1])
        total = gain_face[0]
        for j in range(1, 8):
            total = total + gain_face[j]
        gain_sum[...] = total
        outputs[len(st) + 1].start()

    counts_start()
    spread(Q, 1)
    spread(Q, 2)
    stage_rest()
    spread(K, 1)
    spread(K, 3)
    multicast(Q, 3)
    counts_step()
    spread(O, 3)
    multicast(Q, 0)
    multicast(K, 0)
    multicast(DA, 0)
    spread(K, 2)
    spread(V, 1)
    pair_start(0, n1)
    spread(V, 2)
    multicast(V, 0)
    forward(Q, 0)
    spread(O, 1)
    multicast(O, 1)
    spread(B2, 3)
    forward(DA, 0)
    multicast(B1, 0)
    seed_here()
    multicast(K, 1)
    spread(Q, 3)
    spread(O, 2)
    forward(Q, 3)
    spread(V, 3)
    forward(V, 0)
    forward(O, 1)
    pair_step(0, n1)
    gather_start(1, sd)
    multicast(K, 3)
    multicast(K, 2)
    spread(UA, 3)
    multicast(Q, 2)
    multicast(V, 2)
    forward(K, 3)
    spread(B2, 1)
    multicast(Q, 1)
    multicast(O, 0)
    multicast(O, 2)
    forward(K, 0)
    spread(B2, 2)
    spread(GA, 1)
    spread(DA, 3)
    forward(K, 2)
    multicast(O, 3)
    multicast(B2, 0)
    forward(V, 2)
    spread(B1, 3)
    multicast(V, 3)
    forward(K, 1)
    spread(DA, 1)
    forward(Q, 2)
    forward(Q, 1)
    multicast(V, 1)
    weights_here(Q)
    pair_end(0, n1)
    spread(B1, 2)
    forward(O, 2)
    spread(UA, 1)
    gather_step(1, sd, 1)
    forward(B1, 0)
    project_heads(Q)
    forward(O, 3)
    multicast(UA, 1)
    weights_here(K)
    forward(O, 0)
    forward(V, 3)
    forward(V, 1)
    project_heads(K)
    weights_here(V)
    project_heads(V)
    spread(GA, 3)
    attend()
    spread(GA, 2)
    spread(B1, 1)
    weights_here(O)
    multicast(B2, 2)
    multicast(DA, 1)
    multicast(UA, 0)
    scatter_put(0, dot(att2[...], w[O][...], NT))
    multicast(GA, 0)
    pair_scatter_send(0)
    pair_scatter_step(0)
    forward(B2, 0)
    multicast(B2, 3)
    forward(UA, 1)
    multicast(B1, 1)
    multicast(B2, 1)
    spread(DA, 2)
    multicast(B1, 2)
    gather_step(1, sd, 2)
    attention = pair_scatter_end(0)
    forward(B1, 1)
    second_norm(attention)
    multicast(UA, 3)
    multicast(DA, 3)
    gather_start(2, n2)
    spread(UA, 2)
    multicast(GA, 2)
    forward(B2, 3)
    multicast(GA, 1)
    forward(DA, 1)
    gather_step(1, sd, 3)
    multicast(B1, 3)
    forward(UA, 0)
    multicast(GA, 3)
    multicast(DA, 2)
    gather_step(2, n2, 1)
    forward(GA, 2)
    forward(B1, 2)
    multicast(UA, 2)
    forward(B2, 1)
    forward(B2, 2)
    forward(B1, 3)
    gather_step(2, n2, 2)
    gather_end(1, sd)
    forward(DA, 3)
    forward(DA, 2)
    forward(GA, 0)
    forward(GA, 3)
    gather_step(2, n2, 3)
    forward(UA, 2)
    weights_here(B2)
    weights_here(B1)
    forward(GA, 1)
    weights_here(DA)
    active_dot()
    forward(UA, 3)
    active_dot_tail()
    weights_here(GA)
    weights_here(UA)
    gather_end(2, n2)
    gate_up_rows()
    gate_up_tail()
    active_tail()
    active_back_tail()
    active_rows()
    active_back()
    scatter_put(1, feed_back())
    scatter_add(1, feed_back_tail())
    scatter_send(1, 0)
    scatter_send(1, 1)
    scatter_send(1, 2)
    weight_grad(DA, flat(sd), act2[...])
    scatter_put(2, feed_out())
    reduce_across(DA)
    scatter_send(1, 3)
    scatter_step(1, 1)
    scatter_step(1, 0)
    tail_grad(1)
    scatter_send(2, 0)
    scatter_step(1, 2)
    scatter_step(1, 3)
    scatter_step(1, 4)
    scatter_step(1, 5)
    reduce_across(B2)
    scatter_send(2, 2)
    reduce_column(DA, 2)
    reduce_column(DA, 1)
    tail_grad(0)
    weight_grad(UA, flat(n2), up_grad[...])
    scatter_step(1, 7)
    reduce_across(B1)
    scatter_step(1, 6)
    reduce_across(UA)
    scatter_step(2, 0)
    reduce_column(B2, 2)
    scatter_step(2, 1)
    normed_two_grad = scatter_end(1)
    scatter_send(2, 1)
    second_norm_back(normed_two_grad)
    reduce_column(B1, 2)
    pair_start(3, hl)
    weight_grad(GA, flat(n2), gate_grad[...])
    reduce_column(UA, 2)
    scatter_step(2, 2)
    reduce_column(B1, 3)
    reduce_column(UA, 3)
    reduce_across(GA)
    pair_step(3, hl)
    scatter_step(2, 4)
    reduce_column(GA, 2)
    reduce_column(B2, 3)
    scatter_send(2, 3)
    scatter_step(2, 5)
    reduce_column(UA, 1)
    reduce_column(B1, 1)
    scatter_step(2, 7)
    pair_end(3, hl)
    weight_grad(O, flat(hl), att2[...])
    reduce_column(GA, 1)
    attend_back()
    reduce_column(GA, 3)
    scatter_step(2, 6)
    reduce_across(O)
    scatter_put(3, heads_back())
    weight_grad(V, flat(n1), heads_grad[V][...])
    reduce_column(B1, 0)
    pair_scatter_send(3)
    reduce_column(O, 2)
    reduce_column(DA, 3)
    reduce_column(UA, 0)
    reduce_across(V)
    scatter_step(2, 3)
    pair_scatter_step(3)
    weight_grad(Q, flat(n1), heads_grad[Q][...])
    reduce_column(O, 1)
    reduce_column(O, 3)
    reduce_column(V, 2)
    reduce_across(Q)
    reduce_column(Q, 2)
    reduce_column(V, 3)
    reduce_column(B2, 1)
    reduce_column(O, 0)
    normed_one_grad = pair_scatter_end(3)
    weight_grad(K, flat(n1), heads_grad[K][...])
    first_norm_back(normed_one_grad)
    reduce_column(B2, 0)
    reduce_column(GA, 0)
    reduce_column(Q, 1)
    gains_start()
    output_rows(scatter_end(2))
    reduce_across(K)
    reduce_column(K, 2)
    reduce_column(V, 0)
    reduce_column(Q, 0)
    reduce_column(DA, 0)
    reduce_end(UA)
    reduce_end(B1)
    reduce_column(V, 1)
    half_send(0)
    reduce_column(Q, 3)
    reduce_end(O)
    reduce_end(GA)
    reduce_column(K, 3)
    half_send(1)
    reduce_column(K, 1)
    reduce_end(B2)
    gains_step()
    reduce_column(K, 0)
    half_end(0)
    half_end(1)
    reduce_end(Q)
    gains_end()
    reduce_end(DA)
    reduce_end(V)
    reduce_end(K)
    outputs[len(st)].start()
    for g in range(len(st)):
        if g == B2:
            sent(w[g].at[pl.ds(0, 13 * d_rows), :], wt_s.at[g], cond=even)
            sent(w[g].at[pl.ds(0, 2 * d_rows), :], wt_s.at[g], cond=jnp.logical_not(even))
        else:
            sent(w[g].at[pl.ds(0, 15 * d_rows), :], wt_s.at[g])
        sent(dw[g].at[:, pl.ds(0, 2)], gc_s.at[g], cond=used(g))
        sent(sx[g], gx_s.at[g], cond=used(g))
        sent(rx[g].at[pl.ds(0, 3)], gf_s.at[g], cond=used(g))
    for which, buf in ((1, sd), (2, n2)):
        sent(buf.at[pl.ds(0, 4)], ag_s.at[which, 0])
        sent(buf.at[pl.ds(0, 1)], ag_s.at[which, 1], cond=(z == 0) | (z == ZN - 1))
        sent(buf.at[pl.ds(0, 5)], ag_s.at[which, 1], cond=(z > 0) & (z < ZN - 1))
        sent(sb.at[which], sy_s.at[which])
        sent(so.at[which, pl.ds(0, 3)], sz_s.at[which])
    for which, buf in ((0, n1), (3, hl)):
        sent(buf.at[pl.ds(0, 2)], ag_s.at[which, 0])
        sent(buf.at[pl.ds(0, 1)], ag_s.at[which, 1])
        sent(sb.at[which, pl.ds(0, 2)], sy_s.at[which])
        sent(so.at[which, pl.ds(0, 1)], sz_s.at[which])
    for j in (0, 1):
        sent(cnt.at[j, pl.ds(0, 3)], c_s.at[j])
        sent(halves.at[j, mine], y_s.at[j])
    sent(gain_col.at[pl.ds(0, 3)], g_s.at[0])
    sent(gain_face.at[pl.ds(0, 7)], g_s.at[1])
    for copy in outputs:
        copy.wait()


def output_kernel(
    fi_in, halves_in, gains_in,
    mixed_out, frames_grad_out, grads_out, first_out, second_out,
    fi, halves, gains, grads, first_gain, second_gain, in_s, out_s,
):
    inner = lax.rem(lax.axis_index("dp"), INNER)
    order = (B1, B2, GA, UA, DA, Q, K, V, O)
    copies = {
        g: pltpu.make_async_copy(src, dst, in_s.at[g])
        for g, (src, dst) in enumerate(zip(tuple(fi_in) + (halves_in, gains_in), tuple(fi) + (halves, gains)))
    }
    for g in order + (len(order), len(order) + 1):
        copies[g].start()
    leaving = []

    def leave(src, dst):
        leaving.append(pltpu.make_async_copy(src, dst, out_s.at[len(leaving)]))
        leaving[-1].start()

    units = grads[FEED[0]].shape[2]
    _, first_b1, first_b2 = feed_columns(units)
    copies[B1].wait()
    copies[B2].wait()
    for g, weight in ((GA, 4), (UA, 5), (DA, 6), (Q, 0), (K, 1), (V, 2), (O, 3)):
        copies[g].wait()
        out = grads[weight]
        blocks = ATTENTION_BLOCKS if g <= O else ZN
        n = fi[g].shape[2] // 2
        for b in range(blocks):
            for s in range(2):
                parts = [fi[g][other, :, s * n:(s + 1) * n].astype(F32) for other in range(b, ZN, blocks)]
                out[s, :, b * n:(b + 1) * n] = sum(parts)
        if weight in FEED:
            m = FEED.index(weight)
            lanes = slice(m * LANES, (m + 1) * LANES)
            for tail, first, pair in ((B1, first_b1, (0, 1)), (B1, first_b1 + LANES, (2, 3)), (B2, first_b2, (0, 2))):
                one, two = [fi[tail][b, :, lanes].astype(F32) for b in pair]
                out[0, :, first:first + LANES] = jnp.where(lower_lanes(one), one, swap_halves(two))
                out[1, :, first:first + LANES] = jnp.where(lower_lanes(one), swap_halves(one), two)
        leave(out, grads_out[weight])
    copies[len(order)].wait()
    leave(halves.at[0], mixed_out)
    leave(halves.at[1], frames_grad_out)
    copies[len(order) + 1].wait()
    width = 2 * gains.shape[1]
    share = first_gain.shape[1]
    whole = jnp.concatenate([gains[0:4, :], gains[4:8, :]], axis=1)
    turned = pltpu.roll(whole, lax.rem(width - inner * share, width), 1)
    first_gain[...] = turned[0:2, 0:share]
    second_gain[...] = turned[2:4, 0:share]
    leave(first_gain, first_out)
    leave(second_gain, second_out)
    for copy in leaving:
        copy.wait()


def run_layer(frames, cot, dialogue, padding, position_set, gain_one, gain_two, weights):
    width = frames.shape[2]
    rows = frames.shape[0] * frames.shape[1] // 2
    d_rows = weights[0].shape[1]
    lanes = group_lanes(weights[0].shape[2], weights[FEED[0]].shape[2])
    count = len(lanes)
    group, pair_group = 8 * rows, 4 * rows
    dma = pltpu.SemaphoreType.DMA
    vm = pltpu.VMEM
    shape = jax.ShapeDtypeStruct
    block_rows, pair_rows = (8, rows, width), (4, rows, width)
    four = (4, 4, rows, width)
    own = [(ZN, d_rows, n) for n in lanes]
    qb, part = lanes[Q] // 2, lanes[GA] // 2
    own_frames = (frames.shape[0] // 2,) + frames.shape[1:]
    scratch = (
        [vm(own_frames, BF)] * 2
        + [pltpu.SMEM(v.shape, v.dtype) for v in (dialogue, padding, position_set)]
        + [vm(gain_one.shape, F32)] * 2
        + [[vm(v.shape, BF) for v in weights]]
        + [[vm((ATTENTION_BLOCKS if g <= O else ZN, d_rows, n), BF) for g, n in enumerate(lanes)]]
        + [[vm(v, BF) for v in own]]
        + [[vm((width, n), BF) for n in lanes]]
        + [[vm((ZN, 4, d_rows, n), BF) for n in lanes]]
        + [[vm((2, ZN, d_rows, n), BF) for n in lanes]]
        + [[vm(v, BF) for v in own]] * 3
        + [vm((2, 16, width), BF)]
        + [vm(pair_rows, BF), vm(block_rows, BF), vm(block_rows, BF), vm(pair_rows, BF)] + [vm((2,) + block_rows, F32)]
        + [vm(four, BF)] * 5
        + [[vm((pair_group, qb), BF)] * 3, [vm((pair_group, 2 * qb), BF)] * 3, vm((pair_group, 2 * qb), BF)]
        + [vm((pair_group // LANES, qb // HDIM, LANES, LANES), F32)]
        + [[vm((group, n), F32) for n in (part, LANES)]] * 3
        + [vm((group, 2 * part), BF)] * 3
        + [[vm((group, 2 * LANES), BF)] * 2, [vm((group, LANES), BF)] * 2]
        + [vm((2, 4, 8, LANES), F32), vm((ZN, 8, width // 2), F32), vm((8, 8, width // 2), F32), vm((8, width // 2), F32)]
        + [vm((2,) + frames.shape, BF)]
        + [vm((rows, width), F32)] * 4 + [vm((3, rows, LANES), F32)]
        + [dma((7 + len(weights),)), dma((2 + count,))]
        + [dma((count,)), dma((count, 3)), dma((count, 4)), dma((count,))]
        + [dma((4, 2)), dma((2, 8, CUTS)), dma((2, 4, CUTS))]
        + [dma((4,)), dma((2, 4, CUTS)), dma((2, 2, CUTS)), dma((4,)), dma((2, 4, CUTS)), dma((2, 4, CUTS)), dma((2, CUTS))]
        + [dma((count,)), dma((count, 2)), dma((count,)), dma((count, 4)), dma((count,)), dma((count,))]
        + [dma((2,))] * 6
    )
    any_place = pl.BlockSpec(memory_space=pl.ANY)
    packed = pl.pallas_call(
        layer_kernel,
        out_shape=[[shape(v, BF) for v in own], shape((2,) + frames.shape, BF), shape((8, width // 2), F32)],
        in_specs=[any_place] * 7 + [[any_place] * len(weights)],
        out_specs=[[any_place] * count, any_place, any_place],
        scratch_shapes=scratch,
        compiler_params=pltpu.CompilerParams(
            collective_id=0, has_side_effects=True, vmem_limit_bytes=63 * 2**20
        ),
        cost_estimate=pl.CostEstimate(flops=10**10, bytes_accessed=10**7, transcendentals=0),
        name="layer",
    )(frames, cot, dialogue, padding, position_set, gain_one, gain_two, list(weights))
    grads = [shape(v.shape, F32) for v in weights]
    gain = shape((2, d_rows), F32)
    mixed, frames_grad, grads, first_gain, second_gain = pl.pallas_call(
        output_kernel,
        out_shape=[shape(frames.shape, BF), shape(frames.shape, BF), grads, gain, gain],
        in_specs=[[any_place] * count, any_place, any_place],
        out_specs=[any_place, any_place, [any_place] * len(grads), any_place, any_place],
        scratch_shapes=[
            [vm(v, BF) for v in own], vm((2,) + frames.shape, BF), vm((8, width // 2), F32),
            [vm(v.shape, F32) for v in weights], vm(gain.shape, F32), vm(gain.shape, F32),
            dma((count + 2,)), dma((len(grads) + 4,)),
        ],
        compiler_params=pltpu.CompilerParams(vmem_limit_bytes=63 * 2**20),
        cost_estimate=pl.CostEstimate(flops=10**6, bytes_accessed=10**7, transcendentals=0),
        name="outputs",
    )(*packed)
    return mixed, frames_grad, *grads, first_gain, second_gain


def per_device(
    frames, cotangent, dialogue, padding, position_set,
    query_weight, key_weight, value_weight, output_weight, gate_weight, up_weight, down_weight,
    attention_gain, feedforward_gain,
):
    dp = lax.axis_size("dp")
    outer = dp // INNER
    groups = [[o * INNER + i for o in range(outer)] for i in range(INNER)]
    width = frames.shape[-1]
    turn = (False, False, False, True, False, False, True)
    weights = [query_weight, key_weight, value_weight, output_weight, gate_weight, up_weight, down_weight]
    weights = [jnp.swapaxes(v, 1, 2) if t else v for v, t in zip(weights, turn)]

    def to_kernel(v):
        if outer == 1:
            return v
        cut = v.reshape(v.shape[:-1] + (outer, INNER, width // dp))
        return jnp.swapaxes(cut, -3, -2).reshape(v.shape)

    def from_kernel(v):
        if outer == 1:
            return v
        cut = v.reshape(v.shape[:-1] + (INNER, outer, width // dp))
        return jnp.swapaxes(cut, -3, -2).reshape(v.shape)

    if outer > 1:
        weights = [lax.all_gather(v, "dp", axis=1, tiled=True, axis_index_groups=groups) for v in weights]
    mixed, frames_grad, *rest = run_layer(
        to_kernel(frames), to_kernel(cotangent), dialogue, padding, position_set,
        to_kernel(attention_gain), to_kernel(feedforward_gain), weights,
    )
    grads, gains = rest[:7], rest[7:]
    if outer > 1:
        grads = [
            lax.psum_scatter(v, "dp", scatter_dimension=1, tiled=True, axis_index_groups=groups) for v in grads
        ]
        gains = [
            lax.psum_scatter(v, "dp", scatter_dimension=1, tiled=True, axis_index_groups=groups) for v in gains
        ]
    grads = [jnp.swapaxes(v, 1, 2) if t else v for v, t in zip(grads, turn)]
    return (from_kernel(mixed), from_kernel(frames_grad), *grads, *gains)


def solution(mesh):
    column = P(None, "dp", "tensor")
    row = P(None, "tensor", "dp")
    rows = P("dp", None, None)
    in_specs = (
        rows, rows, P("dp"), P("dp"), P(),
        column, column, column, row, column, column, row, P(), P(),
    )
    out_specs = (
        rows, rows, column, column, column, row, column, column, row, P(None, "dp"), P(None, "dp"),
    )
    return jax.shard_map(per_device, mesh=mesh, in_specs=in_specs, out_specs=out_specs, check_vma=False)
```
